128 devices in a mesh: rows: 16 (over y, x_lo, core), tm: 8 (over z, x_hi).
Axes of the slice: x: 4 (x_hi: 2, x_lo: 2; x = x_hi * 2 + x_lo), y: 4, z: 4, core: 2. Of those that a mesh axis runs over, the one named last changes fastest.
Arguments:
- activations: bfloat16 [64, 256, 64, 512], P('tm', 'rows'), may hold values from -6 to 6
- spectral_weight: float32 [256, 16, 64, 128], P(('rows', 'tm')), may hold values from -0.5 to 0.5
- pointwise: bfloat16 [64, 64], replicated, may hold values from -0.75 to 0.75
- readout: float32 [64], replicated, may hold values from -0.75 to 0.75
- forcing: float32 [256, 512], P('rows'), may hold values from -8 to 8
Outputs:
- grad_activations: bfloat16 [64, 256, 64, 512], P('tm', 'rows')
- grad_spectral: float32 [256, 16, 64, 128], P(('rows', 'tm'))
The draws below stay inside these ranges and needn't reach their ends.
All inputs are finite; a program needn't handle non-finite values.
Results may differ from the reference program's by a relative error of at most 0.0032.
Values sent between devices are 32-bit elements; how exact they have to be, the bound alone decides.
A program may use at most 192 MiB of HBM per device.

```python
import math
import jax
import jax.numpy as jnp
from jax import lax

C = 64
K = 16
NY = 512
NX = 256
NT = 64
PAIRS = 256


def level_of(own_key, dims, shards, smallest, top_value):
    def one(position, blocks):
        draws = jax.random.uniform(jax.random.fold_in(jax.random.fold_in(own_key, 6), position), (blocks,), jnp.float32, smallest / len(shards), top_value / len(shards))
        return jnp.repeat(jnp.exp(draws), dims[position] // blocks).reshape((-1,) + (1,) * (len(dims) - position - 1))

    factor_of = one(*shards[0])
    for cut in shards[1:]:
        factor_of = factor_of * one(*cut)
    return factor_of


def scatter_about(own_key, shape, scale, most, cuts=(), held_as=jnp.bfloat16):
    array = scale * jax.random.normal(own_key, shape, jnp.float32)
    if cuts:
        array = array * level_of(own_key, shape, cuts, -0.22, 0.18)
    return jnp.clip(array, -most, most).astype(held_as)


def setup_inputs(seed: int = 0) -> dict:
    splits = jax.random.split(jax.random.key(seed), 6)
    activations = scatter_about(splits[0], (NT, NX, C, NY), 1.0, 6.0, ((0, 8), (1, 16)))
    spectral_weight = scatter_about(splits[1], (PAIRS, K, C, 2 * C), (2 * C) ** -0.5, 0.5, ((0, 128),), jnp.float32)
    pointwise = scatter_about(splits[2], (C, C), C ** -0.5, 0.75)
    readout = scatter_about(splits[3], (C,), C ** -0.5, 0.75, (), jnp.float32)
    forcing = scatter_about(splits[4], (NX, NY), 2.0, 8.0, ((0, 16),), jnp.float32)
    return dict(activations=activations, spectral_weight=spectral_weight, pointwise=pointwise, readout=readout, forcing=forcing)


VISCOSITY = 0.002
LOSS_WEIGHT = 0.005
PRECISE = lax.Precision.HIGHEST

def contract(left_side, right_side, formula):
    return jnp.einsum(formula, left_side, right_side, precision=PRECISE)

def phases(positions, length, numbers):
    product = positions[:, None] * numbers[None, :] % length
    return 2.0 * math.pi / length * product.astype(jnp.float32)

def mode_numbers(mode_count):
    return jnp.arange(mode_count, dtype=jnp.int32) - mode_count // 2

def pair_angles(time_rows, cell_rows, total_steps, total_cells, mode_count):
    numbers = mode_numbers(mode_count)
    angles = phases(time_rows, total_steps, numbers)[:, None, None, :] + phases(cell_rows, total_cells, numbers)[None, :, :, None]
    return angles.reshape(time_rows.shape[0] * cell_rows.shape[0], mode_count * mode_count)

def line_tables(grid_width, mode_count):
    angles = phases(jnp.arange(grid_width, dtype=jnp.int32), grid_width, mode_numbers(mode_count))
    cos_part = jnp.cos(angles)
    sin_part = jnp.sin(angles)
    forward_table = jnp.concatenate([cos_part, -sin_part], axis=1).astype(jnp.bfloat16)
    inverse_table = jnp.concatenate([cos_part.T, -sin_part.T], axis=0)
    return (forward_table, inverse_table)

def flat_lines(values, table):
    lead = values.shape[:-1]
    flat = jnp.dot(values.reshape(-1, values.shape[-1]), table, preferred_element_type=jnp.float32)
    return flat.reshape(lead + (table.shape[1],))

def channel_map(values, matrix, formula):
    return jnp.einsum(formula, values.astype(jnp.float32), matrix.astype(jnp.float32), precision=PRECISE)

def pair_terms(line_part, angles, first_row, row_count, factor):
    mode_count = line_part.shape[2] // 2
    chosen = lax.dynamic_slice_in_dim(angles, first_row, row_count, 1)
    cos_part = jnp.cos(chosen)
    sin_part = -jnp.sin(chosen)
    real_in = line_part[:, :, :mode_count]
    imag_in = line_part[:, :, mode_count:]
    real_part = contract(jnp.concatenate([cos_part, -sin_part], 0), jnp.concatenate([real_in, imag_in], 0), 'un,uce->nec')
    imag_part = contract(jnp.concatenate([cos_part, sin_part], 0), jnp.concatenate([imag_in, real_in], 0), 'un,uce->nec')
    return factor * jnp.concatenate([real_part, imag_part], axis=1).reshape(row_count, -1)

def pair_fold(running, pieces, first_row, angles):
    row_count = pieces.shape[0]
    mode_count = running.shape[2] // 2
    chosen = lax.dynamic_slice_in_dim(angles, first_row, row_count, 1)
    cos_part = jnp.cos(chosen)
    sin_part = jnp.sin(chosen)
    split_coef = pieces.reshape(row_count, 2, mode_count, -1)
    real_in = split_coef[:, 0]
    imag_in = split_coef[:, 1]
    real_part = contract(jnp.concatenate([cos_part, -sin_part], 1), jnp.concatenate([real_in, imag_in], 0), 'un,neo->uoe')
    imag_part = contract(jnp.concatenate([cos_part, sin_part], 1), jnp.concatenate([imag_in, real_in], 0), 'un,neo->uoe')
    return running + jnp.concatenate([real_part, imag_part], axis=2)

def mix_modes(coefficients, weights):
    pair_count, mode_count, channels = (weights.shape[0], weights.shape[1], weights.shape[2])
    split_coef = coefficients.reshape(pair_count, 2, mode_count, channels)
    weight_real = weights[..., :channels]
    weight_imag = weights[..., channels:]
    real_part = contract(split_coef[:, 0], weight_real, 'nei,neio->neo') - contract(split_coef[:, 1], weight_imag, 'nei,neio->neo')
    imag_part = contract(split_coef[:, 0], weight_imag, 'nei,neio->neo') + contract(split_coef[:, 1], weight_real, 'nei,neio->neo')
    return jnp.stack([real_part, imag_part], axis=1).reshape(pair_count, -1)

def mode_grads(coefficients, weights, grad_mixed):
    pair_count, mode_count, channels = (weights.shape[0], weights.shape[1], weights.shape[2])
    split_coef = coefficients.reshape(pair_count, 2, mode_count, channels)
    split_grad = grad_mixed.reshape(pair_count, 2, mode_count, channels)
    coef_real, coef_imag = (split_coef[:, 0], split_coef[:, 1])
    grad_real, grad_imag = (split_grad[:, 0], split_grad[:, 1])
    weight_real = weights[..., :channels]
    weight_imag = weights[..., channels:]
    weight_grad = jnp.concatenate([contract(coef_real, grad_real, 'nei,neo->neio') + contract(coef_imag, grad_imag, 'nei,neo->neio'), contract(coef_real, grad_imag, 'nei,neo->neio') - contract(coef_imag, grad_real, 'nei,neo->neio')], axis=3)
    coef_grad_real = contract(weight_real, grad_real, 'neio,neo->nei') + contract(weight_imag, grad_imag, 'neio,neo->nei')
    coef_grad_imag = contract(weight_real, grad_imag, 'neio,neo->nei') - contract(weight_imag, grad_real, 'neio,neo->nei')
    return (weight_grad, jnp.stack([coef_grad_real, coef_grad_imag], axis=1).reshape(pair_count, -1))

def cell_waves(total_cells):
    numbers = jnp.arange(total_cells, dtype=jnp.int32)
    signed = jnp.where(numbers < total_cells // 2, numbers, numbers - total_cells).astype(jnp.float32)
    slopes = jnp.where(numbers == total_cells // 2, 0.0, signed).astype(jnp.float32)
    return (signed, slopes)

def wave_factors(signed, column_waves):
    squared = signed[:, None] * signed[:, None] + column_waves[None, :] * column_waves[None, :]
    inverse = jnp.where(squared > 0, 1.0 / jnp.where(squared > 0, squared, 1.0), 0.0)
    return (squared, inverse)

def spectra(values):
    return jnp.fft.fft(jnp.fft.rfft(values, axis=2)[:, :, :NY // 2], axis=1)

def physical(spectrum):
    columns = jnp.fft.ifft(spectrum, axis=1)
    columns = jnp.concatenate([columns, jnp.zeros_like(columns[:, :, :1])], axis=2)
    return jnp.fft.irfft(columns, n=NY, axis=2)

def reference(activations, spectral_weight, pointwise, readout, forcing):
    mode_forward, mode_inverse = line_tables(NY, K)
    grid_scale = 1.0 / math.sqrt(NT * NX * NY)
    mode_scale = 1.0 / math.sqrt(K * K * K)
    time_rows = jnp.arange(NT, dtype=jnp.int32)
    cell_rows = jnp.arange(NX, dtype=jnp.int32)

    def slab_angles(time_now):
        return pair_angles(jnp.reshape(time_now, (1,)), cell_rows, NT, NX, K)

    def slab_lines(values):
        return flat_lines(values, mode_forward)

    def analyze_step(running, item):
        time_now, time_slab = item
        return (running + pair_terms(slab_lines(time_slab), slab_angles(time_now), 0, K * K, grid_scale), None)
    start_modes = jnp.zeros((K * K, 2 * K * C), jnp.float32)
    coefficients, unused = lax.scan(analyze_step, start_modes, (time_rows, activations))
    mixed = mix_modes(coefficients, spectral_weight)

    def synth_slab(coef_all, time_now, factor):
        running = jnp.zeros((NX, C, 2 * K), jnp.float32)
        summed = pair_fold(running, coef_all, 0, slab_angles(time_now))
        return factor * jnp.dot(summed, mode_inverse, precision=PRECISE)

    def hidden_slab(time_now, time_slab):
        return synth_slab(mixed, time_now, mode_scale) + channel_map(time_slab, pointwise, 'xiy,io->xoy')

    def vortex_slab(item):
        time_now, time_slab = item
        return jnp.einsum('xoy,o->xy', jax.nn.gelu(hidden_slab(time_now, time_slab)), readout, precision=PRECISE)
    vorticity = lax.map(vortex_slab, (time_rows, activations))
    signed, slopes = cell_waves(NX)
    column_waves = jnp.arange(NY // 2, dtype=jnp.int32).astype(jnp.float32)
    squared, inverse = wave_factors(signed, column_waves)
    across = slopes[:, None]
    along = column_waves[None, :]
    vortex_hat = spectra(vorticity)
    flow_down = physical(1j * along * inverse * vortex_hat)
    flow_right = physical(-1j * across * inverse * vortex_hat)
    slope_down = physical(1j * across * vortex_hat)
    slope_right = physical(1j * along * vortex_hat)
    curvature = physical(-squared * vortex_hat)
    padded = jnp.pad(vorticity, ((1, 1), (0, 0), (0, 0)))
    time_rate = (padded[2:] - padded[:-2]) * (0.5 * NT)
    inside = ((time_rows > 0) & (time_rows < NT - 1)).astype(jnp.float32)[:, None, None]
    residual = inside * (time_rate + flow_down * slope_down + flow_right * slope_right - VISCOSITY * curvature - forcing[None])
    weighted = LOSS_WEIGHT * residual
    padded_weighted = jnp.pad(weighted, ((1, 1), (0, 0), (0, 0)))
    grad_time = (padded_weighted[:-2] - padded_weighted[2:]) * (0.5 * NT)
    adjoint_hat = VISCOSITY * squared * spectra(weighted) + 1j * (-across * spectra(flow_down * weighted) - along * spectra(flow_right * weighted) - along * inverse * spectra(weighted * slope_down) + across * inverse * spectra(weighted * slope_right))
    grad_vorticity = grad_time + physical(adjoint_hat)

    def grad_step(running, item):
        time_now, time_slab, grad_slab = item
        hidden = hidden_slab(time_now, time_slab)
        primal, gelu_back = jax.vjp(jax.nn.gelu, hidden)
        grad_hidden = gelu_back(readout[None, :, None] * grad_slab[:, None, :])[0].astype(jnp.bfloat16)
        running = running + pair_terms(slab_lines(grad_hidden), slab_angles(time_now), 0, K * K, mode_scale)
        return (running, grad_hidden)
    grad_mixed, grad_hiddens = lax.scan(grad_step, start_modes, (time_rows, activations, grad_vorticity))
    grad_spectral, grad_coefs = mode_grads(coefficients, spectral_weight, grad_mixed)

    def output_slab(item):
        time_now, grad_hidden = item
        summed = synth_slab(grad_coefs, time_now, grid_scale) + channel_map(grad_hidden, pointwise, 'xoy,io->xiy')
        return summed.astype(jnp.bfloat16)
    grad_activations = lax.map(output_slab, (time_rows, grad_hiddens))
    return (grad_activations, grad_spectral)
```

```python
import functools
import math

import jax
import jax.numpy as jnp
import ml_dtypes
import numpy as np
from jax import lax
from jax.experimental import pallas as pl
from jax.experimental.pallas import tpu as pltpu
from jax.sharding import PartitionSpec as P

MESH = pl.DeviceIdType.MESH
VISCOSITY = 0.002
LOSS_WEIGHT = 0.005
C, K, NY, NX, NT = 64, 16, 512, 256, 64
ROWS, TM = 16, 8
CHIPS = ROWS // 2
STEPS, CELLS = NT // TM, NX // ROWS
HALF = NY // 2
S_GRID = 1.0 / math.sqrt(NT * NX * NY)
S_MODE = 1.0 / math.sqrt(K * K * K)
TWO_PI = 2.0 * math.pi
BF16 = jnp.bfloat16
F32 = jnp.float32


def halves(table):
    table = table.astype(np.float32)
    high = table.astype(ml_dtypes.bfloat16)
    low = (table - high.astype(np.float32)).astype(ml_dtypes.bfloat16)
    return high, low


def line_tables():
    numbers = np.arange(K) - K // 2
    angles = (TWO_PI / NY) * (np.outer(numbers, np.arange(NY)) % NY)
    table = np.concatenate([np.cos(angles), -np.sin(angles)], axis=0).astype(np.float32)
    forward = table.astype(ml_dtypes.bfloat16)
    high, low = halves(table)
    return forward, np.concatenate([high, high, low], axis=0)


def time_tables():
    numbers = np.arange(K) - K // 2
    steps = np.arange(NT).reshape(TM, STEPS)
    angles = (TWO_PI / NT) * ((numbers[None, :, None] * steps[:, None, :]) % NT)
    unit = np.eye(K)

    def spread(part):
        return np.einsum("mat,ef->maetf", part, unit).reshape(TM, K * K, STEPS * K)

    cos_part, sin_part = spread(np.cos(angles)), spread(np.sin(angles))
    forward = np.concatenate([cos_part, sin_part], axis=2)
    backward = np.concatenate(
        [cos_part.transpose(0, 2, 1), sin_part.transpose(0, 2, 1)], axis=2
    )
    return forward.astype(np.float32), backward.astype(np.float32)


def row_phases():
    numbers = np.arange(K) - K // 2
    angles = (TWO_PI / ROWS) * (np.outer(np.arange(ROWS), numbers) % ROWS)
    return np.stack([np.cos(angles), np.sin(angles)]).astype(np.float32)


def physics_tables():
    y = np.arange(NY)
    ky = np.arange(HALF)
    angles = (TWO_PI / NY) * (np.outer(y, ky) % NY)
    row_forward = np.concatenate([np.cos(angles), -np.sin(angles)], axis=1)
    scaling = np.where(ky == 0, 1.0, 2.0)[:, None] / NY
    row_back = np.concatenate([scaling * np.cos(angles).T, -scaling * np.sin(angles).T], axis=0)
    gap = np.arange(NY)
    gap_angles = (TWO_PI / NY) * (np.outer(gap, ky) % NY)
    slope = -(2.0 / NY) * (np.sin(gap_angles) * ky).sum(1)
    bend = -(2.0 / NY) * (np.cos(gap_angles) * ky * ky).sum(1)
    turn = (y[None, :] - y[:, None]) % NY
    row_slope, row_bend = slope[turn], bend[turn]
    x = np.arange(NX)
    kx = np.where(x < NX // 2, x, x - NX)
    dx = np.where(x == NX // 2, 0, kx)
    col_angles = (TWO_PI / NX) * (np.outer(x, x) % NX)
    col_slope = -(np.sin(col_angles) * dx).sum(1) / NX
    col_bend = -(np.cos(col_angles) * kx * kx).sum(1) / NX
    col_turn = (x[:, None] - x[None, :]) % NX
    col_slope, col_bend = col_slope[col_turn], col_bend[col_turn]
    col_wave = np.concatenate([np.cos(col_angles), np.sin(col_angles)], axis=0)
    squared = (kx[:, None] ** 2 + ky[None, :] ** 2).astype(np.float64)
    inverse = np.where(squared > 0, 1.0 / np.where(squared > 0, squared, 1.0), 0.0) / NX
    inverse = np.concatenate([inverse, inverse], axis=1).astype(np.float32)
    pairs = [
        halves(t)
        for t in (
            row_forward,
            row_back,
            row_slope,
            VISCOSITY * row_bend,
            col_wave,
            col_slope,
            VISCOSITY * col_bend,
        )
    ]
    return [t for pair in pairs for t in pair] + [inverse]


def low_lanes(shape):
    return lax.broadcasted_iota(jnp.int32, shape, len(shape) - 1) < C


def turned(z):
    moved = pltpu.roll(z, C, len(z.shape) - 1)
    return jnp.where(low_lanes(z.shape), moved, -moved)


def project_rows(lines_ref, phase_ref, store):
    row = lax.axis_index("rows")
    low = low_lanes((8, 2 * C))
    for part in range(2):
        re_rows = slice(8 * part, 8 * part + 8)
        im_rows = slice(K + 8 * part, K + 8 * part + 8)
        z, q = [], []
        for pair in range(CELLS // 2):
            lanes = slice(2 * C * pair, 2 * C * (pair + 1))
            re, im = lines_ref[re_rows, lanes], lines_ref[im_rows, lanes]
            re_moved, im_moved = pltpu.roll(re, C, 1), pltpu.roll(im, C, 1)
            z += [jnp.where(low, re, im_moved), jnp.where(low, re_moved, im)]
            q += [jnp.where(low, im, -re_moved), jnp.where(low, im_moved, -re)]
        for k in range(K // 2 + 1):
            even, odd = None, None
            for x in range(CELLS):
                angle = TWO_PI * (k * x % NX) / NX
                cos_term = z[x] if k * x == 0 else math.cos(angle) * z[x]
                even = cos_term if even is None else even + cos_term
                if k * x:
                    sin_term = math.sin(angle) * q[x]
                    odd = sin_term if odd is None else odd + sin_term
            found = []
            if k < K // 2:
                found.append((K // 2 + k, even if odd is None else even + odd))
            if k > 0:
                found.append((K // 2 - k, even - odd))
            for b, value in found:
                cos_b, sin_b = phase_ref[0, row, b], phase_ref[1, row, b]
                store(b, re_rows, cos_b * value + sin_b * turned(value))


def spread_rows(modes_ref, phase_ref, store):
    row = lax.axis_index("rows")
    for part in range(2):
        rows = slice(8 * part, 8 * part + 8)
        z = []
        for b in range(K):
            cos_b, sin_b = phase_ref[0, row, b], phase_ref[1, row, b]
            value = modes_ref[b, rows, :]
            z.append(cos_b * value - sin_b * turned(value))
        even, odd = [z[K // 2]], [None]
        for k in range(1, K // 2):
            even.append(z[K // 2 + k] + z[K // 2 - k])
            odd.append(turned(z[K // 2 - k] - z[K // 2 + k]))
        even.append(z[0])
        odd.append(turned(z[0]))
        for x in range(CELLS):
            total = even[0]
            for k in range(1, K // 2 + 1):
                angle = TWO_PI * (k * x % NX) / NX
                if x == 0:
                    total = total + even[k]
                else:
                    total = total + math.cos(angle) * even[k] + math.sin(angle) * odd[k]
            store(x, part, total)


def fill_left(left_ref, matrix, modes_ref, phase_ref):
    full = {}

    def store(x, part, total):
        full[x, part] = total

    spread_rows(modes_ref, phase_ref, store)
    for x in range(CELLS):
        whole = jnp.concatenate([full[x, 0], full[x, 1]], axis=0)
        joined = jnp.concatenate([whole[:, :C], pltpu.roll(whole, C, 1)[:, :C]], axis=0)
        high = joined.astype(BF16)
        lower = (joined - high.astype(F32)).astype(BF16)
        left_ref[x] = jnp.concatenate([matrix, high, lower, high], axis=0)


def contract_first(left, right):
    return lax.dot_general(
        left, right, (((0,), (0,)), ((), ())), preferred_element_type=F32
    )


def analyze_kernel(act_ref, table_ref, phase_ref, out_ref, lines):
    flat = act_ref[0].reshape(CELLS * C, NY)
    lines[...] = lax.dot_general(
        table_ref[...], flat, (((1,), (1,)), ((), ())), preferred_element_type=F32
    )

    def store(b, rows, value):
        out_ref[b % 2, b // 2, rows, :] = value

    project_rows(lines, phase_ref, store)


def hidden_kernel(
    act_ref, modes_ref, matrix_ref, table_ref, readout_ref, phase_ref, slope_ref, vort_ref, left
):
    fill_left(left, matrix_ref[...], modes_ref, phase_ref)
    c0 = math.sqrt(2.0 / math.pi)
    c1 = c0 * 0.044715

    def body(x, carry):
        right = jnp.concatenate([act_ref[0, x], table_ref[...]], axis=0)
        hidden = contract_first(left[x], right)
        square = hidden * hidden
        level = 0.5 + 0.5 * jnp.tanh(hidden * (c0 + c1 * square))
        value = hidden * level
        readout = readout_ref[...]
        slope = level + value * (1.0 - level) * (2.0 * c0 + 6.0 * c1 * square)
        slope_ref[0, x] = readout * slope
        vort_ref[0, pl.ds(x, 1), :] = jnp.sum(readout * value, axis=0, keepdims=True)
        return carry

    lax.fori_loop(0, CELLS, body, 0, unroll=2)


def physics_kernel(plane_ref, forcing_ref, *rest):
    tables, out_ref = rest[:-1], rest[-1]
    (rf, rf_low, rb, rb_low, rs, rs_low, rc, rc_low, cw, cw_low, cs, cs_low, cc, cc_low, inverse) = (
        tables
    )

    def parts(value):
        high = value.astype(BF16)
        return high, (value - high.astype(F32)).astype(BF16)

    def dot(a, b):
        return jnp.dot(a, b, preferred_element_type=F32)

    def along(value, high, low):
        v_high, v_low = parts(value)
        return dot(v_high, high[...]) + (dot(v_low, high[...]) + dot(v_high, low[...]))

    def across(high, low, value):
        v_high, v_low = parts(value)
        return dot(high[...], v_high) + (dot(high[...], v_low) + dot(low[...], v_high))

    def minus_i(z):
        return jnp.concatenate([z[:, HALF:], -z[:, :HALF]], axis=1)

    def solve(value):
        spectrum = along(value, rf, rf_low)
        both = across(cw, cw_low, spectrum)
        spectrum = (both[:NX] + minus_i(both[NX:])) * inverse[...]
        both = across(cw, cw_low, spectrum)
        return along(both[:NX] - minus_i(both[NX:]), rb, rb_low)

    sign = jnp.where(lax.broadcasted_iota(jnp.int32, (NX, NY), 1) % 2 == 0, 1.0, -1.0).astype(F32)

    def smooth(value):
        return value - sign * (jnp.sum(value * sign, axis=1, keepdims=True) * (1.0 / NY))

    step = lax.axis_index("tm") * STEPS + lax.axis_index("rows") // 2
    inside = (step > 0) & (step < NT - 1)
    vort = plane_ref[0].reshape(NX, NY)
    rate = plane_ref[1].reshape(NX, NY)
    stream = solve(vort)
    slopes = along(jnp.concatenate([vort, stream], axis=0), rs, rs_low)
    slope_right, flow_down = slopes[:NX], slopes[NX:]
    smoothed = smooth(vort)
    slopes = across(cs, cs_low, jnp.concatenate([smoothed, stream], axis=1))
    slope_down, flow_right = slopes[:, :NY], -slopes[:, NY:]
    bend = along(vort, rc, rc_low) + across(cc, cc_low, smoothed)
    residual = (
        rate * (0.5 * NT)
        + flow_down * slope_down
        + flow_right * slope_right
        - bend
        - forcing_ref[...]
    )
    weighted = jnp.where(inside, LOSS_WEIGHT * residual, 0.0)
    first = weighted * slope_down
    second = weighted * slope_right
    slopes = along(jnp.concatenate([first, flow_right * weighted], axis=0), rs, rs_low)
    first_along, flow_along = slopes[:NX], slopes[NX:]
    slopes = across(
        cs, cs_low, jnp.concatenate([second, smooth(flow_down * weighted)], axis=1)
    )
    second_across, flow_across = slopes[:, :NY], slopes[:, NY:]
    solved = solve(second_across - first_along)
    bend = along(weighted, rc, rc_low) + across(cc, cc_low, smooth(weighted))
    grad = solved - bend - flow_across - flow_along
    out_ref[:, 0] = grad.reshape(ROWS, CELLS, NY)
    out_ref[:, 1] = weighted.reshape(ROWS, CELLS, NY)


def grad_kernel(slope_ref, grad_ref, table_ref, phase_ref, hidden_ref, out_ref, lines):
    for x in range(CELLS):
        value = (slope_ref[0, x] * grad_ref[0, x : x + 1, :]).astype(BF16)
        hidden_ref[0, x] = value
    flat = hidden_ref[0].reshape(CELLS * C, NY)
    lines[...] = lax.dot_general(
        table_ref[...], flat, (((1,), (1,)), ((), ())), preferred_element_type=F32
    )

    def store(b, rows, value):
        out_ref[b % 2, b // 2, rows, :] = value

    project_rows(lines, phase_ref, store)


def output_kernel(hidden_ref, modes_ref, matrix_ref, table_ref, phase_ref, out_ref, left):
    fill_left(left, matrix_ref[...], modes_ref, phase_ref)

    def body(x, carry):
        right = jnp.concatenate([hidden_ref[0, x], table_ref[...]], axis=0)
        out_ref[0, x] = contract_first(left[x], right).astype(BF16)
        return carry

    lax.fori_loop(0, CELLS, body, 0, unroll=2)


def remote(src, dst, send, recv, device):
    return pltpu.make_async_remote_copy(
        src_ref=src, dst_ref=dst, send_sem=send, recv_sem=recv, device_id=device,
        device_id_type=MESH,
    )


def place():
    row, slab = lax.axis_index("rows"), lax.axis_index("tm")
    return row, slab, row // 2, row % 2


def loop(first, last, body):
    def step(j, carry):
        body(j)
        return carry

    lax.fori_loop(first, last, step, 0)


def mode_kernel(
    gradient, m_ref, w_ref, tf_hbm, ts_hbm, out_ref, coef_ref,
    tf, ts, from_core, from_rows, terms, from_slabs, mixed, slabs, gathered,
    load, core_send, core_recv, row_send, row_recv, slab_send, slab_recv,
    mix_send, mix_recv, out_send, out_recv, pass_send, pass_recv,
):
    row, slab, chip, core = place()
    other = row + 1 - 2 * core
    load_f = pltpu.make_async_copy(tf_hbm.at[slab], tf, load.at[0])
    load_s = pltpu.make_async_copy(ts_hbm.at[slab], ts, load.at[1])
    load_f.start()
    load_s.start()
    barrier = pltpu.get_barrier_semaphore()
    pl.semaphore_signal(barrier, inc=1, device_id=(other, slab), device_id_type=MESH)

    def greet(j):
        peer = 2 * ((chip + j) % CHIPS) + core
        pl.semaphore_signal(barrier, inc=1, device_id=(peer, slab), device_id_type=MESH)
        pl.semaphore_signal(
            barrier, inc=1, device_id=(row, (slab + j) % TM), device_id_type=MESH
        )

    loop(1, CHIPS, greet)
    pl.semaphore_wait(barrier, 1 + (CHIPS - 1) + (TM - 1))

    def core_copy(j):
        to = (chip + j) % CHIPS
        return remote(
            m_ref.at[1 - core, to], from_core.at[to], core_send.at[to], core_recv.at[to],
            (other, slab),
        )

    loop(1, CHIPS + 1, lambda j: core_copy(j).start())

    def row_copy(j):
        to = (chip + j) % CHIPS
        return remote(
            from_core.at[to], from_rows.at[chip], row_send.at[to], row_recv.at[chip],
            (2 * to + core, slab),
        )

    def forward(j):
        to = (chip + j) % CHIPS
        core_copy(j).wait_recv()
        from_core[to] = from_core[to] + m_ref[core, to]
        row_copy(j).start()

    loop(1, CHIPS, forward)
    core_copy(CHIPS).wait_recv()
    from_rows[chip] = from_core[chip] + m_ref[core, chip]

    def row_arrival(j):
        source = (chip + CHIPS - j) % CHIPS
        remote(
            from_core.at[source], from_rows.at[source], row_send.at[source],
            row_recv.at[source], (2 * source + core, slab),
        ).wait_recv()

    loop(1, CHIPS, row_arrival)
    total = from_rows[0]
    for source in range(1, CHIPS):
        total = total + from_rows[source]
    load_f.wait()
    found = jnp.dot(
        tf[...], jnp.concatenate([total, turned(total)], axis=0),
        precision=lax.Precision.HIGHEST, preferred_element_type=F32,
    )
    terms[...] = (found * (S_MODE if gradient else S_GRID)).reshape(TM, 2 * K, 2 * C)

    def slab_copy(j):
        to = (slab + j) % TM
        return remote(
            terms.at[to], from_slabs.at[slab], slab_send.at[to], slab_recv.at[slab], (row, to)
        )

    loop(1, TM, lambda j: slab_copy(j).start())
    from_slabs[slab] = terms[slab]

    def slab_arrival(j):
        source = (slab + TM - j) % TM
        remote(
            terms.at[source], from_slabs.at[source], slab_send.at[source],
            slab_recv.at[source], (row, source),
        ).wait_recv()

    loop(1, TM, slab_arrival)
    coef = from_slabs[0]
    for source in range(1, TM):
        coef = coef + from_slabs[source]
    coef_ref[...] = coef
    if gradient:
        turned_coef = turned(coef)
        lane = lax.broadcasted_iota(jnp.int32, (C, 2 * C), 1)
        real = jnp.zeros((C, 2 * C), F32)
        imag = jnp.zeros((C, 2 * C), F32)
        for a in range(2):
            for e in range(K):
                j = a * K + e
                weight = w_ref[a, e]
                re = jnp.sum(weight * coef[j : j + 1, :], axis=1, keepdims=True)
                im = jnp.sum(weight * turned_coef[j : j + 1, :], axis=1, keepdims=True)
                real = jnp.where(lane == j, re, real)
                imag = jnp.where(lane == j, im, imag)
        mixed[...] = jnp.transpose(jnp.concatenate([real, imag], axis=0))[: 2 * K]
    else:
        columns = jnp.transpose(
            jnp.concatenate([coef, jnp.zeros((2 * C - 2 * K, 2 * C), F32)], axis=0)
        )
        for a in range(2):
            for e in range(K):
                j = a * K + e
                weight = w_ref[a, e]
                re = jnp.sum(weight * columns[:C, j : j + 1], axis=0, keepdims=True)
                im = jnp.sum(weight * columns[C:, j : j + 1], axis=0, keepdims=True)
                mixed[j : j + 1, :] = re - turned(im)

    def mix_copy(j):
        to = (slab + j) % TM
        return remote(mixed, slabs.at[slab], mix_send.at[to], mix_recv.at[slab], (row, to))

    loop(1, TM, lambda j: mix_copy(j).start())
    slabs[slab] = mixed[...]

    def mix_arrival(j):
        source = (slab + TM - j) % TM
        remote(
            mixed, slabs.at[source], mix_send.at[source], mix_recv.at[source], (row, source)
        ).wait_recv()

    loop(1, TM, mix_arrival)
    load_s.wait()
    whole = slabs[...].reshape(K * K, 2 * C)
    gathered[row] = (S_GRID if gradient else S_MODE) * jnp.dot(
        ts[...], jnp.concatenate([whole, -turned(whole)], axis=0),
        precision=lax.Precision.HIGHEST, preferred_element_type=F32,
    )

    def out_copy(j):
        to = (chip + j) % CHIPS
        return remote(
            gathered.at[row], gathered.at[row], out_send.at[to], out_recv.at[chip],
            (2 * to + core, slab),
        )

    def pass_copy(source):
        block = 2 * source + core
        return remote(
            gathered.at[block], gathered.at[block], pass_send.at[source], pass_recv.at[source],
            (other, slab),
        )

    def pass_arrival(source):
        block = 2 * source + 1 - core
        remote(
            gathered.at[block], gathered.at[block], pass_send.at[source], pass_recv.at[source],
            (other, slab),
        ).wait_recv()

    loop(1, CHIPS, lambda j: out_copy(j).start())
    pass_copy(chip).start()

    def out_arrival(j):
        source = (chip + CHIPS - j) % CHIPS
        block = 2 * source + core
        remote(
            gathered.at[block], gathered.at[block], out_send.at[source], out_recv.at[source],
            (2 * source + core, slab),
        ).wait_recv()
        pass_copy(source).start()

    loop(1, CHIPS, out_arrival)
    loop(0, CHIPS, pass_arrival)
    out_ref[...] = gathered[...]
    loop(1, CHIPS + 1, lambda j: core_copy(j).wait_send())
    loop(1, CHIPS, lambda j: row_copy(j).wait_send())
    loop(1, TM, lambda j: slab_copy(j).wait_send())
    loop(1, TM, lambda j: mix_copy(j).wait_send())
    loop(1, CHIPS, lambda j: out_copy(j).wait_send())
    loop(0, CHIPS, lambda j: pass_copy(j).wait_send())


def plane_kernel(
    vort_ref, out_ref, halo, rates, planes,
    halo_send, halo_recv, send, recv, pass_send, pass_recv,
):
    row, slab, chip, core = place()
    other = row + 1 - 2 * core
    after, before = (slab + 1) % TM, (slab + TM - 1) % TM
    barrier = pltpu.get_barrier_semaphore()
    for peer in (after, before):
        pl.semaphore_signal(barrier, inc=1, device_id=(row, peer), device_id_type=MESH)
    pl.semaphore_signal(barrier, inc=1, device_id=(other, slab), device_id_type=MESH)

    def greet(j):
        peer = 2 * ((chip + j) % CHIPS) + core
        pl.semaphore_signal(barrier, inc=1, device_id=(peer, slab), device_id_type=MESH)

    loop(1, CHIPS, greet)
    pl.semaphore_wait(barrier, 3 + CHIPS - 1)
    to_after = remote(
        vort_ref.at[STEPS - 1], halo.at[0], halo_send.at[0], halo_recv.at[0], (row, after)
    )
    to_before = remote(vort_ref.at[0], halo.at[1], halo_send.at[1], halo_recv.at[1], (row, before))
    to_after.start()
    to_before.start()

    def copy(field, j):
        to = (chip + j) % CHIPS
        source = (vort_ref, rates)[field].at[to]
        return remote(
            source, planes.at[field, row], send.at[field, to], recv.at[field, chip],
            (2 * to + core, slab),
        )

    def pass_copy(field, source):
        block = 2 * source + core
        return remote(
            planes.at[field, block], planes.at[field, block], pass_send.at[field, source],
            pass_recv.at[field, source], (other, slab),
        )

    def arrival(field, j):
        source = (chip + CHIPS - j) % CHIPS
        block = 2 * source + core
        remote(
            vort_ref.at[source], planes.at[field, block], send.at[field, source],
            recv.at[field, source], (block, slab),
        ).wait_recv()
        pass_copy(field, source).start()

    def pass_arrival(field, source):
        block = 2 * source + 1 - core
        remote(
            planes.at[field, block], planes.at[field, block], pass_send.at[field, source],
            pass_recv.at[field, source], (other, slab),
        ).wait_recv()

    loop(1, CHIPS, lambda j: copy(0, j).start())
    planes[0, row] = vort_ref[chip]
    pass_copy(0, chip).start()
    for step in range(1, STEPS - 1):
        rates[step] = vort_ref[step + 1] - vort_ref[step - 1]
    to_after.wait_recv()
    to_before.wait_recv()
    rates[0] = vort_ref[1] - halo[0]
    rates[STEPS - 1] = halo[1] - vort_ref[STEPS - 2]
    loop(1, CHIPS, lambda j: copy(1, j).start())
    planes[1, row] = rates[chip]
    pass_copy(1, chip).start()
    for field in range(2):
        loop(1, CHIPS, functools.partial(arrival, field))
    for field in range(2):
        loop(0, CHIPS, functools.partial(pass_arrival, field))
    out_ref[...] = planes[...]
    to_after.wait_send()
    to_before.wait_send()
    for field in range(2):
        loop(1, CHIPS, lambda j: copy(field, j).wait_send())
        loop(0, CHIPS, lambda j: pass_copy(field, j).wait_send())


def return_kernel(in_ref, out_ref, steps, halo, send, recv, halo_send, halo_recv):
    row, slab, chip, core = place()
    after, before = (slab + 1) % TM, (slab + TM - 1) % TM
    barrier = pltpu.get_barrier_semaphore()
    for peer in (after, before):
        pl.semaphore_signal(barrier, inc=1, device_id=(row, peer), device_id_type=MESH)

    def greet(j):
        peer = 2 * ((chip + j) % CHIPS) + core
        pl.semaphore_signal(barrier, inc=1, device_id=(peer, slab), device_id_type=MESH)

    loop(1, CHIPS, greet)
    pl.semaphore_wait(barrier, 2 + CHIPS - 1)

    def copy(j):
        to = (chip + j) % CHIPS
        block = 2 * to + core
        return remote(
            in_ref.at[block], steps.at[chip], send.at[to], recv.at[chip], (block, slab)
        )

    loop(1, CHIPS, lambda j: copy(j).start())
    steps[chip] = in_ref[row]

    def arrival(source):
        @pl.when(source != chip)
        def _():
            remote(
                in_ref.at[2 * source + core], steps.at[source], send.at[source],
                recv.at[source], (2 * source + core, slab),
            ).wait_recv()

    arrival(STEPS - 1)
    to_after = remote(
        steps.at[STEPS - 1, 1], halo.at[0], halo_send.at[0], halo_recv.at[0], (row, after)
    )
    to_after.start()
    arrival(0)
    to_before = remote(steps.at[0, 1], halo.at[1], halo_send.at[1], halo_recv.at[1], (row, before))
    to_before.start()
    loop(1, STEPS - 1, arrival)
    for step in range(1, STEPS - 1):
        out_ref[step] = steps[step, 0] + (0.5 * NT) * (steps[step - 1, 1] - steps[step + 1, 1])
    to_after.wait_recv()
    out_ref[0] = steps[0, 0] + (0.5 * NT) * (halo[0] - steps[1, 1])
    to_before.wait_recv()
    out_ref[STEPS - 1] = steps[STEPS - 1, 0] + (0.5 * NT) * (steps[STEPS - 2, 1] - halo[1])
    to_after.wait_send()
    to_before.wait_send()
    loop(1, CHIPS, lambda j: copy(j).wait_send())


VMEM = pl.BlockSpec(memory_space=pltpu.VMEM)
SMEM = pl.BlockSpec(memory_space=pltpu.SMEM)
ANY = pl.BlockSpec(memory_space=pl.ANY)
DMA = pltpu.SemaphoreType.DMA
LIMIT = 56 * 1024 * 1024


def params(collective_id=None):
    if collective_id is None:
        return pltpu.CompilerParams(vmem_limit_bytes=LIMIT)
    return pltpu.CompilerParams(
        collective_id=collective_id, has_side_effects=True, vmem_limit_bytes=LIMIT
    )


def whole_spec(shape):
    return pl.BlockSpec(shape, lambda t: (0,) * len(shape))


def step_spec(shape):
    return pl.BlockSpec((1,) + shape, lambda t: (t,) + (0,) * len(shape))


FIELD = (CELLS, C, NY)
MODES_IN = pl.BlockSpec((K, K, 2 * C), lambda t: (0, t, 0))
MODES_OUT = pl.BlockSpec((2, CHIPS, K, 2 * C), lambda t: (0, 0, t, 0))
MODES = jax.ShapeDtypeStruct((2, CHIPS, STEPS * K, 2 * C), F32)


def run_modes(gradient, terms, weights, tables):
    block = (STEPS * K, 2 * C)
    return pl.pallas_call(
        functools.partial(mode_kernel, gradient),
        out_shape=(
            jax.ShapeDtypeStruct((K,) + block, F32),
            jax.ShapeDtypeStruct((2 * K, 2 * C), F32),
        ),
        in_specs=[VMEM, VMEM, ANY, ANY],
        out_specs=(VMEM, VMEM),
        scratch_shapes=[
            pltpu.VMEM((K * K, 2 * STEPS * K), F32),
            pltpu.VMEM((STEPS * K, 2 * K * K), F32),
            pltpu.VMEM((CHIPS,) + block, F32),
            pltpu.VMEM((CHIPS,) + block, F32),
            pltpu.VMEM((TM, 2 * K, 2 * C), F32),
            pltpu.VMEM((TM, 2 * K, 2 * C), F32),
            pltpu.VMEM((2 * K, 2 * C), F32),
            pltpu.VMEM((TM, 2 * K, 2 * C), F32),
            pltpu.VMEM((K,) + block, F32),
            DMA((2,)),
            *[DMA((8,))] * 12,
        ],
        compiler_params=params(3 if gradient else 0),
        name="grad_modes" if gradient else "modes",
    )(terms, weights, *tables)


def shards(activations, spectral_weight, pointwise, readout, forcing):
    line_forward, line_back = (jnp.asarray(t) for t in line_tables())
    phases = jnp.asarray(row_phases())
    time_parts = tuple(jnp.asarray(t) for t in time_tables())
    physics = [jnp.asarray(t) for t in physics_tables()]
    readout_wide = jnp.broadcast_to(readout[:, None], (C, NY))
    forcing_whole = lax.all_gather(forcing, "rows", axis=0, tiled=True)
    lines_scratch = pltpu.VMEM((2 * K, CELLS * C), F32)
    left_scratch = pltpu.VMEM((CELLS, C + 6 * K, C), BF16)

    terms = pl.pallas_call(
        analyze_kernel,
        grid=(STEPS,),
        out_shape=MODES,
        in_specs=[step_spec(FIELD), whole_spec((2 * K, NY)), SMEM],
        out_specs=MODES_OUT,
        scratch_shapes=[lines_scratch],
        compiler_params=params(),
        name="analyze",
    )(activations, line_forward, phases)

    modes, coef = run_modes(False, terms, spectral_weight, time_parts)

    slopes, vorticity = pl.pallas_call(
        hidden_kernel,
        grid=(STEPS,),
        out_shape=(
            jax.ShapeDtypeStruct((STEPS,) + FIELD, F32),
            jax.ShapeDtypeStruct((STEPS, CELLS, NY), F32),
        ),
        in_specs=[
            step_spec(FIELD), MODES_IN, whole_spec((C, C)), whole_spec((6 * K, NY)),
            whole_spec((C, NY)), SMEM,
        ],
        out_specs=(step_spec(FIELD), step_spec((CELLS, NY))),
        scratch_shapes=[left_scratch],
        compiler_params=params(),
        name="hidden",
    )(activations, modes, pointwise, line_back, readout_wide, phases)

    plane = (2, ROWS, CELLS, NY)
    planes = pl.pallas_call(
        plane_kernel,
        out_shape=jax.ShapeDtypeStruct(plane, F32),
        in_specs=[VMEM],
        out_specs=VMEM,
        scratch_shapes=[
            pltpu.VMEM((2, CELLS, NY), F32),
            pltpu.VMEM((STEPS, CELLS, NY), F32),
            pltpu.VMEM(plane, F32),
            DMA((2,)),
            DMA((2,)),
            *[DMA((2, CHIPS))] * 4,
        ],
        compiler_params=params(1),
        name="planes",
    )(vorticity)

    returned = pl.pallas_call(
        physics_kernel,
        out_shape=jax.ShapeDtypeStruct((ROWS, 2, CELLS, NY), F32),
        in_specs=[VMEM] * (2 + len(physics)),
        out_specs=VMEM,
        compiler_params=params(),
        name="physics",
    )(planes, forcing_whole, *physics)

    grad_vorticity = pl.pallas_call(
        return_kernel,
        out_shape=jax.ShapeDtypeStruct((STEPS, CELLS, NY), F32),
        in_specs=[VMEM],
        out_specs=VMEM,
        scratch_shapes=[
            pltpu.VMEM((CHIPS, 2, CELLS, NY), F32),
            pltpu.VMEM((2, CELLS, NY), F32),
            DMA((CHIPS,)),
            DMA((CHIPS,)),
            DMA((2,)),
            DMA((2,)),
        ],
        compiler_params=params(2),
        name="steps",
    )(returned)

    grad_hidden, grad_terms = pl.pallas_call(
        grad_kernel,
        grid=(STEPS,),
        out_shape=(jax.ShapeDtypeStruct((STEPS,) + FIELD, BF16), MODES),
        in_specs=[
            step_spec(FIELD), step_spec((CELLS, NY)), whole_spec((2 * K, NY)), SMEM,
        ],
        out_specs=(step_spec(FIELD), MODES_OUT),
        scratch_shapes=[lines_scratch],
        compiler_params=params(),
        name="grad",
    )(slopes, grad_vorticity, line_forward, phases)

    grad_modes, grad_mixed = run_modes(True, grad_terms, spectral_weight, time_parts)

    grad_activations = pl.pallas_call(
        output_kernel,
        grid=(STEPS,),
        out_shape=jax.ShapeDtypeStruct((STEPS,) + FIELD, BF16),
        in_specs=[
            step_spec(FIELD), MODES_IN, whole_spec((C, C)), whole_spec((6 * K, NY)), SMEM,
        ],
        out_specs=step_spec(FIELD),
        scratch_shapes=[left_scratch],
        compiler_params=params(),
        name="output",
    )(grad_hidden, grad_modes, pointwise.T, line_back, phases)

    turned_mixed = jnp.concatenate([grad_mixed[:, C:], -grad_mixed[:, :C]], axis=1)
    grad_spectral = (
        coef[:, :C, None] * grad_mixed[:, None, :] + coef[:, C:, None] * turned_mixed[:, None, :]
    )
    return grad_activations, grad_spectral.reshape(2, K, C, 2 * C)


def solution(mesh):
    return jax.shard_map(
        shards,
        mesh=mesh,
        in_specs=(
            P("tm", "rows", None, None),
            P(("rows", "tm"), None, None, None),
            P(),
            P(),
            P("rows", None),
        ),
        out_specs=(P("tm", "rows", None, None), P(("rows", "tm"), None, None, None)),
        check_vma=False,
    )
```

```python
import math

import jax
import jax.numpy as jnp
import ml_dtypes
import numpy as np
from jax import lax
from jax.experimental import pallas as pl
from jax.experimental.pallas import tpu as pltpu
from jax.sharding import PartitionSpec as P

MESH = pl.DeviceIdType.MESH
VISCOSITY = 0.002
LOSS_WEIGHT = 0.005
C, K, NY, NX, NT = 64, 16, 512, 256, 64
ROWS, TM = 16, 8
CHIPS = ROWS // 2
STEPS, CELLS = NT // TM, NX // ROWS
HALF = NY // 2
GROUP, LANES = 4, 128
S_GRID = 1.0 / math.sqrt(NT * NX * NY)
S_MODE = 1.0 / math.sqrt(K * K * K)
TWO_PI = 2.0 * math.pi
BF16 = jnp.bfloat16
F32 = jnp.float32


def halves(table):
    table = table.astype(np.float32)
    high = table.astype(ml_dtypes.bfloat16)
    low = (table - high.astype(np.float32)).astype(ml_dtypes.bfloat16)
    return high, low


def line_tables():
    numbers = np.arange(K) - K // 2
    angles = (TWO_PI / NY) * (np.outer(numbers, np.arange(NY)) % NY)
    table = np.concatenate([np.cos(angles), -np.sin(angles)], axis=0).astype(np.float32)
    forward = np.zeros((GROUP, NY, LANES), ml_dtypes.bfloat16)
    back = np.zeros((GROUP, LANES, NY), ml_dtypes.bfloat16)
    high, low = halves(table)
    for t in range(GROUP):
        forward[t, :, 2 * K * t : 2 * K * (t + 1)] = table.astype(ml_dtypes.bfloat16).T
        for place, part in enumerate((high, high, low)):
            first = 2 * K * ((t + place) % GROUP)
            back[t, first : first + 2 * K] = part
    return forward, back


def time_tables():
    numbers = np.arange(K) - K // 2
    steps = np.arange(NT).reshape(TM, STEPS)
    angles = (TWO_PI / NT) * ((numbers[None, :, None] * steps[:, None, :]) % NT)
    unit = np.eye(K)

    def spread(real, imag):
        both = np.stack([real, imag], axis=3)
        return np.einsum("matr,ef->maetrf", both, unit).reshape(TM, K * K, STEPS * 2 * K)

    cos_part, sin_part = np.cos(angles), np.sin(angles)
    forward = spread(cos_part, sin_part)
    back = np.concatenate([spread(cos_part, sin_part), spread(-sin_part, cos_part)], axis=1)
    return forward.astype(np.float32), back.astype(np.float32)


def row_phases():
    numbers = np.arange(K) - K // 2
    angles = (TWO_PI / ROWS) * (np.outer(np.arange(ROWS), numbers) % ROWS)
    return np.stack([np.cos(angles), np.sin(angles)]).astype(np.float32)


def physics_tables():
    y = np.arange(NY)
    ky = np.arange(HALF)
    angles = (TWO_PI / NY) * (np.outer(y, ky) % NY)
    row_forward = np.concatenate([np.cos(angles), -np.sin(angles)], axis=1)
    scaling = np.where(ky == 0, 1.0, 2.0)[:, None] / NY
    row_back = np.concatenate([scaling * np.cos(angles).T, -scaling * np.sin(angles).T], axis=0)
    gap = np.arange(NY)
    gap_angles = (TWO_PI / NY) * (np.outer(gap, ky) % NY)
    slope = -(2.0 / NY) * (np.sin(gap_angles) * ky).sum(1)
    bend = -(2.0 / NY) * (np.cos(gap_angles) * ky * ky).sum(1)
    turn = (y[None, :] - y[:, None]) % NY
    row_slope, row_bend = slope[turn], bend[turn]
    x = np.arange(NX)
    kx = np.where(x < NX // 2, x, x - NX)
    dx = np.where(x == NX // 2, 0, kx)
    col_angles = (TWO_PI / NX) * (np.outer(x, x) % NX)
    col_slope = -(np.sin(col_angles) * dx).sum(1) / NX
    col_bend = -(np.cos(col_angles) * kx * kx).sum(1) / NX
    col_turn = (x[:, None] - x[None, :]) % NX
    col_slope, col_bend = col_slope[col_turn], col_bend[col_turn]
    col_wave = np.concatenate([np.cos(col_angles), np.sin(col_angles)], axis=0)
    squared = (kx[:, None] ** 2 + ky[None, :] ** 2).astype(np.float64)
    inverse = np.where(squared > 0, 1.0 / np.where(squared > 0, squared, 1.0), 0.0) / NX
    inverse = np.concatenate([inverse, inverse], axis=1).astype(np.float32)
    pairs = [
        halves(t)
        for t in (
            row_forward,
            row_back,
            row_slope,
            VISCOSITY * row_bend,
            col_wave,
            col_slope,
            VISCOSITY * col_bend,
        )
    ]
    return [t for pair in pairs for t in pair] + [inverse]


def turned_halves(z):
    moved = pltpu.roll(z, C, 1)
    low = lax.broadcasted_iota(jnp.int32, z.shape, 1) < C
    return jnp.where(low, moved, -moved)


def turned(z):
    real = lax.broadcasted_iota(jnp.int32, z.shape, 1) % (2 * K) < K
    return jnp.where(real, pltpu.roll(z, LANES - K, 1), -pltpu.roll(z, K, 1))


def loop(first, last, body, unroll=1):
    def step(j, carry):
        body(j)
        return carry

    lax.fori_loop(first, last, step, 0, unroll=unroll)


def project_rows(lines, phase_ref, store):
    row = lax.axis_index("rows")

    def part(chunk):
        rows = pl.ds(pl.multiple_of(8 * chunk, 8), 8)
        z = [lines[x, rows, :] for x in range(CELLS)]
        q = [turned(value) for value in z]
        for k in range(K // 2 + 1):
            even, odd = None, None
            for x in range(CELLS):
                angle = TWO_PI * (k * x % NX) / NX
                cos_term = z[x] if k * x == 0 else math.cos(angle) * z[x]
                even = cos_term if even is None else even + cos_term
                if k * x:
                    sin_term = math.sin(angle) * q[x]
                    odd = sin_term if odd is None else odd + sin_term
            found = []
            if k < K // 2:
                found.append((K // 2 + k, even if odd is None else even + odd))
            if k > 0:
                found.append((K // 2 - k, even - odd))
            for b, value in found:
                cos_b, sin_b = phase_ref[0, row, b], phase_ref[1, row, b]
                store(b, rows, cos_b * value + sin_b * turned(value))

    loop(0, C // 8, part)


def spread_rows(modes, phase_ref, spread):
    row = lax.axis_index("rows")

    def part(chunk):
        rows = pl.ds(pl.multiple_of(8 * chunk, 8), 8)
        z = []
        for b in range(K):
            cos_b, sin_b = phase_ref[0, row, b], phase_ref[1, row, b]
            value = modes(b, rows)
            z.append(cos_b * value - sin_b * turned(value))
        even, odd = [z[K // 2]], [None]
        for k in range(1, K // 2):
            even.append(z[K // 2 + k] + z[K // 2 - k])
            odd.append(turned(z[K // 2 - k] - z[K // 2 + k]))
        even.append(z[0])
        odd.append(turned(z[0]))
        for x in range(CELLS):
            total = even[0]
            for k in range(1, K // 2 + 1):
                angle = TWO_PI * (k * x % NX) / NX
                if x == 0:
                    total = total + even[k]
                else:
                    total = total + math.cos(angle) * even[k] + math.sin(angle) * odd[k]
            spread[x, rows, :] = total

    loop(0, C // 8, part)


def fill_block(block, matrix):
    block[...] = jnp.zeros_like(block)
    for x in range(GROUP):
        block[C * x : C * (x + 1), C * x : C * (x + 1)] = matrix


def combine(block, field, spread, back, t):
    total = spread.reshape(GROUP * C, LANES)
    high = total.astype(BF16).astype(F32)
    lane = lax.broadcasted_iota(jnp.int32, total.shape, 1) // (2 * K)
    left = jnp.where(
        lane == t,
        high,
        jnp.where(lane == (t + 1) % GROUP, pltpu.roll(total - high, 2 * K, 1),
                  pltpu.roll(high, 4 * K, 1)),
    ).astype(BF16)
    return jnp.dot(
        block, field.reshape(GROUP * C, NY), preferred_element_type=F32
    ) + jnp.dot(left, back, preferred_element_type=F32)


def physics_kernel(plane_ref, *rest):
    tables, out_ref = rest[:-1], rest[-1]
    (rf, rf_low, rb, rb_low, rs, rs_low, rc, rc_low, cw, cw_low, cs, cs_low, cc, cc_low, inverse) = (
        tables
    )

    def parts(value):
        high = value.astype(BF16)
        return high, (value - high.astype(F32)).astype(BF16)

    def dot(a, b):
        return jnp.dot(a, b, preferred_element_type=F32)

    def along(value, high, low):
        v_high, v_low = parts(value)
        return dot(v_high, high[...]) + (dot(v_low, high[...]) + dot(v_high, low[...]))

    def across(high, low, value):
        v_high, v_low = parts(value)
        return dot(high[...], v_high) + (dot(high[...], v_low) + dot(low[...], v_high))

    def minus_i(z):
        return jnp.concatenate([z[:, HALF:], -z[:, :HALF]], axis=1)

    def solve(value):
        spectrum = along(value, rf, rf_low)
        both = across(cw, cw_low, spectrum)
        spectrum = (both[:NX] + minus_i(both[NX:])) * inverse[...]
        both = across(cw, cw_low, spectrum)
        return along(both[:NX] - minus_i(both[NX:]), rb, rb_low)

    sign = jnp.where(lax.broadcasted_iota(jnp.int32, (NX, NY), 1) % 2 == 0, 1.0, -1.0).astype(F32)

    def smooth(value):
        return value - sign * (jnp.sum(value * sign, axis=1, keepdims=True) * (1.0 / NY))

    step = lax.axis_index("tm") * STEPS + lax.axis_index("rows") // 2
    inside = (step > 0) & (step < NT - 1)
    vort = plane_ref[0].reshape(NX, NY)
    rate = plane_ref[1].reshape(NX, NY)
    stream = solve(vort)
    slopes = along(jnp.concatenate([vort, stream], axis=0), rs, rs_low)
    slope_right, flow_down = slopes[:NX], slopes[NX:]
    smoothed = smooth(vort)
    slopes = across(cs, cs_low, jnp.concatenate([smoothed, stream], axis=1))
    slope_down, flow_right = slopes[:, :NY], -slopes[:, NY:]
    bend = along(vort, rc, rc_low) + across(cc, cc_low, smoothed)
    residual = (
        rate
        + flow_down * slope_down
        + flow_right * slope_right
        - bend
    )
    weighted = jnp.where(inside, LOSS_WEIGHT * residual, 0.0)
    first = weighted * slope_down
    second = weighted * slope_right
    slopes = along(jnp.concatenate([first, flow_right * weighted], axis=0), rs, rs_low)
    first_along, flow_along = slopes[:NX], slopes[NX:]
    slopes = across(
        cs, cs_low, jnp.concatenate([second, smooth(flow_down * weighted)], axis=1)
    )
    second_across, flow_across = slopes[:, :NY], slopes[:, NY:]
    solved = solve(second_across - first_along)
    bend = along(weighted, rc, rc_low) + across(cc, cc_low, smooth(weighted))
    grad = solved - bend - flow_across - flow_along
    out_ref[:, 0] = grad.reshape(ROWS, CELLS, NY)
    out_ref[:, 1] = weighted.reshape(ROWS, CELLS, NY)


def output_kernel(
    hidden_ref, modes_ref, matrix_ref, back_ref, coef_ref, grad_ref, phase_ref, out_ref, mode_ref,
    block, spread,
):
    t = pl.program_id(0)
    inner = t % GROUP

    @pl.when(t == 0)
    def _():
        fill_block(block, matrix_ref[...])

    @pl.when(inner == 0)
    def _():
        spread_rows(lambda b, rows: modes_ref[0, b, rows, :], phase_ref, spread)

    for chunk in range(GROUP):
        rows = slice(GROUP * chunk, GROUP * (chunk + 1))
        found = combine(block[...], hidden_ref[0, rows], spread[rows], back_ref[inner], inner)
        out_ref[0, rows] = found.astype(BF16).reshape(GROUP, C, NY)
    first = lax.broadcasted_iota(jnp.int32, (C, 2 * C), 0)
    lane = lax.broadcasted_iota(jnp.int32, (C, 2 * C), 1)
    for i in range(GROUP):
        own = coef_ref[pl.ds(GROUP * t + i, 1), :]
        grad = grad_ref[pl.ds(GROUP * t + i, 1), :]
        real = jnp.sum(jnp.where(lane == first, own, 0.0), axis=1, keepdims=True)
        imag = jnp.sum(jnp.where(lane == first + C, own, 0.0), axis=1, keepdims=True)
        mode_ref[0, i] = real * grad + imag * turned_halves(grad)


def remote(src, dst, send, recv, device):
    return pltpu.make_async_remote_copy(
        src_ref=src, dst_ref=dst, send_sem=send, recv_sem=recv, device_id=device,
        device_id_type=MESH,
    )


def place():
    row, slab = lax.axis_index("rows"), lax.axis_index("tm")
    return row, slab, row // 2, row % 2


def greet_all():
    row, slab, chip, core = place()
    barrier = pltpu.get_barrier_semaphore()
    pl.semaphore_signal(
        barrier, inc=1, device_id=(row + 1 - 2 * core, slab), device_id_type=MESH
    )

    def greet(j):
        peer = 2 * ((chip + j) % CHIPS) + core
        pl.semaphore_signal(barrier, inc=1, device_id=(peer, slab), device_id_type=MESH)
        pl.semaphore_signal(
            barrier, inc=1, device_id=(row, (slab + j) % TM), device_id_type=MESH
        )

    loop(1, CHIPS, greet)
    pl.semaphore_wait(barrier, 1 + (CHIPS - 1) + (TM - 1))


class Modes:
    def __init__(self, gradient, w_hbm, sum_hbm, back_hbm, coef_ref, scratch):
        (
            self.weight, self.sum_table, self.back_table, self.terms, self.from_core,
            self.from_rows, self.parts, self.from_slabs, self.mixed, self.slabs, self.gathered,
            self.load, self.core_send, self.core_recv, self.row_send, self.row_recv,
            self.slab_send, self.slab_recv, self.mix_send, self.mix_recv, self.out_send,
            self.out_recv, self.pass_send, self.pass_recv,
        ) = scratch
        self.gradient, self.coef_ref = gradient, coef_ref
        self.row, self.slab, self.chip, self.core = place()
        self.other = (self.row + 1 - 2 * self.core, self.slab)
        self.loads = [
            pltpu.make_async_copy(src, dst, self.load.at[i])
            for i, (src, dst) in enumerate(
                (
                    (sum_hbm.at[self.slab], self.sum_table),
                    (w_hbm, self.weight),
                    (back_hbm.at[self.slab], self.back_table),
                )
            )
        ]

    def start_loads(self):
        for load in self.loads:
            load.start()

    def store(self, group):
        def put(b, rows, value):
            self.terms[b % 2, b // 2, group, rows, :] = value

        return put

    def core_copy(self, group, j):
        to = (self.chip + j) % CHIPS
        return remote(
            self.terms.at[1 - self.core, to, group], self.from_core.at[to, group],
            self.core_send.at[to, group], self.core_recv.at[to, group], self.other,
        )

    def row_copy(self, group, j):
        to = (self.chip + j) % CHIPS
        return remote(
            self.from_core.at[to, group], self.from_rows.at[self.chip, group],
            self.row_send.at[to, group], self.row_recv.at[self.chip, group],
            (2 * to + self.core, self.slab),
        )

    def start_core(self, group):
        loop(1, CHIPS + 1, lambda j: self.core_copy(group, j).start())

    def forward(self, group):
        def step(j):
            to = (self.chip + j) % CHIPS
            self.core_copy(group, j).wait_recv()
            self.from_core[to, group] = (
                self.from_core[to, group] + self.terms[self.core, to, group]
            )
            self.row_copy(group, j).start()

        loop(1, CHIPS, step)
        self.core_copy(group, CHIPS).wait_recv()
        self.from_rows[self.chip, group] = (
            self.from_core[self.chip, group] + self.terms[self.core, self.chip, group]
        )

    def arrivals(self, group):
        def step(j):
            source = (self.chip + CHIPS - j) % CHIPS
            remote(
                self.from_core.at[source, group], self.from_rows.at[source, group],
                self.row_send.at[source, group], self.row_recv.at[source, group],
                (2 * source + self.core, self.slab),
            ).wait_recv()

        loop(1, CHIPS, step)
        total = self.from_rows[0, group]
        for source in range(1, CHIPS):
            total = total + self.from_rows[source, group]
        return total

    def slab_copy(self, j):
        to = (self.slab + j) % TM
        return remote(
            self.parts.at[to], self.from_slabs.at[self.slab], self.slab_send.at[to],
            self.slab_recv.at[self.slab], (self.row, to),
        )

    def mix_copy(self, j):
        to = (self.slab + j) % TM
        return remote(
            self.mixed, self.slabs.at[self.slab], self.mix_send.at[to],
            self.mix_recv.at[self.slab], (self.row, to),
        )

    def exchange_slabs(self):
        totals = [self.arrivals(group) for group in range(2)]
        both = jnp.concatenate(
            [
                jnp.concatenate(totals, axis=1),
                jnp.concatenate([turned(total) for total in totals], axis=1),
            ],
            axis=0,
        )
        self.loads[0].wait()
        found = lax.dot_general(
            self.sum_table[...], both, (((1,), (1,)), ((), ())),
            precision=lax.Precision.HIGHEST, preferred_element_type=F32,
        )
        self.parts[...] = (found * (S_MODE if self.gradient else S_GRID)).reshape(
            TM, 2 * K, 2 * C
        )
        loop(1, TM, lambda j: self.slab_copy(j).start())
        self.from_slabs[self.slab] = self.parts[self.slab]
        self.loads[1].wait()

        def slab_arrival(j):
            source = (self.slab + TM - j) % TM
            remote(
                self.parts.at[source], self.from_slabs.at[source], self.slab_send.at[source],
                self.slab_recv.at[source], (self.row, source),
            ).wait_recv()

        loop(1, TM, slab_arrival)
        coef = self.from_slabs[0]
        for source in range(1, TM):
            coef = coef + self.from_slabs[source]
        self.coef_ref[...] = coef
        if self.gradient:
            self.mix_back(coef)
        else:
            self.mix(coef)
        loop(1, TM, lambda j: self.mix_copy(j).start())
        self.slabs[self.slab] = self.mixed[...]

        def mix_arrival(j):
            source = (self.slab + TM - j) % TM
            remote(
                self.mixed, self.slabs.at[source], self.mix_send.at[source],
                self.mix_recv.at[source], (self.row, source),
            ).wait_recv()

        loop(1, TM, mix_arrival)
        self.loads[2].wait()
        whole = jnp.transpose(self.slabs[...].reshape(K * K, 2 * C))
        spread = (S_GRID if self.gradient else S_MODE) * jnp.dot(
            jnp.concatenate([whole[:C], whole[C:]], axis=1), self.back_table[...],
            precision=lax.Precision.HIGHEST, preferred_element_type=F32,
        )
        self.gathered[0, self.row] = spread[:, :LANES]
        self.gathered[1, self.row] = spread[:, LANES:]
        for group in range(2):
            loop(1, CHIPS, lambda j: self.out_copy(group, j).start())
            self.pass_copy(group, self.chip).start()

    def mix(self, coef):
        columns = jnp.transpose(
            jnp.concatenate([coef, jnp.zeros((2 * C - 2 * K, 2 * C), F32)], axis=0)
        )
        for j in range(2 * K):
            weight = self.weight[j // K, j % K]
            re = jnp.sum(weight * columns[:C, j : j + 1], axis=0, keepdims=True)
            im = jnp.sum(weight * columns[C:, j : j + 1], axis=0, keepdims=True)
            self.mixed[j : j + 1, :] = re - turned_halves(im)

    def mix_back(self, coef):
        turned_coef = turned_halves(coef)
        lane = lax.broadcasted_iota(jnp.int32, (C, 2 * C), 1)
        real = jnp.zeros((C, 2 * C), F32)
        imag = jnp.zeros((C, 2 * C), F32)
        for j in range(2 * K):
            weight = self.weight[j // K, j % K]
            re = jnp.sum(weight * coef[j : j + 1, :], axis=1, keepdims=True)
            im = jnp.sum(weight * turned_coef[j : j + 1, :], axis=1, keepdims=True)
            real = jnp.where(lane == j, re, real)
            imag = jnp.where(lane == j, im, imag)
        self.mixed[...] = jnp.transpose(jnp.concatenate([real, imag], axis=0))[: 2 * K]

    def out_copy(self, group, j):
        to = (self.chip + j) % CHIPS
        block = self.gathered.at[group, self.row]
        return remote(
            block, block, self.out_send.at[to, group], self.out_recv.at[self.chip, group],
            (2 * to + self.core, self.slab),
        )

    def pass_copy(self, group, source):
        block = self.gathered.at[group, 2 * source + self.core]
        return remote(
            block, block, self.pass_send.at[source, group], self.pass_recv.at[source, group],
            self.other,
        )

    def pass_on(self, group):
        def step(j):
            source = (self.chip + CHIPS - j) % CHIPS
            block = self.gathered.at[group, 2 * source + self.core]
            remote(
                block, block, self.out_send.at[source, group], self.out_recv.at[source, group],
                (2 * source + self.core, self.slab),
            ).wait_recv()
            self.pass_copy(group, source).start()

        loop(1, CHIPS, step)

    def gather_done(self, group):
        def step(source):
            block = self.gathered.at[group, 2 * source + 1 - self.core]
            remote(
                block, block, self.pass_send.at[source, group], self.pass_recv.at[source, group],
                self.other,
            ).wait_recv()

        loop(0, CHIPS, step)

    def wait_sends(self):
        loop(1, TM, lambda j: self.slab_copy(j).wait_send())
        loop(1, TM, lambda j: self.mix_copy(j).wait_send())
        for group in range(2):
            loop(1, CHIPS + 1, lambda j: self.core_copy(group, j).wait_send())
            loop(1, CHIPS, lambda j: self.row_copy(group, j).wait_send())
            loop(1, CHIPS, lambda j: self.out_copy(group, j).wait_send())
            loop(0, CHIPS, lambda j: self.pass_copy(group, j).wait_send())


class Planes:
    def __init__(self, forcing_ref, scratch):
        (
            self.vort, self.rates, self.halo, self.planes, self.halo_send, self.halo_recv,
            self.send, self.recv, self.pass_send, self.pass_recv,
        ) = scratch
        self.forcing = forcing_ref
        self.row, self.slab, self.chip, self.core = place()
        self.other = (self.row + 1 - 2 * self.core, self.slab)
        after, before = (self.slab + 1) % TM, (self.slab + TM - 1) % TM
        self.to_after = remote(
            self.vort.at[STEPS - 1], self.halo.at[0], self.halo_send.at[0], self.halo_recv.at[0],
            (self.row, after),
        )
        self.to_before = remote(
            self.vort.at[0], self.halo.at[1], self.halo_send.at[1], self.halo_recv.at[1],
            (self.row, before),
        )

    def copy(self, field, to):
        source = (self.vort, self.rates)[field].at[to]
        return remote(
            source, self.planes.at[field, self.row], self.send.at[field, to],
            self.recv.at[field, self.chip], (2 * to + self.core, self.slab),
        )

    def pass_copy(self, field, source):
        block = self.planes.at[field, 2 * source + self.core]
        return remote(
            block, block, self.pass_send.at[field, source], self.pass_recv.at[field, source],
            self.other,
        )

    def send_step(self, field, to):
        @pl.when(to != self.chip)
        def _():
            self.copy(field, to).start()

        @pl.when(to == self.chip)
        def _():
            self.planes[field, self.row] = (self.vort, self.rates)[field][to]
            self.pass_copy(field, self.chip).start()

    def rate(self, step, low, high):
        self.rates[step] = (0.5 * NT) * (high - low) - self.forcing[...]

    def inner_rates(self, first, last):
        for step in range(first, last):
            self.rate(step, self.vort[step - 1], self.vort[step + 1])
            self.send_step(1, step)

    def arrivals(self, field):
        def step(j):
            source = (self.chip + CHIPS - j) % CHIPS
            block = 2 * source + self.core
            remote(
                self.vort.at[source], self.planes.at[field, block], self.send.at[field, source],
                self.recv.at[field, source], (block, self.slab),
            ).wait_recv()
            self.pass_copy(field, source).start()

        loop(1, CHIPS, step)

    def pass_arrivals(self, field):
        def step(source):
            block = self.planes.at[field, 2 * source + 1 - self.core]
            remote(
                block, block, self.pass_send.at[field, source], self.pass_recv.at[field, source],
                self.other,
            ).wait_recv()

        loop(0, CHIPS, step)

    def wait_sends(self):
        self.to_after.wait_send()
        self.to_before.wait_send()
        for field in range(2):
            loop(1, CHIPS, lambda j: self.copy(field, (self.chip + j) % CHIPS).wait_send())
            loop(0, CHIPS, lambda j: self.pass_copy(field, j).wait_send())


def front_kernel(
    act_hbm, w_hbm, matrix_ref, readout_ref, forcing_ref, forward_ref, back_ref, phase_ref,
    sum_hbm, back_hbm, slope_hbm, coef_ref, planes_ref,
    act, lines, block, wide, slopes, act_load, slope_store, *scratch,
):
    modes = Modes(False, w_hbm, sum_hbm, back_hbm, coef_ref, scratch[:MODE_SCRATCH])
    planes = Planes(forcing_ref, scratch[MODE_SCRATCH:])

    def load(t):
        return pltpu.make_async_copy(act_hbm.at[t], act.at[t], act_load.at[t])

    for t in range(STEPS):
        load(t).start()
    modes.start_loads()
    greet_all()
    same = lax.broadcasted_iota(jnp.int32, (C, C), 0) == lax.broadcasted_iota(
        jnp.int32, (C, C), 1
    )
    unit = jnp.where(same, 1.0, 0.0).astype(BF16)
    fill_block(
        block,
        lax.dot_general(
            matrix_ref[...], unit, (((0,), (0,)), ((), ())), preferred_element_type=F32
        ).astype(BF16),
    )
    wide[...] = jnp.broadcast_to(
        jnp.sum(jnp.where(same, readout_ref[...], 0.0), axis=1, keepdims=True), (C, LANES)
    )

    def make_lines(group):
        for t in range(GROUP):
            load(GROUP * group + t).wait()

        def part(chunk):
            rows = pl.ds(GROUP * chunk, GROUP)
            total = None
            for t in range(GROUP):
                term = jnp.dot(
                    act[GROUP * group + t, rows].reshape(GROUP * C, NY), forward_ref[t],
                    preferred_element_type=F32,
                )
                total = term if total is None else total + term
            lines[rows] = total.reshape(GROUP, C, LANES)

        loop(0, GROUP, part)

    make_lines(0)
    project_rows(lines, phase_ref, modes.store(0))
    modes.start_core(0)
    make_lines(1)
    modes.forward(0)
    project_rows(lines, phase_ref, modes.store(1))
    modes.start_core(1)
    modes.forward(1)
    modes.exchange_slabs()

    c0 = math.sqrt(2.0 / math.pi)
    c1 = c0 * 0.044715

    def slope_copy(group, i):
        t = GROUP * group + i % GROUP
        return pltpu.make_async_copy(
            slopes.at[i % 2], slope_hbm.at[t, pl.ds(GROUP * (i // GROUP), GROUP)],
            slope_store.at[i % 2],
        )

    def hide(group):
        def part(i):
            inner, chunk = i % GROUP, i // GROUP
            t = GROUP * group + inner
            rows = pl.ds(GROUP * chunk, GROUP)
            hidden = combine(block[...], act[t, rows], lines[rows], back_ref[inner], inner)
            if group == 0:
                @pl.when(i >= 2)
                def _():
                    slope_copy(group, i).wait()
            else:
                slope_copy(group, i).wait()
            for x in range(GROUP):
                total = None
                for part_of in range(C // 16):
                    own = slice(16 * part_of, 16 * part_of + 16)
                    readout = jnp.concatenate([wide[own]] * (NY // LANES), axis=1)
                    value = hidden[C * x + 16 * part_of : C * x + 16 * part_of + 16]
                    square = value * value
                    level = 0.5 + 0.5 * jnp.tanh(value * (c0 + c1 * square))
                    active = value * level
                    slope = level + active * (1.0 - level) * (2.0 * c0 + 6.0 * c1 * square)
                    slopes[i % 2, x, own, :] = readout * slope
                    term = readout * active
                    term = term[:8] + term[8:]
                    total = term if total is None else total + term
                planes.vort[t, pl.ds(GROUP * chunk + x, 1), :] = jnp.sum(
                    total, axis=0, keepdims=True
                )
            slope_copy(group, i).start()

        loop(0, GROUP * GROUP, part, unroll=UNROLL)

    modes.pass_on(0)
    modes.gather_done(0)
    spread_rows(lambda b, rows: modes.gathered[0, b, rows, :], phase_ref, lines)
    modes.pass_on(1)
    hide(0)
    planes.to_before.start()
    for t in range(GROUP):
        planes.send_step(0, t)
    planes.inner_rates(1, GROUP - 1)
    modes.gather_done(1)
    spread_rows(lambda b, rows: modes.gathered[1, b, rows, :], phase_ref, lines)
    hide(1)
    planes.to_after.start()
    for t in range(GROUP, STEPS):
        planes.send_step(0, t)
    planes.inner_rates(GROUP - 1, STEPS - 1)
    planes.to_after.wait_recv()
    planes.rate(0, planes.halo[0], planes.vort[1])
    planes.send_step(1, 0)
    planes.to_before.wait_recv()
    planes.rate(STEPS - 1, planes.vort[STEPS - 2], planes.halo[1])
    planes.send_step(1, STEPS - 1)
    for field in range(2):
        planes.arrivals(field)
    for field in range(2):
        planes.pass_arrivals(field)
    planes_ref[...] = planes.planes[...]
    slope_copy(1, GROUP * GROUP - 2).wait()
    slope_copy(1, GROUP * GROUP - 1).wait()
    modes.wait_sends()
    planes.wait_sends()


def back_kernel(
    in_ref, slope_hbm, w_hbm, forward_ref, phase_ref, sum_hbm, back_hbm,
    hidden_hbm, modes_ref, coef_ref,
    steps, halo, grads, lines, slopes, hidden, send, recv, halo_send, halo_recv,
    slope_load, hidden_store, *scratch,
):
    modes = Modes(True, w_hbm, sum_hbm, back_hbm, coef_ref, scratch)
    row, slab, chip, core = place()
    after, before = (slab + 1) % TM, (slab + TM - 1) % TM

    def slope_copy(group, chunk, t):
        return pltpu.make_async_copy(
            slope_hbm.at[GROUP * group + t, pl.ds(GROUP * chunk, GROUP)], slopes.at[t],
            slope_load.at[t],
        )

    def hidden_copy(group, chunk, t):
        return pltpu.make_async_copy(
            hidden.at[t], hidden_hbm.at[GROUP * group + t, pl.ds(GROUP * chunk, GROUP)],
            hidden_store.at[t],
        )

    for t in range(GROUP):
        slope_copy(0, 0, t).start()
    modes.start_loads()
    greet_all()

    def copy(j):
        to = (chip + j) % CHIPS
        block = 2 * to + core
        return remote(
            in_ref.at[block], steps.at[chip], send.at[to], recv.at[chip], (block, slab)
        )

    loop(1, CHIPS, lambda j: copy(j).start())
    steps[chip] = in_ref[row]

    def arrival(source):
        @pl.when(source != chip)
        def _():
            remote(
                in_ref.at[2 * source + core], steps.at[source], send.at[source],
                recv.at[source], (2 * source + core, slab),
            ).wait_recv()

    arrival(STEPS - 1)
    to_after = remote(
        steps.at[STEPS - 1, 1], halo.at[0], halo_send.at[0], halo_recv.at[0], (row, after)
    )
    to_after.start()
    arrival(0)
    to_before = remote(steps.at[0, 1], halo.at[1], halo_send.at[1], halo_recv.at[1], (row, before))
    to_before.start()
    loop(1, STEPS - 1, arrival)

    def grad(step, low, high):
        grads[step] = steps[step, 0] + (0.5 * NT) * (low - high)

    for step in range(1, STEPS - 1):
        grad(step, steps[step - 1, 1], steps[step + 1, 1])
    to_after.wait_recv()
    grad(0, halo[0], steps[1, 1])
    to_before.wait_recv()
    grad(STEPS - 1, steps[STEPS - 2, 1], halo[1])

    def make_lines(group):
        def part(chunk):
            total = None
            for t in range(GROUP):
                slope_copy(group, chunk, t).wait()
                if group == 0:
                    @pl.when(chunk > 0)
                    def _():
                        hidden_copy(group, chunk, t).wait()
                else:
                    hidden_copy(group, chunk, t).wait()
                for x in range(GROUP):
                    weight = grads[GROUP * group + t, pl.ds(GROUP * chunk + x, 1), :]
                    hidden[t, x] = (slopes[t, x] * weight).astype(BF16)
                hidden_copy(group, chunk, t).start()
                if group == 0:
                    last = chunk == GROUP - 1
                    following = pltpu.make_async_copy(
                        slope_hbm.at[
                            jnp.where(last, GROUP + t, t),
                            pl.ds(jnp.where(last, 0, GROUP * (chunk + 1)), GROUP),
                        ],
                        slopes.at[t],
                        slope_load.at[t],
                    )
                    following.start()
                else:
                    @pl.when(chunk < GROUP - 1)
                    def _():
                        slope_copy(group, chunk + 1, t).start()
                term = jnp.dot(
                    hidden[t].reshape(GROUP * C, NY), forward_ref[t], preferred_element_type=F32
                )
                total = term if total is None else total + term
            lines[pl.ds(GROUP * chunk, GROUP)] = total.reshape(GROUP, C, LANES)

        loop(0, GROUP, part)

    make_lines(0)
    project_rows(lines, phase_ref, modes.store(0))
    modes.start_core(0)
    make_lines(1)
    modes.forward(0)
    project_rows(lines, phase_ref, modes.store(1))
    modes.start_core(1)
    modes.forward(1)
    modes.exchange_slabs()
    for group in range(2):
        modes.pass_on(group)
    for group in range(2):
        modes.gather_done(group)
        modes_ref[group] = modes.gathered[group]
    for t in range(GROUP):
        hidden_copy(1, GROUP - 1, t).wait()
    to_after.wait_send()
    to_before.wait_send()
    loop(1, CHIPS, lambda j: copy(j).wait_send())
    modes.wait_sends()


VMEM = pl.BlockSpec(memory_space=pltpu.VMEM)
SMEM = pl.BlockSpec(memory_space=pltpu.SMEM)
ANY = pl.BlockSpec(memory_space=pl.ANY)
DMA = pltpu.SemaphoreType.DMA
LIMIT = 56 * 1024 * 1024
UNROLL = 2


def params(collective_id=None):
    if collective_id is None:
        return pltpu.CompilerParams(vmem_limit_bytes=LIMIT)
    return pltpu.CompilerParams(
        collective_id=collective_id, has_side_effects=True, vmem_limit_bytes=LIMIT
    )


def whole_spec(shape):
    return pl.BlockSpec(shape, lambda t: (0,) * len(shape))


def step_spec(shape):
    return pl.BlockSpec((1,) + shape, lambda t: (t,) + (0,) * len(shape))


FIELD = (CELLS, C, NY)
PLANE = (CELLS, NY)
PART = (C, LANES)
PAIR = (2 * K, 2 * C)


def vmem(*shape, dtype=F32):
    return pltpu.VMEM(shape, dtype)


def mode_scratch():
    return [
        vmem(2, K, C, 2 * C),
        vmem(K * K, 2 * LANES),
        vmem(2 * K * K, 2 * LANES),
        vmem(2, CHIPS, 2, *PART),
        vmem(CHIPS, 2, *PART),
        vmem(CHIPS, 2, *PART),
        vmem(TM, *PAIR),
        vmem(TM, *PAIR),
        vmem(*PAIR),
        vmem(TM, *PAIR),
        vmem(2, K, *PART),
        DMA((3,)),
        *[DMA((CHIPS, 2))] * 4,
        *[DMA((TM,))] * 4,
        *[DMA((CHIPS, 2))] * 4,
    ]


MODE_SCRATCH = 24


def shards(activations, spectral_weight, pointwise, readout, forcing):
    line_forward, line_back = (jnp.asarray(t) for t in line_tables())
    phases = jnp.asarray(row_phases())
    sum_table, back_table = (jnp.asarray(t) for t in time_tables())
    physics = [jnp.asarray(t) for t in physics_tables()]
    plane = (2, ROWS) + PLANE

    slopes, coef, planes = pl.pallas_call(
        front_kernel,
        out_shape=(
            jax.ShapeDtypeStruct((STEPS,) + FIELD, F32),
            jax.ShapeDtypeStruct(PAIR, F32),
            jax.ShapeDtypeStruct(plane, F32),
        ),
        in_specs=[ANY, ANY, VMEM, VMEM, VMEM, VMEM, VMEM, SMEM, ANY, ANY],
        out_specs=(ANY, VMEM, VMEM),
        scratch_shapes=[
            vmem(STEPS, *FIELD, dtype=BF16),
            vmem(CELLS, *PART),
            vmem(GROUP * C, GROUP * C, dtype=BF16),
            vmem(C, LANES),
            vmem(2, GROUP, C, NY),
            DMA((STEPS,)),
            DMA((2,)),
            *mode_scratch(),
            vmem(STEPS, *PLANE),
            vmem(STEPS, *PLANE),
            vmem(2, *PLANE),
            vmem(*plane),
            DMA((2,)),
            DMA((2,)),
            *[DMA((2, CHIPS))] * 4,
        ],
        compiler_params=params(0),
        name="front",
    )(
        activations, spectral_weight, pointwise, readout.reshape(1, C), forcing, line_forward,
        line_back, phases, sum_table, back_table,
    )

    returned = pl.pallas_call(
        physics_kernel,
        out_shape=jax.ShapeDtypeStruct((ROWS, 2) + PLANE, F32),
        in_specs=[VMEM] * (1 + len(physics)),
        out_specs=VMEM,
        compiler_params=params(),
        name="physics",
    )(planes, *physics)

    grad_hidden, grad_modes, grad_mixed = pl.pallas_call(
        back_kernel,
        out_shape=(
            jax.ShapeDtypeStruct((STEPS,) + FIELD, BF16),
            jax.ShapeDtypeStruct((2, K) + PART, F32),
            jax.ShapeDtypeStruct(PAIR, F32),
        ),
        in_specs=[VMEM, ANY, ANY, VMEM, SMEM, ANY, ANY],
        out_specs=(ANY, VMEM, VMEM),
        scratch_shapes=[
            vmem(CHIPS, 2, *PLANE),
            vmem(2, *PLANE),
            vmem(STEPS, *PLANE),
            vmem(CELLS, *PART),
            vmem(GROUP, GROUP, C, NY),
            vmem(GROUP, GROUP, C, NY, dtype=BF16),
            DMA((CHIPS,)),
            DMA((CHIPS,)),
            DMA((2,)),
            DMA((2,)),
            DMA((GROUP,)),
            DMA((GROUP,)),
            *mode_scratch(),
        ],
        compiler_params=params(1),
        name="back",
    )(returned, slopes, spectral_weight, line_forward, phases, sum_table, back_table)

    return pl.pallas_call(
        output_kernel,
        grid=(STEPS,),
        out_shape=(
            jax.ShapeDtypeStruct((STEPS,) + FIELD, BF16),
            jax.ShapeDtypeStruct((2, K, C, 2 * C), F32),
        ),
        in_specs=[
            step_spec(FIELD),
            pl.BlockSpec((1, K) + PART, lambda t: (t // GROUP, 0, 0, 0)),
            whole_spec((C, C)),
            whole_spec((GROUP, LANES, NY)),
            whole_spec(PAIR),
            whole_spec(PAIR),
            SMEM,
        ],
        out_specs=(
            step_spec(FIELD),
            pl.BlockSpec((1, GROUP, C, 2 * C), lambda t: (t // GROUP, t % GROUP, 0, 0)),
        ),
        scratch_shapes=[vmem(GROUP * C, GROUP * C, dtype=BF16), vmem(CELLS, *PART)],
        compiler_params=params(),
        name="output",
    )(grad_hidden, grad_modes, pointwise, line_back, coef, grad_mixed, phases)


def solution(mesh):
    return jax.shard_map(
        shards,
        mesh=mesh,
        in_specs=(
            P("tm", "rows", None, None),
            P(("rows", "tm"), None, None, None),
            P(),
            P(),
            P("rows", None),
        ),
        out_specs=(P("tm", "rows", None, None), P(("rows", "tm"), None, None, None)),
        check_vma=False,
    )
```

```python
import math

import jax
import jax.numpy as jnp
import ml_dtypes
import numpy as np
from jax import lax
from jax.experimental import pallas as pl
from jax.experimental.pallas import tpu as pltpu
from jax.sharding import PartitionSpec as P

MESH = pl.DeviceIdType.MESH
VISCOSITY = 0.002
LOSS_WEIGHT = 0.005
C, K, NY, NX, NT = 64, 16, 512, 256, 64
ROWS, TM = 16, 8
CHIPS = ROWS // 2
STEPS, CELLS = NT // TM, NX // ROWS
HALF = NY // 2
GROUP, LANES = 4, 128
S_GRID = 1.0 / math.sqrt(NT * NX * NY)
S_MODE = 1.0 / math.sqrt(K * K * K)
TWO_PI = 2.0 * math.pi
BF16 = jnp.bfloat16
F32 = jnp.float32


def halves(table):
    table = table.astype(np.float32)
    high = table.astype(ml_dtypes.bfloat16)
    low = (table - high.astype(np.float32)).astype(ml_dtypes.bfloat16)
    return high, low


def line_tables():
    numbers = np.arange(K) - K // 2
    angles = (TWO_PI / NY) * (np.outer(numbers, np.arange(NY)) % NY)
    table = np.concatenate([np.cos(angles), -np.sin(angles)], axis=0).astype(np.float32)
    forward = np.zeros((GROUP, NY, LANES), ml_dtypes.bfloat16)
    back = np.zeros((GROUP, LANES, NY), ml_dtypes.bfloat16)
    high, low = halves(table)
    for t in range(GROUP):
        forward[t, :, 2 * K * t : 2 * K * (t + 1)] = table.astype(ml_dtypes.bfloat16).T
        for place, part in enumerate((high, high, low)):
            first = 2 * K * ((t + place) % GROUP)
            back[t, first : first + 2 * K] = part
    return forward, back


def time_tables():
    numbers = np.arange(K) - K // 2
    steps = np.arange(NT).reshape(TM, STEPS)
    angles = (TWO_PI / NT) * ((numbers[None, :, None] * steps[:, None, :]) % NT)
    unit = np.eye(K)

    def spread(real, imag):
        both = np.stack([real, imag], axis=3)
        return np.einsum("matr,ef->maetrf", both, unit).reshape(TM, K * K, STEPS * 2 * K)

    cos_part, sin_part = np.cos(angles), np.sin(angles)
    forward = spread(cos_part, sin_part)
    back = np.concatenate([spread(cos_part, sin_part), spread(-sin_part, cos_part)], axis=1)
    return forward.astype(np.float32), back.astype(np.float32)


def row_phases():
    numbers = np.arange(K) - K // 2
    angles = (TWO_PI / ROWS) * (np.outer(np.arange(ROWS), numbers) % ROWS)
    return np.stack([np.cos(angles), np.sin(angles)]).astype(np.float32)


def physics_tables():
    y = np.arange(NY)
    ky = np.arange(HALF)
    angles = (TWO_PI / NY) * (np.outer(y, ky) % NY)
    row_forward = np.concatenate([np.cos(angles), -np.sin(angles)], axis=1)
    scaling = np.where(ky == 0, 1.0, 2.0)[:, None] / NY
    row_back = np.concatenate([scaling * np.cos(angles).T, -scaling * np.sin(angles).T], axis=0)
    gap = np.arange(NY)
    gap_angles = (TWO_PI / NY) * (np.outer(gap, ky) % NY)
    slope = -(2.0 / NY) * (np.sin(gap_angles) * ky).sum(1)
    bend = -(2.0 / NY) * (np.cos(gap_angles) * ky * ky).sum(1)
    turn = (y[None, :] - y[:, None]) % NY
    row_slope, row_bend = slope[turn], bend[turn]
    x = np.arange(NX)
    kx = np.where(x < NX // 2, x, x - NX)
    dx = np.where(x == NX // 2, 0, kx)
    col_angles = (TWO_PI / NX) * (np.outer(x, x) % NX)
    col_slope = -(np.sin(col_angles) * dx).sum(1) / NX
    col_bend = -(np.cos(col_angles) * kx * kx).sum(1) / NX
    col_turn = (x[:, None] - x[None, :]) % NX
    col_slope, col_bend = col_slope[col_turn], col_bend[col_turn]
    col_wave = np.concatenate([np.cos(col_angles), np.sin(col_angles)], axis=0)
    squared = (kx[:, None] ** 2 + ky[None, :] ** 2).astype(np.float64)
    inverse = np.where(squared > 0, 1.0 / np.where(squared > 0, squared, 1.0), 0.0) / NX
    inverse = np.concatenate([inverse, inverse], axis=1).astype(np.float32)
    pairs = [
        halves(t)
        for t in (
            row_forward,
            row_back,
            row_slope,
            VISCOSITY * row_bend,
            col_wave,
            col_slope,
            VISCOSITY * col_bend,
        )
    ]
    return [t for pair in pairs for t in pair] + [inverse]


def turned_halves(z):
    moved = pltpu.roll(z, C, 1)
    low = lax.broadcasted_iota(jnp.int32, z.shape, 1) < C
    return jnp.where(low, moved, -moved)


def turned(z):
    real = lax.broadcasted_iota(jnp.int32, z.shape, 1) % (2 * K) < K
    return jnp.where(real, pltpu.roll(z, LANES - K, 1), -pltpu.roll(z, K, 1))


def loop(first, last, body, unroll=1):
    def step(j, carry):
        body(j)
        return carry

    lax.fori_loop(first, last, step, 0, unroll=unroll)


def project_rows(lines, phase_ref, store):
    row = lax.axis_index("rows")

    def part(chunk):
        rows = pl.ds(pl.multiple_of(8 * chunk, 8), 8)
        z = [lines[x, rows, :] for x in range(CELLS)]
        q = [turned(value) for value in z]
        for k in range(K // 2 + 1):
            even, odd = None, None
            for x in range(CELLS):
                angle = TWO_PI * (k * x % NX) / NX
                cos_term = z[x] if k * x == 0 else math.cos(angle) * z[x]
                even = cos_term if even is None else even + cos_term
                if k * x:
                    sin_term = math.sin(angle) * q[x]
                    odd = sin_term if odd is None else odd + sin_term
            found = []
            if k < K // 2:
                found.append((K // 2 + k, even if odd is None else even + odd))
            if k > 0:
                found.append((K // 2 - k, even - odd))
            for b, value in found:
                cos_b, sin_b = phase_ref[0, row, b], phase_ref[1, row, b]
                store(b, rows, cos_b * value + sin_b * turned(value))

    loop(0, C // 8, part)


def spread_rows(modes, phase_ref, spread):
    row = lax.axis_index("rows")

    def part(chunk):
        rows = pl.ds(pl.multiple_of(8 * chunk, 8), 8)
        z = []
        for b in range(K):
            cos_b, sin_b = phase_ref[0, row, b], phase_ref[1, row, b]
            value = modes(b, rows)
            z.append(cos_b * value - sin_b * turned(value))
        even, odd = [z[K // 2]], [None]
        for k in range(1, K // 2):
            even.append(z[K // 2 + k] + z[K // 2 - k])
            odd.append(turned(z[K // 2 - k] - z[K // 2 + k]))
        even.append(z[0])
        odd.append(turned(z[0]))
        for x in range(CELLS):
            total = even[0]
            for k in range(1, K // 2 + 1):
                angle = TWO_PI * (k * x % NX) / NX
                if x == 0:
                    total = total + even[k]
                else:
                    total = total + math.cos(angle) * even[k] + math.sin(angle) * odd[k]
            spread[x, rows, :] = total

    loop(0, C // 8, part)


def fill_block(block, matrix):
    block[...] = jnp.zeros_like(block)
    for x in range(GROUP):
        block[C * x : C * (x + 1), C * x : C * (x + 1)] = matrix


def spread_part(spread, back, t):
    total = spread.reshape(GROUP * C, LANES)
    high = total.astype(BF16).astype(F32)
    lane = lax.broadcasted_iota(jnp.int32, total.shape, 1) // (2 * K)
    left = jnp.where(
        lane == t,
        high,
        jnp.where(
            lane == (t + 1) % GROUP,
            pltpu.roll(total - high, 2 * K, 1),
            pltpu.roll(high, 4 * K, 1),
        ),
    ).astype(BF16)
    return jnp.dot(left, back, preferred_element_type=F32)


def physics(planes, step, tables, send_weighted, send_grad):
    (rf, rf_low, rb, rb_low, rs, rs_low, rc, rc_low, cw, cw_low, cs, cs_low, cc, cc_low, inverse) = (
        tables
    )

    def parts(value):
        high = value.astype(BF16)
        return high, (value - high.astype(F32)).astype(BF16)

    def dot(a, b):
        return jnp.dot(a, b, preferred_element_type=F32)

    def along(value, high, low):
        v_high, v_low = parts(value)
        return dot(v_high, high[...]) + (dot(v_low, high[...]) + dot(v_high, low[...]))

    def across(high, low, value):
        v_high, v_low = parts(value)
        return dot(high[...], v_high) + (dot(high[...], v_low) + dot(low[...], v_high))

    def minus_i(z):
        return jnp.concatenate([z[:, HALF:], -z[:, :HALF]], axis=1)

    def solve(value):
        spectrum = along(value, rf, rf_low)
        both = across(cw, cw_low, spectrum)
        spectrum = (both[:NX] + minus_i(both[NX:])) * inverse[...]
        both = across(cw, cw_low, spectrum)
        return along(both[:NX] - minus_i(both[NX:]), rb, rb_low)

    sign = jnp.where(lax.broadcasted_iota(jnp.int32, (NX, NY), 1) % 2 == 0, 1.0, -1.0).astype(F32)

    def smooth(value):
        return value - sign * (jnp.sum(value * sign, axis=1, keepdims=True) * (1.0 / NY))

    inside = (step > 0) & (step < NT - 1)
    vort = planes[0].reshape(NX, NY)
    rate = planes[1].reshape(NX, NY)
    stream = solve(vort)
    slopes = along(jnp.concatenate([vort, stream], axis=0), rs, rs_low)
    slope_right, flow_down = slopes[:NX], slopes[NX:]
    smoothed = smooth(vort)
    slopes = across(cs, cs_low, jnp.concatenate([smoothed, stream], axis=1))
    slope_down, flow_right = slopes[:, :NY], -slopes[:, NY:]
    bend = along(vort, rc, rc_low) + across(cc, cc_low, smoothed)
    residual = (
        rate
        + flow_down * slope_down
        + flow_right * slope_right
        - bend
    )
    weighted = jnp.where(inside, LOSS_WEIGHT * residual, 0.0)
    send_weighted(weighted)
    first = weighted * slope_down
    second = weighted * slope_right
    slopes = along(jnp.concatenate([first, flow_right * weighted], axis=0), rs, rs_low)
    first_along, flow_along = slopes[:NX], slopes[NX:]
    slopes = across(
        cs, cs_low, jnp.concatenate([second, smooth(flow_down * weighted)], axis=1)
    )
    second_across, flow_across = slopes[:, :NY], slopes[:, NY:]
    solved = solve(second_across - first_along)
    bend = along(weighted, rc, rc_low) + across(cc, cc_low, smooth(weighted))
    grad = solved - bend - flow_across - flow_along
    send_grad(grad)


def remote(src, dst, send, recv, device):
    return pltpu.make_async_remote_copy(
        src_ref=src, dst_ref=dst, send_sem=send, recv_sem=recv, device_id=device,
        device_id_type=MESH,
    )


def place():
    row, slab = lax.axis_index("rows"), lax.axis_index("tm")
    return row, slab, row // 2, row % 2


def greet_all():
    row, slab, chip, core = place()
    barrier = pltpu.get_barrier_semaphore()
    pl.semaphore_signal(
        barrier, inc=1, device_id=(row + 1 - 2 * core, slab), device_id_type=MESH
    )

    def greet(j):
        peer = 2 * ((chip + j) % CHIPS) + core
        pl.semaphore_signal(barrier, inc=1, device_id=(peer, slab), device_id_type=MESH)
        pl.semaphore_signal(
            barrier, inc=1, device_id=(row, (slab + j) % TM), device_id_type=MESH
        )

    loop(1, CHIPS, greet)
    pl.semaphore_wait(barrier, 1 + (CHIPS - 1) + (TM - 1))


class Modes:
    def __init__(self, w_hbm, sum_hbm, back_hbm, scratch):
        (
            self.weight, self.sum_table, self.back_table, self.terms, self.from_core,
            self.from_rows, self.parts, self.from_slabs, self.mixed, self.slabs, self.gathered,
            self.load, self.core_send, self.core_recv, self.row_send, self.row_recv,
            self.slab_send, self.slab_recv, self.mix_send, self.mix_recv, self.out_send,
            self.out_recv, self.pass_send, self.pass_recv,
        ) = scratch
        self.row, self.slab, self.chip, self.core = place()
        self.other = (self.row + 1 - 2 * self.core, self.slab)
        self.loads = [
            pltpu.make_async_copy(src, dst, self.load.at[i])
            for i, (src, dst) in enumerate(
                (
                    (sum_hbm.at[self.slab], self.sum_table),
                    (w_hbm, self.weight),
                    (back_hbm.at[self.slab], self.back_table),
                )
            )
        ]

    def start_loads(self):
        for load in self.loads:
            load.start()

    def store(self, group):
        def put(b, rows, value):
            self.terms[b % 2, b // 2, group, rows, :] = value

        return put

    def core_copy(self, group, j):
        to = (self.chip + j) % CHIPS
        return remote(
            self.terms.at[1 - self.core, to, group], self.from_core.at[to, group],
            self.core_send.at[to, group], self.core_recv.at[to, group], self.other,
        )

    def row_copy(self, group, j):
        to = (self.chip + j) % CHIPS
        return remote(
            self.from_core.at[to, group], self.from_rows.at[self.chip, group],
            self.row_send.at[to, group], self.row_recv.at[self.chip, group],
            (2 * to + self.core, self.slab),
        )

    def start_core(self, group):
        loop(1, CHIPS + 1, lambda j: self.core_copy(group, j).start())

    def forward(self, group):
        def step(j):
            to = (self.chip + j) % CHIPS
            self.core_copy(group, j).wait_recv()
            self.from_core[to, group] = (
                self.from_core[to, group] + self.terms[self.core, to, group]
            )
            self.row_copy(group, j).start()

        loop(1, CHIPS, step)
        self.core_copy(group, CHIPS).wait_recv()
        self.from_rows[self.chip, group] = (
            self.from_core[self.chip, group] + self.terms[self.core, self.chip, group]
        )

    def arrivals(self, group):
        def step(j):
            source = (self.chip + CHIPS - j) % CHIPS
            remote(
                self.from_core.at[source, group], self.from_rows.at[source, group],
                self.row_send.at[source, group], self.row_recv.at[source, group],
                (2 * source + self.core, self.slab),
            ).wait_recv()

        loop(1, CHIPS, step)
        total = self.from_rows[0, group]
        for source in range(1, CHIPS):
            total = total + self.from_rows[source, group]
        return total

    def slab_copy(self, j):
        to = (self.slab + j) % TM
        return remote(
            self.parts.at[to], self.from_slabs.at[self.slab], self.slab_send.at[to],
            self.slab_recv.at[self.slab], (self.row, to),
        )

    def mix_copy(self, j):
        to = (self.slab + j) % TM
        return remote(
            self.mixed, self.slabs.at[self.slab], self.mix_send.at[to],
            self.mix_recv.at[self.slab], (self.row, to),
        )

    def exchange_slabs(self, gradient, coef_ref, first, second):
        totals = [self.arrivals(group) for group in range(2)]
        both = jnp.concatenate(
            [
                jnp.concatenate(totals, axis=1),
                jnp.concatenate([turned(total) for total in totals], axis=1),
            ],
            axis=0,
        )
        if not gradient:
            self.loads[0].wait()
        found = lax.dot_general(
            self.sum_table[...], both, (((1,), (1,)), ((), ())),
            precision=lax.Precision.HIGHEST, preferred_element_type=F32,
        )
        self.parts[...] = (found * (S_MODE if gradient else S_GRID)).reshape(
            TM, 2 * K, 2 * C
        )
        loop(1, TM, lambda j: self.slab_copy(j).start())
        self.from_slabs[self.slab] = self.parts[self.slab]
        first()
        if not gradient:
            self.loads[1].wait()

        def slab_arrival(j):
            source = (self.slab + TM - j) % TM
            remote(
                self.parts.at[source], self.from_slabs.at[source], self.slab_send.at[source],
                self.slab_recv.at[source], (self.row, source),
            ).wait_recv()

        loop(1, TM, slab_arrival)
        coef = self.from_slabs[0]
        for source in range(1, TM):
            coef = coef + self.from_slabs[source]
        coef_ref[...] = coef
        if gradient:
            self.mix_back(coef)
        else:
            self.mix(coef)
        loop(1, TM, lambda j: self.mix_copy(j).start())
        self.slabs[self.slab] = self.mixed[...]
        second()

        def mix_arrival(j):
            source = (self.slab + TM - j) % TM
            remote(
                self.mixed, self.slabs.at[source], self.mix_send.at[source],
                self.mix_recv.at[source], (self.row, source),
            ).wait_recv()

        loop(1, TM, mix_arrival)
        if not gradient:
            self.loads[2].wait()
        whole = jnp.transpose(self.slabs[...].reshape(K * K, 2 * C))
        spread = (S_GRID if gradient else S_MODE) * jnp.dot(
            jnp.concatenate([whole[:C], whole[C:]], axis=1), self.back_table[...],
            precision=lax.Precision.HIGHEST, preferred_element_type=F32,
        )
        self.gathered[0, self.row] = spread[:, :LANES]
        self.gathered[1, self.row] = spread[:, LANES:]
        for group in range(2):
            loop(1, CHIPS, lambda j: self.out_copy(group, j).start())
            self.pass_copy(group, self.chip).start()

    def mix(self, coef):
        columns = jnp.transpose(
            jnp.concatenate([coef, jnp.zeros((2 * C - 2 * K, 2 * C), F32)], axis=0)
        )
        for j in range(2 * K):
            weight = self.weight[j // K, j % K]
            re = jnp.sum(weight * columns[:C, j : j + 1], axis=0, keepdims=True)
            im = jnp.sum(weight * columns[C:, j : j + 1], axis=0, keepdims=True)
            self.mixed[j : j + 1, :] = re - turned_halves(im)

    def mix_back(self, coef):
        turned_coef = turned_halves(coef)
        lane = lax.broadcasted_iota(jnp.int32, (C, 2 * C), 1)
        real = jnp.zeros((C, 2 * C), F32)
        imag = jnp.zeros((C, 2 * C), F32)
        for j in range(2 * K):
            weight = self.weight[j // K, j % K]
            re = jnp.sum(weight * coef[j : j + 1, :], axis=1, keepdims=True)
            im = jnp.sum(weight * turned_coef[j : j + 1, :], axis=1, keepdims=True)
            real = jnp.where(lane == j, re, real)
            imag = jnp.where(lane == j, im, imag)
        self.mixed[...] = jnp.transpose(jnp.concatenate([real, imag], axis=0))[: 2 * K]

    def out_copy(self, group, j):
        to = (self.chip + j) % CHIPS
        block = self.gathered.at[group, self.row]
        return remote(
            block, block, self.out_send.at[to, group], self.out_recv.at[self.chip, group],
            (2 * to + self.core, self.slab),
        )

    def pass_copy(self, group, source):
        block = self.gathered.at[group, 2 * source + self.core]
        return remote(
            block, block, self.pass_send.at[source, group], self.pass_recv.at[source, group],
            self.other,
        )

    def pass_on(self, group):
        def step(j):
            source = (self.chip + CHIPS - j) % CHIPS
            block = self.gathered.at[group, 2 * source + self.core]
            remote(
                block, block, self.out_send.at[source, group], self.out_recv.at[source, group],
                (2 * source + self.core, self.slab),
            ).wait_recv()
            self.pass_copy(group, source).start()

        loop(1, CHIPS, step)

    def gather_done(self, group):
        def step(source):
            block = self.gathered.at[group, 2 * source + 1 - self.core]
            remote(
                block, block, self.pass_send.at[source, group], self.pass_recv.at[source, group],
                self.other,
            ).wait_recv()

        loop(0, CHIPS, step)

    def wait_sends(self):
        loop(1, TM, lambda j: self.slab_copy(j).wait_send())
        loop(1, TM, lambda j: self.mix_copy(j).wait_send())
        for group in range(2):
            loop(1, CHIPS + 1, lambda j: self.core_copy(group, j).wait_send())
            loop(1, CHIPS, lambda j: self.row_copy(group, j).wait_send())
            loop(1, CHIPS, lambda j: self.out_copy(group, j).wait_send())
            loop(0, CHIPS, lambda j: self.pass_copy(group, j).wait_send())


class Planes:
    def __init__(self, forcing_ref, scratch):
        (
            self.vort, self.rates, self.halo, self.planes, self.halo_send, self.halo_recv,
            self.send, self.recv, self.pass_send, self.pass_recv,
        ) = scratch
        self.forcing = forcing_ref
        self.row, self.slab, self.chip, self.core = place()
        self.other = (self.row + 1 - 2 * self.core, self.slab)
        after, before = (self.slab + 1) % TM, (self.slab + TM - 1) % TM
        self.to_after = remote(
            self.vort.at[STEPS - 1], self.halo.at[0], self.halo_send.at[0], self.halo_recv.at[0],
            (self.row, after),
        )
        self.to_before = remote(
            self.vort.at[0], self.halo.at[1], self.halo_send.at[1], self.halo_recv.at[1],
            (self.row, before),
        )

    def copy(self, field, to):
        source = (self.vort, self.rates)[field].at[to]
        return remote(
            source, self.planes.at[field, self.row], self.send.at[field, to],
            self.recv.at[field, self.chip], (2 * to + self.core, self.slab),
        )

    def pass_copy(self, field, source):
        block = self.planes.at[field, 2 * source + self.core]
        return remote(
            block, block, self.pass_send.at[field, source], self.pass_recv.at[field, source],
            self.other,
        )

    def send_step(self, field, to):
        @pl.when(to != self.chip)
        def _():
            self.copy(field, to).start()

        @pl.when(to == self.chip)
        def _():
            self.planes[field, self.row] = (self.vort, self.rates)[field][to]
            self.pass_copy(field, self.chip).start()

    def rate(self, step, low, high):
        self.rates[step] = (0.5 * NT) * (high - low) - self.forcing[...]

    def inner_rates(self, first, last):
        for step in range(first, last):
            self.rate(step, self.vort[step - 1], self.vort[step + 1])
            self.send_step(1, step)

    def arrivals(self, field):
        def step(j):
            source = (self.chip + CHIPS - j) % CHIPS
            block = 2 * source + self.core
            remote(
                self.vort.at[source], self.planes.at[field, block], self.send.at[field, source],
                self.recv.at[field, source], (block, self.slab),
            ).wait_recv()
            self.pass_copy(field, source).start()

        loop(1, CHIPS, step)

    def pass_arrivals(self, field):
        def step(source):
            block = self.planes.at[field, 2 * source + 1 - self.core]
            remote(
                block, block, self.pass_send.at[field, source], self.pass_recv.at[field, source],
                self.other,
            ).wait_recv()

        loop(0, CHIPS, step)

    def wait_sends(self):
        self.to_after.wait_send()
        self.to_before.wait_send()
        for field in range(2):
            loop(1, CHIPS, lambda j: self.copy(field, (self.chip + j) % CHIPS).wait_send())
            loop(0, CHIPS, lambda j: self.pass_copy(field, j).wait_send())


class Returns:
    def __init__(self, scratch):
        (
            self.source, self.steps, self.halo, self.send, self.recv, self.halo_send,
            self.halo_recv,
        ) = scratch
        self.row, self.slab, self.chip, self.core = place()
        after, before = (self.slab + 1) % TM, (self.slab + TM - 1) % TM
        self.to_after = remote(
            self.steps.at[1, STEPS - 1], self.halo.at[0], self.halo_send.at[0],
            self.halo_recv.at[0], (self.row, after),
        )
        self.to_before = remote(
            self.steps.at[1, 0], self.halo.at[1], self.halo_send.at[1], self.halo_recv.at[1],
            (self.row, before),
        )

    def copy(self, field, j):
        to = (self.chip + j) % CHIPS
        block = 2 * to + self.core
        return remote(
            self.source.at[field, block], self.steps.at[field, self.chip],
            self.send.at[field, to], self.recv.at[field, self.chip], (block, self.slab),
        )

    def start(self, field, value):
        self.source[field] = value.reshape(ROWS, CELLS, NY)
        loop(1, CHIPS, lambda j: self.copy(field, j).start())
        self.steps[field, self.chip] = self.source[field, self.row]

    def arrivals(self, field):
        def step(j):
            source = (self.chip + CHIPS - j) % CHIPS
            block = 2 * source + self.core
            remote(
                self.source.at[field, block], self.steps.at[field, source],
                self.send.at[field, source], self.recv.at[field, source], (block, self.slab),
            ).wait_recv()

        loop(1, CHIPS, step)

    def finish(self, grads):
        self.arrivals(1)
        self.to_after.start()
        self.to_before.start()
        self.arrivals(0)

        def grad(step, low, high):
            grads[step] = self.steps[0, step] + (0.5 * NT) * (low - high)

        for step in range(1, STEPS - 1):
            grad(step, self.steps[1, step - 1], self.steps[1, step + 1])
        self.to_after.wait_recv()
        grad(0, self.halo[0], self.steps[1, 1])
        self.to_before.wait_recv()
        grad(STEPS - 1, self.steps[1, STEPS - 2], self.halo[1])

    def wait_sends(self):
        self.to_after.wait_send()
        self.to_before.wait_send()
        for field in range(2):
            loop(1, CHIPS, lambda j: self.copy(field, j).wait_send())


def whole_kernel(
    act_hbm, w_hbm, matrix_ref, readout_ref, forcing_ref, forward_ref, back_ref, phase_ref,
    sum_hbm, back_hbm, *rest,
):
    table_hbm, rest = rest[:PHYSICS], rest[PHYSICS:]
    out_hbm, mode_ref, act, lines, block, wide, fields, grads, coef, grad_mixed = rest[:10]
    act_load, out_store, table_load = rest[10:13]
    rest = rest[13:]
    tables, rest = rest[:PHYSICS], rest[PHYSICS:]
    modes = Modes(w_hbm, sum_hbm, back_hbm, rest[:MODE_SCRATCH])
    planes = Planes(forcing_ref, rest[MODE_SCRATCH : MODE_SCRATCH + PLANE_SCRATCH])
    returns = Returns(rest[MODE_SCRATCH + PLANE_SCRATCH :])

    def load(t):
        return pltpu.make_async_copy(act_hbm.at[t], act.at[t], act_load.at[t])

    table_loads = [
        pltpu.make_async_copy(src, dst, table_load.at[i])
        for i, (src, dst) in enumerate(zip(table_hbm, tables))
    ]
    for t in range(STEPS):
        load(t).start()
    modes.start_loads()
    for copy in table_loads:
        copy.start()
    greet_all()
    same = lax.broadcasted_iota(jnp.int32, (C, C), 0) == lax.broadcasted_iota(
        jnp.int32, (C, C), 1
    )
    unit = jnp.where(same, 1.0, 0.0).astype(BF16)
    fill_block(
        block,
        lax.dot_general(
            matrix_ref[...], unit, (((0,), (0,)), ((), ())), preferred_element_type=F32
        ).astype(BF16),
    )
    wide[...] = jnp.broadcast_to(
        jnp.sum(jnp.where(same, readout_ref[...], 0.0), axis=1, keepdims=True), (C, LANES)
    )

    def make_lines(group, prepare):
        def part(chunk):
            rows = pl.ds(GROUP * chunk, GROUP)
            total = None
            for inner in range(GROUP):
                t = GROUP * group + inner
                prepare(t, chunk, rows)
                term = jnp.dot(
                    act[t, rows].reshape(GROUP * C, NY), forward_ref[inner],
                    preferred_element_type=F32,
                )
                total = term if total is None else total + term
            lines[rows] = total.reshape(GROUP, C, LANES)

        loop(0, GROUP, part)

    def analyze(prepare, before):
        before(0)
        make_lines(0, prepare)
        project_rows(lines, phase_ref, modes.store(0))
        modes.start_core(0)
        before(1)
        make_lines(1, prepare)
        modes.forward(0)
        project_rows(lines, phase_ref, modes.store(1))
        modes.start_core(1)
        modes.forward(1)

    def local(group):
        def part(i):
            t, rows = GROUP * group + i % GROUP, pl.ds(GROUP * (i // GROUP), GROUP)
            fields[t, rows] = jnp.dot(
                block[...], act[t, rows].reshape(GROUP * C, NY), preferred_element_type=F32
            ).reshape(GROUP, C, NY)

        loop(0, GROUP * GROUP, part, unroll=UNROLL)

    def wait_load(group):
        for t in range(GROUP):
            load(GROUP * group + t).wait()

    analyze(lambda t, chunk, rows: None, wait_load)
    modes.exchange_slabs(False, coef, lambda: local(0), lambda: local(1))

    c0 = math.sqrt(2.0 / math.pi)
    c1 = c0 * 0.044715

    def hide(group):
        def part(i):
            inner, chunk = i % GROUP, i // GROUP
            t = GROUP * group + inner
            found = spread_part(lines[pl.ds(GROUP * chunk, GROUP)], back_ref[inner], inner)
            for x in range(GROUP):
                total = None
                for part_of in range(C // 16):
                    own = slice(16 * part_of, 16 * part_of + 16)
                    readout = jnp.concatenate([wide[own]] * (NY // LANES), axis=1)
                    place_of = C * x + 16 * part_of
                    value = found[place_of : place_of + 16] + fields[t, GROUP * chunk + x, own, :]
                    square = value * value
                    level = 0.5 + 0.5 * jnp.tanh(value * (c0 + c1 * square))
                    active = value * level
                    slope = level + active * (1.0 - level) * (2.0 * c0 + 6.0 * c1 * square)
                    fields[t, GROUP * chunk + x, own, :] = readout * slope
                    term = readout * active
                    term = term[:8] + term[8:]
                    total = term if total is None else total + term
                planes.vort[t, pl.ds(GROUP * chunk + x, 1), :] = jnp.sum(
                    total, axis=0, keepdims=True
                )

        loop(0, GROUP * GROUP, part, unroll=UNROLL)

    def spread(group):
        spread_rows(lambda b, rows: modes.gathered[group, b, rows, :], phase_ref, lines)

    modes.pass_on(0)
    modes.gather_done(0)
    spread(0)
    modes.pass_on(1)
    hide(0)
    planes.to_before.start()
    for t in range(GROUP):
        planes.send_step(0, t)
    planes.inner_rates(1, GROUP - 1)
    modes.gather_done(1)
    spread(1)
    hide(1)
    planes.to_after.start()
    for t in range(GROUP, STEPS):
        planes.send_step(0, t)
    planes.inner_rates(GROUP - 1, STEPS - 1)
    modes.wait_sends()
    planes.to_after.wait_recv()
    planes.rate(0, planes.halo[0], planes.vort[1])
    planes.send_step(1, 0)
    planes.to_before.wait_recv()
    planes.rate(STEPS - 1, planes.vort[STEPS - 2], planes.halo[1])
    planes.send_step(1, STEPS - 1)
    for field in range(2):
        planes.arrivals(field)
    fill_block(block, matrix_ref[...])
    for copy in table_loads:
        copy.wait()
    for field in range(2):
        planes.pass_arrivals(field)

    physics(
        planes.planes, modes.slab * STEPS + modes.chip, tables,
        lambda value: returns.start(1, value), lambda value: returns.start(0, value),
    )
    returns.finish(grads)

    def prepare(t, chunk, rows):
        for x in range(GROUP):
            weight = grads[t, pl.ds(GROUP * chunk + x, 1), :]
            act[t, GROUP * chunk + x] = (fields[t, GROUP * chunk + x] * weight).astype(BF16)

    analyze(prepare, lambda group: None)

    def mode_grads():
        lane = lax.broadcasted_iota(jnp.int32, (C, 2 * C), 1)
        first = lax.broadcasted_iota(jnp.int32, (C, 2 * C), 0)
        for j in range(2 * K):
            own, grad = coef[j : j + 1, :], grad_mixed[j : j + 1, :]
            real = jnp.sum(jnp.where(lane == first, own, 0.0), axis=1, keepdims=True)
            imag = jnp.sum(jnp.where(lane == first + C, own, 0.0), axis=1, keepdims=True)
            mode_ref[j // K, j % K] = real * grad + imag * turned_halves(grad)

    def second():
        local(1)
        mode_grads()

    modes.exchange_slabs(True, grad_mixed, lambda: local(0), second)

    def out_copy(t, chunk):
        rows = pl.ds(GROUP * chunk, GROUP)
        return pltpu.make_async_copy(
            act.at[t, rows], out_hbm.at[t, rows], out_store.at[t, chunk]
        )

    def put_out(group):
        def part(i):
            inner, chunk = i % GROUP, i // GROUP
            t, rows = GROUP * group + inner, pl.ds(GROUP * chunk, GROUP)
            found = spread_part(lines[rows], back_ref[inner], inner).reshape(GROUP, C, NY)
            act[t, rows] = (found + fields[t, rows]).astype(BF16)
            out_copy(t, chunk).start()

        loop(0, GROUP * GROUP, part, unroll=UNROLL)

    modes.pass_on(0)
    modes.gather_done(0)
    spread(0)
    modes.pass_on(1)
    put_out(0)
    modes.gather_done(1)
    spread(1)
    put_out(1)
    modes.wait_sends()
    planes.wait_sends()
    returns.wait_sends()
    for t in range(STEPS):
        loop(0, GROUP, lambda chunk: out_copy(t, chunk).wait())


VMEM = pl.BlockSpec(memory_space=pltpu.VMEM)
SMEM = pl.BlockSpec(memory_space=pltpu.SMEM)
ANY = pl.BlockSpec(memory_space=pl.ANY)
DMA = pltpu.SemaphoreType.DMA
LIMIT = 61 * 1024 * 1024
UNROLL = 2

FIELD = (CELLS, C, NY)
PLANE = (CELLS, NY)
PART = (C, LANES)
PAIR = (2 * K, 2 * C)


def vmem(*shape, dtype=F32):
    return pltpu.VMEM(shape, dtype)


MODE_SCRATCH, PLANE_SCRATCH, PHYSICS = 24, 10, 15


def mode_scratch():
    return [
        vmem(2, K, C, 2 * C),
        vmem(K * K, 2 * LANES),
        vmem(2 * K * K, 2 * LANES),
        vmem(2, CHIPS, 2, *PART),
        vmem(CHIPS, 2, *PART),
        vmem(CHIPS, 2, *PART),
        vmem(TM, *PAIR),
        vmem(TM, *PAIR),
        vmem(*PAIR),
        vmem(TM, *PAIR),
        vmem(2, K, *PART),
        DMA((3,)),
        *[DMA((CHIPS, 2))] * 4,
        *[DMA((TM,))] * 4,
        *[DMA((CHIPS, 2))] * 4,
    ]


def shards(activations, spectral_weight, pointwise, readout, forcing):
    line_forward, line_back = (jnp.asarray(t) for t in line_tables())
    phases = jnp.asarray(row_phases())
    sum_table, back_table = (jnp.asarray(t) for t in time_tables())
    physics_parts = [jnp.asarray(t) for t in physics_tables()]
    return pl.pallas_call(
        whole_kernel,
        out_shape=(
            jax.ShapeDtypeStruct((STEPS,) + FIELD, BF16),
            jax.ShapeDtypeStruct((2, K, C, 2 * C), F32),
        ),
        in_specs=[ANY, ANY, VMEM, VMEM, VMEM, VMEM, VMEM, SMEM, ANY, ANY] + [ANY] * PHYSICS,
        out_specs=(ANY, VMEM),
        scratch_shapes=[
            vmem(STEPS, *FIELD, dtype=BF16),
            vmem(CELLS, *PART),
            vmem(GROUP * C, GROUP * C, dtype=BF16),
            vmem(C, LANES),
            vmem(STEPS, *FIELD),
            vmem(STEPS, *PLANE),
            vmem(*PAIR),
            vmem(*PAIR),
            DMA((STEPS,)),
            DMA((STEPS, GROUP)),
            DMA((PHYSICS,)),
            *[vmem(*t.shape, dtype=t.dtype) for t in physics_parts],
            *mode_scratch(),
            vmem(STEPS, *PLANE),
            vmem(STEPS, *PLANE),
            vmem(2, *PLANE),
            vmem(2, ROWS, *PLANE),
            DMA((2,)),
            DMA((2,)),
            *[DMA((2, CHIPS))] * 4,
            vmem(2, ROWS, *PLANE),
            vmem(2, CHIPS, *PLANE),
            vmem(2, *PLANE),
            *[DMA((2, CHIPS))] * 2,
            DMA((2,)),
            DMA((2,)),
        ],
        compiler_params=pltpu.CompilerParams(
            collective_id=0, has_side_effects=True, vmem_limit_bytes=LIMIT
        ),
        name="whole",
    )(
        activations, spectral_weight, pointwise, readout.reshape(1, C), forcing, line_forward,
        line_back, phases, sum_table, back_table, *physics_parts,
    )


def solution(mesh):
    return jax.shard_map(
        shards,
        mesh=mesh,
        in_specs=(
            P("tm", "rows", None, None),
            P(("rows", "tm"), None, None, None),
            P(),
            P(),
            P("rows", None),
        ),
        out_specs=(P("tm", "rows", None, None), P(("rows", "tm"), None, None, None)),
        check_vma=False,
    )
```

```python
import math

import jax
import jax.numpy as jnp
import ml_dtypes
import numpy as np
from jax import lax
from jax.experimental import pallas as pl
from jax.experimental.pallas import tpu as pltpu
from jax.sharding import PartitionSpec as P

MESH = pl.DeviceIdType.MESH
VISCOSITY = 0.002
LOSS_WEIGHT = 0.005
C, K, NY, NX, NT = 64, 16, 512, 256, 64
ROWS, TM = 16, 8
CHIPS = ROWS // 2
STEPS, CELLS = NT // TM, NX // ROWS
HALF = NY // 2
GROUP, LANES = 4, 128
MIDDLE = (CELLS - 1) / 2
S_GRID = 1.0 / math.sqrt(NT * NX * NY)
S_MODE = 1.0 / math.sqrt(K * K * K)
TWO_PI = 2.0 * math.pi
BF16 = jnp.bfloat16
F32 = jnp.float32


def halves(table):
    table = table.astype(np.float32)
    high = table.astype(ml_dtypes.bfloat16)
    low = (table - high.astype(np.float32)).astype(ml_dtypes.bfloat16)
    return high, low


def line_tables():
    numbers = np.arange(K) - K // 2
    angles = (TWO_PI / NY) * (np.outer(numbers, np.arange(NY)) % NY)
    table = np.concatenate([np.cos(angles), -np.sin(angles)], axis=0).astype(np.float32)
    forward = np.zeros((GROUP, NY, LANES), ml_dtypes.bfloat16)
    back = np.zeros((GROUP, LANES, NY), ml_dtypes.bfloat16)
    high, low = halves(table)
    for t in range(GROUP):
        forward[t, :, 2 * K * t : 2 * K * (t + 1)] = table.astype(ml_dtypes.bfloat16).T
        for place, part in enumerate((high, high, low)):
            first = 2 * K * ((t + place) % GROUP)
            back[t, first : first + 2 * K] = part
    return forward, back


def time_tables():
    numbers = np.arange(K) - K // 2
    steps = np.arange(NT).reshape(TM, STEPS)
    angles = (TWO_PI / NT) * ((numbers[None, :, None] * steps[:, None, :]) % NT)
    unit = np.eye(K)

    def spread(real, imag):
        both = np.stack([real, imag], axis=3)
        return np.einsum("matr,ef->maetrf", both, unit).reshape(TM, K * K, STEPS * 2 * K)

    cos_part, sin_part = np.cos(angles), np.sin(angles)
    forward = spread(cos_part, sin_part)
    back = np.concatenate([spread(cos_part, sin_part), spread(-sin_part, cos_part)], axis=1)
    return forward.astype(np.float32), back.astype(np.float32)


def row_phases():
    numbers = np.arange(K) - K // 2
    angles = (TWO_PI / NX) * np.outer(CELLS * np.arange(ROWS) + MIDDLE, numbers)
    return np.stack([np.cos(angles), np.sin(angles)]).astype(np.float32)


def physics_tables():
    y = np.arange(NY)
    ky = np.arange(HALF)
    angles = (TWO_PI / NY) * (np.outer(y, ky) % NY)
    row_forward = np.concatenate([np.cos(angles), -np.sin(angles)], axis=1)
    scaling = np.where(ky == 0, 1.0, 2.0)[:, None] / NY
    row_back = np.concatenate([scaling * np.cos(angles).T, -scaling * np.sin(angles).T], axis=0)
    gap = np.arange(NY)
    gap_angles = (TWO_PI / NY) * (np.outer(gap, ky) % NY)
    slope = -(2.0 / NY) * (np.sin(gap_angles) * ky).sum(1)
    bend = -(2.0 / NY) * (np.cos(gap_angles) * ky * ky).sum(1)
    turn = (y[None, :] - y[:, None]) % NY
    row_slope, row_bend = slope[turn], bend[turn]
    x = np.arange(NX)
    kx = np.where(x < NX // 2, x, x - NX)
    dx = np.where(x == NX // 2, 0, kx)
    col_angles = (TWO_PI / NX) * (np.outer(x, x) % NX)
    col_slope = -(np.sin(col_angles) * dx).sum(1) / NX
    col_bend = -(np.cos(col_angles) * kx * kx).sum(1) / NX
    col_turn = (x[:, None] - x[None, :]) % NX
    col_slope, col_bend = col_slope[col_turn], col_bend[col_turn]
    col_wave = np.concatenate([np.cos(col_angles), np.sin(col_angles)], axis=0)
    squared = (kx[:, None] ** 2 + ky[None, :] ** 2).astype(np.float64)
    inverse = np.where(squared > 0, 1.0 / np.where(squared > 0, squared, 1.0), 0.0) / NX
    inverse = np.concatenate([inverse, inverse], axis=1).astype(np.float32)
    pairs = [
        halves(t)
        for t in (
            row_forward,
            row_back,
            row_slope,
            VISCOSITY * row_bend,
            col_wave,
            col_slope,
            VISCOSITY * col_bend,
        )
    ]
    return [t for pair in pairs for t in pair] + [inverse]


def turned_halves(z):
    moved = pltpu.roll(z, C, 1)
    low = lax.broadcasted_iota(jnp.int32, z.shape, 1) < C
    return jnp.where(low, moved, -moved)


def turned(z):
    real = lax.broadcasted_iota(jnp.int32, z.shape, 1) % (2 * K) < K
    return jnp.where(real, pltpu.roll(z, LANES - K, 1), -pltpu.roll(z, K, 1))


def loop(first, last, body, unroll=1):
    def step(j, carry):
        body(j)
        return carry

    lax.fori_loop(first, last, step, 0, unroll=unroll)


def project_rows(lines, phase_ref, store):
    row = lax.axis_index("rows")

    def part(chunk):
        rows = pl.ds(pl.multiple_of(8 * chunk, 8), 8)
        far = range(CELLS // 2, CELLS)
        pairs = [(lines[x, rows, :], lines[CELLS - 1 - x, rows, :]) for x in far]
        added = [right + left for right, left in pairs]
        taken = [turned(right - left) for right, left in pairs]
        for k in range(K // 2 + 1):
            even, odd = None, None
            for x, both, gap in zip(far, added, taken):
                angle = TWO_PI * k * (x - MIDDLE) / NX
                cos_term = both if k == 0 else math.cos(angle) * both
                even = cos_term if even is None else even + cos_term
                if k:
                    sin_term = math.sin(angle) * gap
                    odd = sin_term if odd is None else odd + sin_term
            found = []
            if k < K // 2:
                found.append((K // 2 + k, even if odd is None else even + odd))
            if k > 0:
                found.append((K // 2 - k, even - odd))
            for b, value in found:
                cos_b, sin_b = phase_ref[0, row, b], phase_ref[1, row, b]
                store(b, rows, cos_b * value + sin_b * turned(value))

    loop(0, C // 8, part)


def spread_rows(modes, phase_ref, spread):
    row = lax.axis_index("rows")

    def part(chunk):
        rows = pl.ds(pl.multiple_of(8 * chunk, 8), 8)
        z = []
        for b in range(K):
            cos_b, sin_b = phase_ref[0, row, b], phase_ref[1, row, b]
            value = modes(b, rows)
            z.append(cos_b * value - sin_b * turned(value))
        even, odd = [z[K // 2]], [None]
        for k in range(1, K // 2):
            even.append(z[K // 2 + k] + z[K // 2 - k])
            odd.append(turned(z[K // 2 - k] - z[K // 2 + k]))
        even.append(z[0])
        odd.append(turned(z[0]))
        for x in range(CELLS // 2, CELLS):
            same, changed = even[0], None
            for k in range(1, K // 2 + 1):
                angle = TWO_PI * k * (x - MIDDLE) / NX
                same = same + math.cos(angle) * even[k]
                term = math.sin(angle) * odd[k]
                changed = term if changed is None else changed + term
            spread[x, rows, :] = same + changed
            spread[CELLS - 1 - x, rows, :] = same - changed

    loop(0, C // 8, part)


def fill_block(block, matrix):
    block[...] = jnp.zeros_like(block)
    for x in range(GROUP):
        block[C * x : C * (x + 1), C * x : C * (x + 1)] = matrix


def spread_part(spread, back, t):
    total = spread.reshape(GROUP * C, LANES)
    high = total.astype(BF16).astype(F32)
    lane = lax.broadcasted_iota(jnp.int32, total.shape, 1) // (2 * K)
    left = jnp.where(
        lane == t,
        high,
        jnp.where(
            lane == (t + 1) % GROUP,
            pltpu.roll(total - high, 2 * K, 1),
            pltpu.roll(high, 4 * K, 1),
        ),
    ).astype(BF16)
    return jnp.dot(left, back, preferred_element_type=F32)


def physics(planes, step, tables, between, wait_rate, send_weighted, send_grad):
    (rf, rf_low, rb, rb_low, rs, rs_low, rc, rc_low, cw, cw_low, cs, cs_low, cc, cc_low, inverse) = (
        tables
    )

    def parts(value):
        high = value.astype(BF16)
        return high, (value - high.astype(F32)).astype(BF16)

    def dot(a, b):
        return jnp.dot(a, b, preferred_element_type=F32)

    def along(value, high, low):
        v_high, v_low = parts(value)
        return dot(v_high, high[...]) + (dot(v_low, high[...]) + dot(v_high, low[...]))

    def across(high, low, value):
        v_high, v_low = parts(value)
        return dot(high[...], v_high) + (dot(high[...], v_low) + dot(low[...], v_high))

    def minus_i(z):
        return jnp.concatenate([z[:, HALF:], -z[:, :HALF]], axis=1)

    def solve(value):
        spectrum = along(value, rf, rf_low)
        both = across(cw, cw_low, spectrum)
        spectrum = (both[:NX] + minus_i(both[NX:])) * inverse[...]
        both = across(cw, cw_low, spectrum)
        return along(both[:NX] - minus_i(both[NX:]), rb, rb_low)

    sign = jnp.where(lax.broadcasted_iota(jnp.int32, (NX, NY), 1) % 2 == 0, 1.0, -1.0).astype(F32)

    def smooth(value):
        return value - sign * (jnp.sum(value * sign, axis=1, keepdims=True) * (1.0 / NY))

    inside = (step > 0) & (step < NT - 1)
    vort = planes[0].reshape(NX, NY)
    stream = solve(vort)
    between()
    slopes = along(jnp.concatenate([vort, stream], axis=0), rs, rs_low)
    slope_right, flow_down = slopes[:NX], slopes[NX:]
    smoothed = smooth(vort)
    slopes = across(cs, cs_low, jnp.concatenate([smoothed, stream], axis=1))
    slope_down, flow_right = slopes[:, :NY], -slopes[:, NY:]
    bend = along(vort, rc, rc_low) + across(cc, cc_low, smoothed)
    wait_rate()
    rate = planes[1].reshape(NX, NY)
    residual = (
        rate
        + flow_down * slope_down
        + flow_right * slope_right
        - bend
    )
    weighted = jnp.where(inside, LOSS_WEIGHT * residual, 0.0)
    send_weighted(weighted)
    first = weighted * slope_down
    second = weighted * slope_right
    slopes = along(jnp.concatenate([first, flow_right * weighted], axis=0), rs, rs_low)
    first_along, flow_along = slopes[:NX], slopes[NX:]
    slopes = across(
        cs, cs_low, jnp.concatenate([second, smooth(flow_down * weighted)], axis=1)
    )
    second_across, flow_across = slopes[:, :NY], slopes[:, NY:]
    solved = solve(second_across - first_along)
    bend = along(weighted, rc, rc_low) + across(cc, cc_low, smooth(weighted))
    grad = solved - bend - flow_across - flow_along
    send_grad(grad)


def remote(src, dst, send, recv, device):
    return pltpu.make_async_remote_copy(
        src_ref=src, dst_ref=dst, send_sem=send, recv_sem=recv, device_id=device,
        device_id_type=MESH,
    )


def place():
    row, slab = lax.axis_index("rows"), lax.axis_index("tm")
    return row, slab, row // 2, row % 2


def greet():
    row, slab, chip, core = place()
    barrier = pltpu.get_barrier_semaphore()
    pl.semaphore_signal(
        barrier, inc=1, device_id=(row + 1 - 2 * core, slab), device_id_type=MESH
    )

    def tell(j):
        peer = 2 * ((chip + j) % CHIPS) + core
        pl.semaphore_signal(barrier, inc=1, device_id=(peer, slab), device_id_type=MESH)
        pl.semaphore_signal(
            barrier, inc=1, device_id=(row, (slab + j) % TM), device_id_type=MESH
        )

    loop(1, CHIPS, tell)


def all_here():
    pl.semaphore_wait(pltpu.get_barrier_semaphore(), 1 + (CHIPS - 1) + (TM - 1))


class Modes:
    def __init__(self, w_hbm, sum_hbm, back_hbm, scratch):
        (
            self.weight, self.sum_table, self.back_table, self.terms, self.from_core,
            self.from_rows, self.parts, self.from_slabs, self.mixed, self.slabs, self.gathered,
            self.load, self.core_send, self.core_recv, self.row_send, self.row_recv,
            self.slab_send, self.slab_recv, self.mix_send, self.mix_recv, self.out_send,
            self.out_recv, self.pass_send, self.pass_recv,
        ) = scratch
        self.row, self.slab, self.chip, self.core = place()
        self.other = (self.row + 1 - 2 * self.core, self.slab)
        self.loads = [
            pltpu.make_async_copy(src, dst, self.load.at[i])
            for i, (src, dst) in enumerate(
                (
                    (sum_hbm.at[self.slab], self.sum_table),
                    (w_hbm, self.weight),
                    (back_hbm.at[self.slab], self.back_table),
                )
            )
        ]

    def start_loads(self):
        for load in self.loads:
            load.start()

    def store(self, group):
        def put(b, rows, value):
            self.terms[b % 2, b // 2, group, rows, :] = value

        return put

    def core_copy(self, group, j):
        to = (self.chip + j) % CHIPS
        return remote(
            self.terms.at[1 - self.core, to, group], self.from_core.at[to, group],
            self.core_send.at[to, group], self.core_recv.at[to, group], self.other,
        )

    def row_copy(self, group, j):
        to = (self.chip + j) % CHIPS
        return remote(
            self.from_core.at[to, group], self.from_rows.at[self.chip, group],
            self.row_send.at[to, group], self.row_recv.at[self.chip, group],
            (2 * to + self.core, self.slab),
        )

    def start_core(self, group):
        loop(1, CHIPS + 1, lambda j: self.core_copy(group, j).start())

    def forward(self, group):
        def step(j):
            to = (self.chip + j) % CHIPS
            self.core_copy(group, j).wait_recv()
            self.from_core[to, group] = (
                self.from_core[to, group] + self.terms[self.core, to, group]
            )
            self.row_copy(group, j).start()

        loop(1, CHIPS, step)
        self.core_copy(group, CHIPS).wait_recv()
        self.from_rows[self.chip, group] = (
            self.from_core[self.chip, group] + self.terms[self.core, self.chip, group]
        )

    def arrivals(self, group):
        def step(j):
            source = (self.chip + CHIPS - j) % CHIPS
            remote(
                self.from_core.at[source, group], self.from_rows.at[source, group],
                self.row_send.at[source, group], self.row_recv.at[source, group],
                (2 * source + self.core, self.slab),
            ).wait_recv()

        loop(1, CHIPS, step)
        total = self.from_rows[0, group]
        for source in range(1, CHIPS):
            total = total + self.from_rows[source, group]
        return total

    def slab_copy(self, j):
        to = (self.slab + j) % TM
        return remote(
            self.parts.at[to], self.from_slabs.at[self.slab], self.slab_send.at[to],
            self.slab_recv.at[self.slab], (self.row, to),
        )

    def mix_copy(self, j):
        to = (self.slab + j) % TM
        return remote(
            self.mixed, self.slabs.at[self.slab], self.mix_send.at[to],
            self.mix_recv.at[self.slab], (self.row, to),
        )

    def exchange_slabs(self, gradient, coef_ref, first, second):
        totals = [self.arrivals(group) for group in range(2)]
        both = jnp.concatenate(
            [
                jnp.concatenate(totals, axis=1),
                jnp.concatenate([turned(total) for total in totals], axis=1),
            ],
            axis=0,
        )
        if not gradient:
            self.loads[0].wait()
        found = lax.dot_general(
            self.sum_table[...], both, (((1,), (1,)), ((), ())),
            precision=lax.Precision.HIGHEST, preferred_element_type=F32,
        )
        self.parts[...] = (found * (S_MODE if gradient else S_GRID)).reshape(
            TM, 2 * K, 2 * C
        )
        loop(1, TM, lambda j: self.slab_copy(j).start())
        self.from_slabs[self.slab] = self.parts[self.slab]
        first()
        if not gradient:
            self.loads[1].wait()

        def slab_arrival(j):
            source = (self.slab + TM - j) % TM
            remote(
                self.parts.at[source], self.from_slabs.at[source], self.slab_send.at[source],
                self.slab_recv.at[source], (self.row, source),
            ).wait_recv()

        loop(1, TM, slab_arrival)
        coef = self.from_slabs[0]
        for source in range(1, TM):
            coef = coef + self.from_slabs[source]
        coef_ref[...] = coef
        if gradient:
            self.mix_back(coef)
        else:
            self.mix(coef)
        loop(1, TM, lambda j: self.mix_copy(j).start())
        self.slabs[self.slab] = self.mixed[...]
        second()

        def mix_arrival(j):
            source = (self.slab + TM - j) % TM
            remote(
                self.mixed, self.slabs.at[source], self.mix_send.at[source],
                self.mix_recv.at[source], (self.row, source),
            ).wait_recv()

        loop(1, TM, mix_arrival)
        if not gradient:
            self.loads[2].wait()
        whole = jnp.transpose(self.slabs[...].reshape(K * K, 2 * C))
        spread = (S_GRID if gradient else S_MODE) * jnp.dot(
            jnp.concatenate([whole[:C], whole[C:]], axis=1), self.back_table[...],
            precision=lax.Precision.HIGHEST, preferred_element_type=F32,
        )
        self.gathered[0, self.row] = spread[:, :LANES]
        self.gathered[1, self.row] = spread[:, LANES:]
        for group in range(2):
            loop(1, CHIPS, lambda j: self.out_copy(group, j).start())
            self.pass_copy(group, self.chip).start()

    def mix(self, coef):
        columns = jnp.transpose(
            jnp.concatenate([coef, jnp.zeros((2 * C - 2 * K, 2 * C), F32)], axis=0)
        )
        for j in range(2 * K):
            weight = self.weight[j // K, j % K]
            re = jnp.sum(weight * columns[:C, j : j + 1], axis=0, keepdims=True)
            im = jnp.sum(weight * columns[C:, j : j + 1], axis=0, keepdims=True)
            self.mixed[j : j + 1, :] = re - turned_halves(im)

    def mix_back(self, coef):
        turned_coef = turned_halves(coef)
        lane = lax.broadcasted_iota(jnp.int32, (C, 2 * C), 1)
        real = jnp.zeros((C, 2 * C), F32)
        imag = jnp.zeros((C, 2 * C), F32)
        for j in range(2 * K):
            weight = self.weight[j // K, j % K]
            re = jnp.sum(weight * coef[j : j + 1, :], axis=1, keepdims=True)
            im = jnp.sum(weight * turned_coef[j : j + 1, :], axis=1, keepdims=True)
            real = jnp.where(lane == j, re, real)
            imag = jnp.where(lane == j, im, imag)
        self.mixed[...] = jnp.transpose(jnp.concatenate([real, imag], axis=0))[: 2 * K]

    def out_copy(self, group, j):
        to = (self.chip + j) % CHIPS
        block = self.gathered.at[group, self.row]
        return remote(
            block, block, self.out_send.at[to, group], self.out_recv.at[self.chip, group],
            (2 * to + self.core, self.slab),
        )

    def pass_copy(self, group, source):
        block = self.gathered.at[group, 2 * source + self.core]
        return remote(
            block, block, self.pass_send.at[source, group], self.pass_recv.at[source, group],
            self.other,
        )

    def pass_on(self, group):
        def step(j):
            source = (self.chip + CHIPS - j) % CHIPS
            block = self.gathered.at[group, 2 * source + self.core]
            remote(
                block, block, self.out_send.at[source, group], self.out_recv.at[source, group],
                (2 * source + self.core, self.slab),
            ).wait_recv()
            self.pass_copy(group, source).start()

        loop(1, CHIPS, step)

    def gather_done(self, group):
        def step(source):
            block = self.gathered.at[group, 2 * source + 1 - self.core]
            remote(
                block, block, self.pass_send.at[source, group], self.pass_recv.at[source, group],
                self.other,
            ).wait_recv()

        loop(0, CHIPS, step)

    def wait_sends(self):
        loop(1, TM, lambda j: self.slab_copy(j).wait_send())
        loop(1, TM, lambda j: self.mix_copy(j).wait_send())
        for group in range(2):
            loop(1, CHIPS + 1, lambda j: self.core_copy(group, j).wait_send())
            loop(1, CHIPS, lambda j: self.row_copy(group, j).wait_send())
            loop(1, CHIPS, lambda j: self.out_copy(group, j).wait_send())
            loop(0, CHIPS, lambda j: self.pass_copy(group, j).wait_send())


class Planes:
    def __init__(self, forcing_ref, scratch):
        (
            self.vort, self.rates, self.halo, self.planes, self.halo_send, self.halo_recv,
            self.send, self.recv, self.pass_send, self.pass_recv,
        ) = scratch
        self.forcing = forcing_ref
        self.row, self.slab, self.chip, self.core = place()
        self.other = (self.row + 1 - 2 * self.core, self.slab)
        after, before = (self.slab + 1) % TM, (self.slab + TM - 1) % TM
        self.to_after = remote(
            self.vort.at[STEPS - 1], self.halo.at[0], self.halo_send.at[0], self.halo_recv.at[0],
            (self.row, after),
        )
        self.to_before = remote(
            self.vort.at[0], self.halo.at[1], self.halo_send.at[1], self.halo_recv.at[1],
            (self.row, before),
        )

    def copy(self, field, to):
        source = (self.vort, self.rates)[field].at[to]
        return remote(
            source, self.planes.at[field, self.row], self.send.at[field, to],
            self.recv.at[field, self.chip], (2 * to + self.core, self.slab),
        )

    def pass_copy(self, field, source):
        block = self.planes.at[field, 2 * source + self.core]
        return remote(
            block, block, self.pass_send.at[field, source], self.pass_recv.at[field, source],
            self.other,
        )

    def send_step(self, field, to):
        @pl.when(to != self.chip)
        def _():
            self.copy(field, to).start()

        @pl.when(to == self.chip)
        def _():
            self.planes[field, self.row] = (self.vort, self.rates)[field][to]
            self.pass_copy(field, self.chip).start()

    def rate(self, step, low, high):
        self.rates[step] = (0.5 * NT) * (high - low) - self.forcing[...]

    def inner_rates(self, first, last):
        for step in range(first, last):
            self.rate(step, self.vort[step - 1], self.vort[step + 1])
            self.send_step(1, step)

    def arrivals(self, field):
        def step(j):
            source = (self.chip + CHIPS - j) % CHIPS
            block = 2 * source + self.core
            remote(
                self.vort.at[source], self.planes.at[field, block], self.send.at[field, source],
                self.recv.at[field, source], (block, self.slab),
            ).wait_recv()
            self.pass_copy(field, source).start()

        loop(1, CHIPS, step)

    def pass_arrivals(self, field):
        def step(source):
            block = self.planes.at[field, 2 * source + 1 - self.core]
            remote(
                block, block, self.pass_send.at[field, source], self.pass_recv.at[field, source],
                self.other,
            ).wait_recv()

        loop(0, CHIPS, step)

    def wait_sends(self):
        self.to_after.wait_send()
        self.to_before.wait_send()
        for field in range(2):
            loop(1, CHIPS, lambda j: self.copy(field, (self.chip + j) % CHIPS).wait_send())
            loop(0, CHIPS, lambda j: self.pass_copy(field, j).wait_send())


class Returns:
    def __init__(self, scratch):
        (
            self.source, self.steps, self.halo, self.send, self.recv, self.halo_send,
            self.halo_recv,
        ) = scratch
        self.row, self.slab, self.chip, self.core = place()
        after, before = (self.slab + 1) % TM, (self.slab + TM - 1) % TM
        self.to_after = remote(
            self.steps.at[1, STEPS - 1], self.halo.at[0], self.halo_send.at[0],
            self.halo_recv.at[0], (self.row, after),
        )
        self.to_before = remote(
            self.steps.at[1, 0], self.halo.at[1], self.halo_send.at[1], self.halo_recv.at[1],
            (self.row, before),
        )

    def copy(self, field, j):
        to = (self.chip + j) % CHIPS
        block = 2 * to + self.core
        return remote(
            self.source.at[field, block], self.steps.at[field, self.chip],
            self.send.at[field, to], self.recv.at[field, self.chip], (block, self.slab),
        )

    def start(self, field, value):
        self.source[field] = value.reshape(ROWS, CELLS, NY)
        loop(1, CHIPS, lambda j: self.copy(field, j).start())
        self.steps[field, self.chip] = self.source[field, self.row]

    def arrivals(self, field):
        def step(j):
            source = (self.chip + CHIPS - j) % CHIPS
            block = 2 * source + self.core
            remote(
                self.source.at[field, block], self.steps.at[field, source],
                self.send.at[field, source], self.recv.at[field, source], (block, self.slab),
            ).wait_recv()

        loop(1, CHIPS, step)

    def finish(self, grads):
        self.arrivals(1)
        self.to_after.start()
        self.to_before.start()
        self.arrivals(0)

        def grad(step, low, high):
            grads[step] = self.steps[0, step] + (0.5 * NT) * (low - high)

        for step in range(1, STEPS - 1):
            grad(step, self.steps[1, step - 1], self.steps[1, step + 1])
        self.to_after.wait_recv()
        grad(0, self.halo[0], self.steps[1, 1])
        self.to_before.wait_recv()
        grad(STEPS - 1, self.steps[1, STEPS - 2], self.halo[1])

    def wait_sends(self):
        self.to_after.wait_send()
        self.to_before.wait_send()
        for field in range(2):
            loop(1, CHIPS, lambda j: self.copy(field, j).wait_send())


def whole_kernel(
    act_hbm, w_hbm, matrix_ref, readout_ref, forcing_ref, forward_ref, back_ref, phase_ref,
    sum_hbm, back_hbm, *rest,
):
    table_hbm, rest = rest[:PHYSICS], rest[PHYSICS:]
    act, mode_ref, lines, block, wide, fields, grads, coef, grad_mixed = rest[:9]
    act_load, table_load = rest[9:11]
    rest = rest[11:]
    tables, rest = rest[:PHYSICS], rest[PHYSICS:]
    modes = Modes(w_hbm, sum_hbm, back_hbm, rest[:MODE_SCRATCH])
    planes = Planes(forcing_ref, rest[MODE_SCRATCH : MODE_SCRATCH + PLANE_SCRATCH])
    returns = Returns(rest[MODE_SCRATCH + PLANE_SCRATCH :])

    def load(t):
        return pltpu.make_async_copy(act_hbm.at[t], act.at[t], act_load.at[t])

    table_loads = [
        pltpu.make_async_copy(src, dst, table_load.at[i])
        for i, (src, dst) in enumerate(zip(table_hbm, tables))
    ]
    greet()
    for t in range(STEPS):
        load(t).start()
    modes.start_loads()
    for copy in table_loads:
        copy.start()
    same = lax.broadcasted_iota(jnp.int32, (C, C), 0) == lax.broadcasted_iota(
        jnp.int32, (C, C), 1
    )
    unit = jnp.where(same, 1.0, 0.0).astype(BF16)
    fill_block(
        block,
        lax.dot_general(
            matrix_ref[...], unit, (((0,), (0,)), ((), ())), preferred_element_type=F32
        ).astype(BF16),
    )
    wide[...] = 0.5 * jnp.broadcast_to(
        jnp.sum(jnp.where(same, readout_ref[...], 0.0), axis=1, keepdims=True), (C, LANES)
    )

    def make_lines(group, prepare):
        def part(chunk):
            rows = pl.ds(GROUP * chunk, GROUP)
            total = None
            for inner in range(GROUP):
                t = GROUP * group + inner
                prepare(t, chunk, rows)
                term = jnp.dot(
                    act[t, rows].reshape(GROUP * C, NY), forward_ref[inner],
                    preferred_element_type=F32,
                )
                total = term if total is None else total + term
            lines[rows] = total.reshape(GROUP, C, LANES)

        loop(0, GROUP, part)

    def analyze(prepare, before, ready):
        before(0)
        make_lines(0, prepare)
        project_rows(lines, phase_ref, modes.store(0))
        ready()
        modes.start_core(0)
        before(1)
        make_lines(1, prepare)
        modes.forward(0)
        project_rows(lines, phase_ref, modes.store(1))
        modes.start_core(1)
        modes.forward(1)

    def local(quarter):
        def part(i):
            t, rows = 2 * quarter + i % 2, pl.ds(GROUP * (i // 2), GROUP)
            fields[t, rows] = jnp.dot(
                block[...], act[t, rows].reshape(GROUP * C, NY), preferred_element_type=F32
            ).reshape(GROUP, C, NY)

        loop(0, 2 * GROUP, part, unroll=UNROLL)

    def wait_load(group):
        for t in range(GROUP):
            load(GROUP * group + t).wait()

    analyze(lambda t, chunk, rows: None, wait_load, all_here)
    local(0)
    modes.exchange_slabs(False, coef, lambda: local(1), lambda: local(2))
    local(3)

    c0 = math.sqrt(2.0 / math.pi)
    c1 = c0 * 0.044715

    def hide(group):
        def part(i):
            inner, chunk = i % GROUP, i // GROUP
            t = GROUP * group + inner
            found = spread_part(lines[pl.ds(GROUP * chunk, GROUP)], back_ref[inner], inner)
            for x in range(GROUP):
                total = None
                for part_of in range(C // 16):
                    own = slice(16 * part_of, 16 * part_of + 16)
                    readout = jnp.concatenate([wide[own]] * (NY // LANES), axis=1)
                    place_of = C * x + 16 * part_of
                    value = found[place_of : place_of + 16] + fields[t, GROUP * chunk + x, own, :]
                    square = value * value
                    bend = jnp.tanh(value * (c0 + c1 * square))
                    scaled = readout * (1.0 + bend)
                    steep = (1.0 - bend) * (value * (c0 + 3.0 * c1 * square))
                    fields[t, GROUP * chunk + x, own, :] = scaled + scaled * steep
                    term = scaled * value
                    term = term[:8] + term[8:]
                    total = term if total is None else total + term
                planes.vort[t, pl.ds(GROUP * chunk + x, 1), :] = jnp.sum(
                    total, axis=0, keepdims=True
                )

        loop(0, GROUP * GROUP, part, unroll=UNROLL)

    def spread(group):
        spread_rows(lambda b, rows: modes.gathered[group, b, rows, :], phase_ref, lines)

    modes.pass_on(0)
    modes.gather_done(0)
    spread(0)
    modes.pass_on(1)
    hide(0)
    planes.to_before.start()
    for t in range(GROUP):
        planes.send_step(0, t)
    planes.inner_rates(1, GROUP - 1)
    modes.gather_done(1)
    spread(1)
    hide(1)
    planes.to_after.start()
    for t in range(GROUP, STEPS):
        planes.send_step(0, t)
    planes.inner_rates(GROUP - 1, STEPS - 1)
    modes.wait_sends()
    planes.to_after.wait_recv()
    planes.rate(0, planes.halo[0], planes.vort[1])
    planes.send_step(1, 0)
    planes.to_before.wait_recv()
    planes.rate(STEPS - 1, planes.vort[STEPS - 2], planes.halo[1])
    planes.send_step(1, STEPS - 1)
    planes.arrivals(0)
    fill_block(block, matrix_ref[...])
    for copy in table_loads:
        copy.wait()
    planes.pass_arrivals(0)

    physics(
        planes.planes, modes.slab * STEPS + modes.chip, tables,
        lambda: planes.arrivals(1), lambda: planes.pass_arrivals(1),
        lambda value: returns.start(1, value), lambda value: returns.start(0, value),
    )
    returns.finish(grads)

    def prepare(t, chunk, rows):
        for x in range(GROUP):
            weight = grads[t, pl.ds(GROUP * chunk + x, 1), :]
            act[t, GROUP * chunk + x] = (fields[t, GROUP * chunk + x] * weight).astype(BF16)

    analyze(prepare, lambda group: None, lambda: None)

    def mode_grads():
        lane = lax.broadcasted_iota(jnp.int32, (C, 2 * C), 1)
        first = lax.broadcasted_iota(jnp.int32, (C, 2 * C), 0)
        for j in range(2 * K):
            own, grad = coef[j : j + 1, :], grad_mixed[j : j + 1, :]
            real = jnp.sum(jnp.where(lane == first, own, 0.0), axis=1, keepdims=True)
            imag = jnp.sum(jnp.where(lane == first + C, own, 0.0), axis=1, keepdims=True)
            mode_ref[j // K, j % K] = real * grad + imag * turned_halves(grad)

    def second():
        local(2)
        mode_grads()

    local(0)
    modes.exchange_slabs(True, grad_mixed, lambda: local(1), second)
    local(3)

    def put_out(group):
        def part(i):
            inner, chunk = i % GROUP, i // GROUP
            t, rows = GROUP * group + inner, pl.ds(GROUP * chunk, GROUP)
            found = spread_part(lines[rows], back_ref[inner], inner).reshape(GROUP, C, NY)
            act[t, rows] = (found + fields[t, rows]).astype(BF16)

        loop(0, GROUP * GROUP, part, unroll=UNROLL)

    modes.pass_on(0)
    modes.gather_done(0)
    spread(0)
    modes.pass_on(1)
    put_out(0)
    modes.gather_done(1)
    spread(1)
    put_out(1)
    modes.wait_sends()
    planes.wait_sends()
    returns.wait_sends()


VMEM = pl.BlockSpec(memory_space=pltpu.VMEM)
SMEM = pl.BlockSpec(memory_space=pltpu.SMEM)
ANY = pl.BlockSpec(memory_space=pl.ANY)
DMA = pltpu.SemaphoreType.DMA
LIMIT = 46 * 1024 * 1024
UNROLL = 2

FIELD = (CELLS, C, NY)
PLANE = (CELLS, NY)
PART = (C, LANES)
PAIR = (2 * K, 2 * C)


def vmem(*shape, dtype=F32):
    return pltpu.VMEM(shape, dtype)


MODE_SCRATCH, PLANE_SCRATCH, PHYSICS = 24, 10, 15


def mode_scratch():
    return [
        vmem(2, K, C, 2 * C),
        vmem(K * K, 2 * LANES),
        vmem(2 * K * K, 2 * LANES),
        vmem(2, CHIPS, 2, *PART),
        vmem(CHIPS, 2, *PART),
        vmem(CHIPS, 2, *PART),
        vmem(TM, *PAIR),
        vmem(TM, *PAIR),
        vmem(*PAIR),
        vmem(TM, *PAIR),
        vmem(2, K, *PART),
        DMA((3,)),
        *[DMA((CHIPS, 2))] * 4,
        *[DMA((TM,))] * 4,
        *[DMA((CHIPS, 2))] * 4,
    ]


def shards(activations, spectral_weight, pointwise, readout, forcing):
    line_forward, line_back = (jnp.asarray(t) for t in line_tables())
    phases = jnp.asarray(row_phases())
    sum_table, back_table = (jnp.asarray(t) for t in time_tables())
    physics_parts = [jnp.asarray(t) for t in physics_tables()]
    return pl.pallas_call(
        whole_kernel,
        out_shape=(
            pltpu.VMEM((STEPS,) + FIELD, BF16),
            pltpu.VMEM((2, K, C, 2 * C), F32),
        ),
        in_specs=[ANY, ANY, VMEM, VMEM, VMEM, VMEM, VMEM, SMEM, ANY, ANY] + [ANY] * PHYSICS,
        out_specs=(VMEM, VMEM),
        scratch_shapes=[
            vmem(CELLS, *PART),
            vmem(GROUP * C, GROUP * C, dtype=BF16),
            vmem(C, LANES),
            vmem(STEPS, *FIELD),
            vmem(STEPS, *PLANE),
            vmem(*PAIR),
            vmem(*PAIR),
            DMA((STEPS,)),
            DMA((PHYSICS,)),
            *[vmem(*t.shape, dtype=t.dtype) for t in physics_parts],
            *mode_scratch(),
            vmem(STEPS, *PLANE),
            vmem(STEPS, *PLANE),
            vmem(2, *PLANE),
            vmem(2, ROWS, *PLANE),
            DMA((2,)),
            DMA((2,)),
            *[DMA((2, CHIPS))] * 4,
            vmem(2, ROWS, *PLANE),
            vmem(2, CHIPS, *PLANE),
            vmem(2, *PLANE),
            *[DMA((2, CHIPS))] * 2,
            DMA((2,)),
            DMA((2,)),
        ],
        compiler_params=pltpu.CompilerParams(
            collective_id=0, has_side_effects=True, vmem_limit_bytes=LIMIT
        ),
        name="whole",
    )(
        activations, spectral_weight, pointwise, readout.reshape(1, C), forcing, line_forward,
        line_back, phases, sum_table, back_table, *physics_parts,
    )


def solution(mesh):
    return jax.shard_map(
        shards,
        mesh=mesh,
        in_specs=(
            P("tm", "rows", None, None),
            P(("rows", "tm"), None, None, None),
            P(),
            P(),
            P("rows", None),
        ),
        out_specs=(P("tm", "rows", None, None), P(("rows", "tm"), None, None, None)),
        check_vma=False,
    )
```

```python
import math

import jax
import jax.numpy as jnp
import ml_dtypes
import numpy as np
from jax import lax
from jax.experimental import pallas as pl
from jax.experimental.pallas import tpu as pltpu
from jax.sharding import PartitionSpec as P

MESH = pl.DeviceIdType.MESH
VISCOSITY = 0.002
LOSS_WEIGHT = 0.005
C, K, NY, NX, NT = 64, 16, 512, 256, 64
ROWS, TM = 16, 8
CHIPS = ROWS // 2
STEPS, CELLS = NT // TM, NX // ROWS
HALF = NY // 2
GROUP, LANES = 4, 128
MIDDLE = (CELLS - 1) / 2
S_GRID = 1.0 / math.sqrt(NT * NX * NY)
S_MODE = 1.0 / math.sqrt(K * K * K)
TWO_PI = 2.0 * math.pi
BF16 = jnp.bfloat16
F32 = jnp.float32


def halves(table):
    table = table.astype(np.float32)
    high = table.astype(ml_dtypes.bfloat16)
    low = (table - high.astype(np.float32)).astype(ml_dtypes.bfloat16)
    return high, low


def line_tables():
    numbers = np.arange(K) - K // 2
    angles = (TWO_PI / NY) * (np.outer(numbers, np.arange(NY)) % NY)
    table = np.concatenate([np.cos(angles), -np.sin(angles)], axis=0).astype(np.float32)
    forward = np.zeros((GROUP, NY, LANES), ml_dtypes.bfloat16)
    back = np.zeros((GROUP, LANES, NY), ml_dtypes.bfloat16)
    high, low = halves(table)
    for t in range(GROUP):
        forward[t, :, 2 * K * t : 2 * K * (t + 1)] = table.astype(ml_dtypes.bfloat16).T
        for place, part in enumerate((high, high, low)):
            first = 2 * K * ((t + place) % GROUP)
            back[t, first : first + 2 * K] = part
    return forward, back


def time_tables():
    numbers = np.arange(K) - K // 2
    steps = np.arange(NT).reshape(TM, STEPS)
    angles = (TWO_PI / NT) * ((numbers[None, :, None] * steps[:, None, :]) % NT)
    unit = np.eye(K)

    def spread(real, imag):
        both = np.stack([real, imag], axis=3)
        return np.einsum("matr,ef->maetrf", both, unit).reshape(TM, K * K, STEPS * 2 * K)

    cos_part, sin_part = np.cos(angles), np.sin(angles)
    forward = spread(cos_part, sin_part)
    back = np.concatenate([spread(cos_part, sin_part), spread(-sin_part, cos_part)], axis=1)
    return forward.astype(np.float32), back.astype(np.float32)


def row_phases():
    numbers = np.arange(K) - K // 2
    angles = (TWO_PI / NX) * np.outer(CELLS * np.arange(ROWS) + MIDDLE, numbers)
    return np.stack([np.cos(angles), np.sin(angles)]).astype(np.float32)


def physics_tables():
    y = np.arange(NY)
    ky = np.arange(HALF)
    angles = (TWO_PI / NY) * (np.outer(y, ky) % NY)
    row_forward = np.concatenate([np.cos(angles), -np.sin(angles)], axis=1)
    scaling = np.where(ky == 0, 1.0, 2.0)[:, None] / NY
    row_back = np.concatenate([scaling * np.cos(angles).T, -scaling * np.sin(angles).T], axis=0)
    gap = np.arange(NY)
    gap_angles = (TWO_PI / NY) * (np.outer(gap, ky) % NY)
    slope = -(2.0 / NY) * (np.sin(gap_angles) * ky).sum(1)
    bend = -(2.0 / NY) * (np.cos(gap_angles) * ky * ky).sum(1)
    turn = (y[None, :] - y[:, None]) % NY
    row_slope, row_bend = slope[turn], bend[turn]
    x = np.arange(NX)
    kx = np.where(x < NX // 2, x, x - NX)
    dx = np.where(x == NX // 2, 0, kx)
    col_angles = (TWO_PI / NX) * (np.outer(x, x) % NX)
    col_slope = -(np.sin(col_angles) * dx).sum(1) / NX
    col_bend = -(np.cos(col_angles) * kx * kx).sum(1) / NX
    col_turn = (x[:, None] - x[None, :]) % NX
    col_slope, col_bend = col_slope[col_turn], col_bend[col_turn]
    col_wave = np.concatenate([np.cos(col_angles), np.sin(col_angles)], axis=0)
    squared = (kx[:, None] ** 2 + ky[None, :] ** 2).astype(np.float64)
    inverse = np.where(squared > 0, 1.0 / np.where(squared > 0, squared, 1.0), 0.0) / NX
    inverse = np.concatenate([inverse, inverse], axis=1).astype(np.float32)
    pairs = [
        halves(t)
        for t in (
            row_forward,
            row_back,
            row_slope,
            VISCOSITY * row_bend,
            col_wave,
            col_slope,
            VISCOSITY * col_bend,
        )
    ]
    return [t for pair in pairs for t in pair] + [inverse]


def turned_halves(z):
    moved = pltpu.roll(z, C, 1)
    low = lax.broadcasted_iota(jnp.int32, z.shape, 1) < C
    return jnp.where(low, moved, -moved)


def turned(z):
    real = lax.broadcasted_iota(jnp.int32, z.shape, 1) % (2 * K) < K
    return jnp.where(real, pltpu.roll(z, LANES - K, 1), -pltpu.roll(z, K, 1))


def loop(first, last, body, unroll=1):
    def step(j, carry):
        body(j)
        return carry

    lax.fori_loop(first, last, step, 0, unroll=unroll)


def project_rows(lines, phase_ref, store):
    row = lax.axis_index("rows")

    def part(chunk):
        rows = pl.ds(pl.multiple_of(8 * chunk, 8), 8)
        far = range(CELLS // 2, CELLS)
        pairs = [(lines[x, rows, :], lines[CELLS - 1 - x, rows, :]) for x in far]
        added = [right + left for right, left in pairs]
        taken = [turned(right - left) for right, left in pairs]
        for k in range(K // 2 + 1):
            even, odd = None, None
            for x, both, gap in zip(far, added, taken):
                angle = TWO_PI * k * (x - MIDDLE) / NX
                cos_term = both if k == 0 else math.cos(angle) * both
                even = cos_term if even is None else even + cos_term
                if k:
                    sin_term = math.sin(angle) * gap
                    odd = sin_term if odd is None else odd + sin_term
            found = []
            if k < K // 2:
                found.append((K // 2 + k, even if odd is None else even + odd))
            if k > 0:
                found.append((K // 2 - k, even - odd))
            for b, value in found:
                cos_b, sin_b = phase_ref[0, row, b], phase_ref[1, row, b]
                store(b, rows, cos_b * value + sin_b * turned(value))

    loop(0, C // 8, part)


def spread_rows(modes, phase_ref, spread):
    row = lax.axis_index("rows")

    def part(chunk):
        rows = pl.ds(pl.multiple_of(8 * chunk, 8), 8)
        z = []
        for b in range(K):
            cos_b, sin_b = phase_ref[0, row, b], phase_ref[1, row, b]
            value = modes(b, rows)
            z.append(cos_b * value - sin_b * turned(value))
        even, odd = [z[K // 2]], [None]
        for k in range(1, K // 2):
            even.append(z[K // 2 + k] + z[K // 2 - k])
            odd.append(turned(z[K // 2 - k] - z[K // 2 + k]))
        even.append(z[0])
        odd.append(turned(z[0]))
        for x in range(CELLS // 2, CELLS):
            same, changed = even[0], None
            for k in range(1, K // 2 + 1):
                angle = TWO_PI * k * (x - MIDDLE) / NX
                same = same + math.cos(angle) * even[k]
                term = math.sin(angle) * odd[k]
                changed = term if changed is None else changed + term
            spread[x, rows, :] = same + changed
            spread[CELLS - 1 - x, rows, :] = same - changed

    loop(0, C // 8, part)


def fill_block(block, matrix):
    block[...] = jnp.zeros_like(block)
    for x in range(GROUP):
        block[C * x : C * (x + 1), C * x : C * (x + 1)] = matrix


def spread_part(spread, back, t):
    total = spread.reshape(GROUP * C, LANES)
    high = total.astype(BF16).astype(F32)
    lane = lax.broadcasted_iota(jnp.int32, total.shape, 1) // (2 * K)
    left = jnp.where(
        lane == t,
        high,
        jnp.where(
            lane == (t + 1) % GROUP,
            pltpu.roll(total - high, 2 * K, 1),
            pltpu.roll(high, 4 * K, 1),
        ),
    ).astype(BF16)
    return jnp.dot(left, back, preferred_element_type=F32)


def physics(planes, step, tables, between, wait_rate, send_weighted, send_grad):
    (rf, rf_low, rb, rb_low, rs, rs_low, rc, rc_low, cw, cw_low, cs, cs_low, cc, cc_low, inverse) = (
        tables
    )

    def parts(value):
        high = value.astype(BF16)
        return high, (value - high.astype(F32)).astype(BF16)

    def dot(a, b):
        return jnp.dot(a, b, preferred_element_type=F32)

    def along(value, high, low):
        v_high, v_low = parts(value)
        return dot(v_high, high[...]) + (dot(v_low, high[...]) + dot(v_high, low[...]))

    def across(high, low, value):
        v_high, v_low = parts(value)
        return dot(high[...], v_high) + (dot(high[...], v_low) + dot(low[...], v_high))

    def minus_i(z):
        return jnp.concatenate([z[:, HALF:], -z[:, :HALF]], axis=1)

    def solve(value):
        spectrum = along(value, rf, rf_low)
        both = across(cw, cw_low, spectrum)
        spectrum = (both[:NX] + minus_i(both[NX:])) * inverse[...]
        both = across(cw, cw_low, spectrum)
        return along(both[:NX] - minus_i(both[NX:]), rb, rb_low)

    sign = jnp.where(lax.broadcasted_iota(jnp.int32, (NX, NY), 1) % 2 == 0, 1.0, -1.0).astype(F32)

    def smooth(value):
        return value - sign * (jnp.sum(value * sign, axis=1, keepdims=True) * (1.0 / NY))

    inside = (step > 0) & (step < NT - 1)
    vort = planes[0].reshape(NX, NY)
    stream = solve(vort)
    between()
    slopes = along(jnp.concatenate([vort, stream], axis=0), rs, rs_low)
    slope_right, flow_down = slopes[:NX], slopes[NX:]
    smoothed = smooth(vort)
    slopes = across(cs, cs_low, jnp.concatenate([smoothed, stream], axis=1))
    slope_down, flow_right = slopes[:, :NY], -slopes[:, NY:]
    bend = along(vort, rc, rc_low) + across(cc, cc_low, smoothed)
    wait_rate()
    rate = planes[1].reshape(NX, NY)
    residual = (
        rate
        + flow_down * slope_down
        + flow_right * slope_right
        - bend
    )
    weighted = jnp.where(inside, LOSS_WEIGHT * residual, 0.0)
    send_weighted(weighted)
    first = weighted * slope_down
    second = weighted * slope_right
    slopes = along(jnp.concatenate([first, flow_right * weighted], axis=0), rs, rs_low)
    first_along, flow_along = slopes[:NX], slopes[NX:]
    slopes = across(
        cs, cs_low, jnp.concatenate([second, smooth(flow_down * weighted)], axis=1)
    )
    second_across, flow_across = slopes[:, :NY], slopes[:, NY:]
    solved = solve(second_across - first_along)
    bend = along(weighted, rc, rc_low) + across(cc, cc_low, smooth(weighted))
    grad = solved - bend - flow_across - flow_along
    send_grad(grad)


def remote(src, dst, send, recv, device):
    return pltpu.make_async_remote_copy(
        src_ref=src, dst_ref=dst, send_sem=send, recv_sem=recv, device_id=device,
        device_id_type=MESH,
    )


def place():
    row, slab = lax.axis_index("rows"), lax.axis_index("tm")
    return row, slab, row // 2, row % 2


def greet():
    row, slab, chip, core = place()
    barrier = pltpu.get_barrier_semaphore()
    pl.semaphore_signal(
        barrier, inc=1, device_id=(row + 1 - 2 * core, slab), device_id_type=MESH
    )

    def tell(j):
        peer = 2 * ((chip + j) % CHIPS) + core
        pl.semaphore_signal(barrier, inc=1, device_id=(peer, slab), device_id_type=MESH)
        pl.semaphore_signal(
            barrier, inc=1, device_id=(row, (slab + j) % TM), device_id_type=MESH
        )

    loop(1, CHIPS, tell)


def all_here():
    pl.semaphore_wait(pltpu.get_barrier_semaphore(), 1 + (CHIPS - 1) + (TM - 1))


class Modes:
    def __init__(self, w_hbm, sum_hbm, back_hbm, scratch):
        (
            self.weight, self.sum_table, self.back_table, self.terms, self.from_core,
            self.from_rows, self.parts, self.from_slabs, self.mixed, self.slabs, self.gathered,
            self.load, self.core_send, self.core_recv, self.row_send, self.row_recv,
            self.slab_send, self.slab_recv, self.mix_send, self.mix_recv, self.out_send,
            self.out_recv, self.pass_send, self.pass_recv,
        ) = scratch
        self.row, self.slab, self.chip, self.core = place()
        self.other = (self.row + 1 - 2 * self.core, self.slab)
        self.loads = [
            pltpu.make_async_copy(src, dst, self.load.at[i])
            for i, (src, dst) in enumerate(
                (
                    (sum_hbm.at[self.slab], self.sum_table),
                    (w_hbm, self.weight),
                    (back_hbm.at[self.slab], self.back_table),
                )
            )
        ]

    def start_loads(self):
        for load in self.loads:
            load.start()

    def store(self, group):
        def put(b, rows, value):
            self.terms[b % 2, b // 2, group, rows, :] = value

        return put

    def core_copy(self, group, j):
        to = (self.chip + j) % CHIPS
        return remote(
            self.terms.at[1 - self.core, to, group], self.from_core.at[to, group],
            self.core_send.at[to, group], self.core_recv.at[to, group], self.other,
        )

    def row_copy(self, group, j):
        to = (self.chip + j) % CHIPS
        return remote(
            self.from_core.at[to, group], self.from_rows.at[self.chip, group],
            self.row_send.at[to, group], self.row_recv.at[self.chip, group],
            (2 * to + self.core, self.slab),
        )

    def start_core(self, group):
        loop(1, CHIPS + 1, lambda j: self.core_copy(group, j).start())

    def forward(self, group):
        def step(j):
            to = (self.chip + j) % CHIPS
            self.core_copy(group, j).wait_recv()
            self.from_core[to, group] = (
                self.from_core[to, group] + self.terms[self.core, to, group]
            )
            self.row_copy(group, j).start()

        loop(1, CHIPS, step)
        self.core_copy(group, CHIPS).wait_recv()
        self.from_rows[self.chip, group] = (
            self.from_core[self.chip, group] + self.terms[self.core, self.chip, group]
        )

    def arrivals(self, group):
        def step(j):
            source = (self.chip + CHIPS - j) % CHIPS
            remote(
                self.from_core.at[source, group], self.from_rows.at[source, group],
                self.row_send.at[source, group], self.row_recv.at[source, group],
                (2 * source + self.core, self.slab),
            ).wait_recv()

        loop(1, CHIPS, step)
        total = self.from_rows[0, group]
        for source in range(1, CHIPS):
            total = total + self.from_rows[source, group]
        return total

    def slab_copy(self, j):
        to = (self.slab + j) % TM
        return remote(
            self.parts.at[to], self.from_slabs.at[self.slab], self.slab_send.at[to],
            self.slab_recv.at[self.slab], (self.row, to),
        )

    def mix_copy(self, j):
        to = (self.slab + j) % TM
        return remote(
            self.mixed, self.slabs.at[self.slab], self.mix_send.at[to],
            self.mix_recv.at[self.slab], (self.row, to),
        )

    def exchange_slabs(self, gradient, coef_ref, first, second):
        totals = [self.arrivals(group) for group in range(2)]
        both = jnp.concatenate(
            [
                jnp.concatenate(totals, axis=1),
                jnp.concatenate([turned(total) for total in totals], axis=1),
            ],
            axis=0,
        )
        if not gradient:
            self.loads[0].wait()
        found = lax.dot_general(
            self.sum_table[...], both, (((1,), (1,)), ((), ())),
            precision=lax.Precision.HIGHEST, preferred_element_type=F32,
        )
        self.parts[...] = (found * (S_MODE if gradient else S_GRID)).reshape(
            TM, 2 * K, 2 * C
        )
        loop(1, TM, lambda j: self.slab_copy(j).start())
        self.from_slabs[self.slab] = self.parts[self.slab]
        first()
        if not gradient:
            self.loads[1].wait()

        def slab_arrival(j):
            source = (self.slab + TM - j) % TM
            remote(
                self.parts.at[source], self.from_slabs.at[source], self.slab_send.at[source],
                self.slab_recv.at[source], (self.row, source),
            ).wait_recv()

        loop(1, TM, slab_arrival)
        coef = self.from_slabs[0]
        for source in range(1, TM):
            coef = coef + self.from_slabs[source]
        coef_ref[...] = coef
        if gradient:
            self.mix_back(coef)
        else:
            self.mix(coef)
        loop(1, TM, lambda j: self.mix_copy(j).start())
        self.slabs[self.slab] = self.mixed[...]
        second()

        def mix_arrival(j):
            source = (self.slab + TM - j) % TM
            remote(
                self.mixed, self.slabs.at[source], self.mix_send.at[source],
                self.mix_recv.at[source], (self.row, source),
            ).wait_recv()

        loop(1, TM, mix_arrival)
        if not gradient:
            self.loads[2].wait()
        whole = jnp.transpose(self.slabs[...].reshape(K * K, 2 * C))
        spread = (S_GRID if gradient else S_MODE) * jnp.dot(
            jnp.concatenate([whole[:C], whole[C:]], axis=1), self.back_table[...],
            precision=lax.Precision.HIGHEST, preferred_element_type=F32,
        )
        self.gathered[0, self.row] = spread[:, :LANES]
        self.gathered[1, self.row] = spread[:, LANES:]
        for group in range(2):
            loop(1, CHIPS, lambda j: self.out_copy(group, j).start())
            self.pass_copy(group, self.chip).start()

    def mix(self, coef):
        columns = jnp.transpose(
            jnp.concatenate([coef, jnp.zeros((2 * C - 2 * K, 2 * C), F32)], axis=0)
        )
        for j in range(2 * K):
            weight = self.weight[j // K, j % K]
            re = jnp.sum(weight * columns[:C, j : j + 1], axis=0, keepdims=True)
            im = jnp.sum(weight * columns[C:, j : j + 1], axis=0, keepdims=True)
            self.mixed[j : j + 1, :] = re - turned_halves(im)

    def mix_back(self, coef):
        turned_coef = turned_halves(coef)
        lane = lax.broadcasted_iota(jnp.int32, (C, 2 * C), 1)
        real = jnp.zeros((C, 2 * C), F32)
        imag = jnp.zeros((C, 2 * C), F32)
        for j in range(2 * K):
            weight = self.weight[j // K, j % K]
            re = jnp.sum(weight * coef[j : j + 1, :], axis=1, keepdims=True)
            im = jnp.sum(weight * turned_coef[j : j + 1, :], axis=1, keepdims=True)
            real = jnp.where(lane == j, re, real)
            imag = jnp.where(lane == j, im, imag)
        self.mixed[...] = jnp.transpose(jnp.concatenate([real, imag], axis=0))[: 2 * K]

    def out_copy(self, group, j):
        to = (self.chip + j) % CHIPS
        block = self.gathered.at[group, self.row]
        return remote(
            block, block, self.out_send.at[to, group], self.out_recv.at[self.chip, group],
            (2 * to + self.core, self.slab),
        )

    def pass_copy(self, group, source):
        block = self.gathered.at[group, 2 * source + self.core]
        return remote(
            block, block, self.pass_send.at[source, group], self.pass_recv.at[source, group],
            self.other,
        )

    def pass_on(self, group):
        def step(j):
            source = (self.chip + CHIPS - j) % CHIPS
            block = self.gathered.at[group, 2 * source + self.core]
            remote(
                block, block, self.out_send.at[source, group], self.out_recv.at[source, group],
                (2 * source + self.core, self.slab),
            ).wait_recv()
            self.pass_copy(group, source).start()

        loop(1, CHIPS, step)

    def gather_done(self, group):
        def step(source):
            block = self.gathered.at[group, 2 * source + 1 - self.core]
            remote(
                block, block, self.pass_send.at[source, group], self.pass_recv.at[source, group],
                self.other,
            ).wait_recv()

        loop(0, CHIPS, step)

    def wait_sums(self):
        loop(1, TM, lambda j: self.slab_copy(j).wait_send())
        loop(1, TM, lambda j: self.mix_copy(j).wait_send())
        for group in range(2):
            loop(1, CHIPS + 1, lambda j: self.core_copy(group, j).wait_send())
            loop(1, CHIPS, lambda j: self.row_copy(group, j).wait_send())

    def wait_gathers(self):
        for group in range(2):
            loop(1, CHIPS, lambda j: self.out_copy(group, j).wait_send())
            loop(0, CHIPS, lambda j: self.pass_copy(group, j).wait_send())


class Planes:
    def __init__(self, forcing_ref, scratch):
        (
            self.vort, self.rates, self.halo, self.planes, self.halo_send, self.halo_recv,
            self.send, self.recv, self.pass_send, self.pass_recv,
        ) = scratch
        self.forcing = forcing_ref
        self.row, self.slab, self.chip, self.core = place()
        self.other = (self.row + 1 - 2 * self.core, self.slab)
        after, before = (self.slab + 1) % TM, (self.slab + TM - 1) % TM
        self.to_after = remote(
            self.vort.at[STEPS - 1], self.halo.at[0], self.halo_send.at[0], self.halo_recv.at[0],
            (self.row, after),
        )
        self.to_before = remote(
            self.vort.at[0], self.halo.at[1], self.halo_send.at[1], self.halo_recv.at[1],
            (self.row, before),
        )

    def copy(self, field, to):
        source = (self.vort, self.rates)[field].at[to]
        return remote(
            source, self.planes.at[field, self.row], self.send.at[field, to],
            self.recv.at[field, self.chip], (2 * to + self.core, self.slab),
        )

    def pass_copy(self, field, source):
        block = self.planes.at[field, 2 * source + self.core]
        return remote(
            block, block, self.pass_send.at[field, source], self.pass_recv.at[field, source],
            self.other,
        )

    def send_step(self, field, to):
        @pl.when(to != self.chip)
        def _():
            self.copy(field, to).start()

        @pl.when(to == self.chip)
        def _():
            self.planes[field, self.row] = (self.vort, self.rates)[field][to]
            self.pass_copy(field, self.chip).start()

    def rate(self, step, low, high):
        self.rates[step] = (0.5 * NT) * (high - low) - self.forcing[...]

    def inner_rates(self, first, last):
        for step in range(first, last):
            self.rate(step, self.vort[step - 1], self.vort[step + 1])
            self.send_step(1, step)

    def arrivals(self, field):
        def step(j):
            source = (self.chip + CHIPS - j) % CHIPS
            block = 2 * source + self.core
            remote(
                self.vort.at[source], self.planes.at[field, block], self.send.at[field, source],
                self.recv.at[field, source], (block, self.slab),
            ).wait_recv()
            self.pass_copy(field, source).start()

        loop(1, CHIPS, step)

    def pass_arrivals(self, field):
        def step(source):
            block = self.planes.at[field, 2 * source + 1 - self.core]
            remote(
                block, block, self.pass_send.at[field, source], self.pass_recv.at[field, source],
                self.other,
            ).wait_recv()

        loop(0, CHIPS, step)

    def wait_sends(self):
        self.to_after.wait_send()
        self.to_before.wait_send()
        for field in range(2):
            loop(1, CHIPS, lambda j: self.copy(field, (self.chip + j) % CHIPS).wait_send())
            loop(0, CHIPS, lambda j: self.pass_copy(field, j).wait_send())


class Returns:
    def __init__(self, scratch):
        (
            self.source, self.steps, self.halo, self.send, self.recv, self.halo_send,
            self.halo_recv,
        ) = scratch
        self.row, self.slab, self.chip, self.core = place()
        after, before = (self.slab + 1) % TM, (self.slab + TM - 1) % TM
        self.to_after = remote(
            self.steps.at[1, STEPS - 1], self.halo.at[0], self.halo_send.at[0],
            self.halo_recv.at[0], (self.row, after),
        )
        self.to_before = remote(
            self.steps.at[1, 0], self.halo.at[1], self.halo_send.at[1], self.halo_recv.at[1],
            (self.row, before),
        )

    def copy(self, field, j):
        to = (self.chip + j) % CHIPS
        block = 2 * to + self.core
        return remote(
            self.source.at[field, block], self.steps.at[field, self.chip],
            self.send.at[field, to], self.recv.at[field, self.chip], (block, self.slab),
        )

    def start(self, field, value):
        self.source[field] = value.reshape(ROWS, CELLS, NY)
        loop(1, CHIPS, lambda j: self.copy(field, j).start())
        self.steps[field, self.chip] = self.source[field, self.row]

    def arrivals(self, field):
        def step(j):
            source = (self.chip + CHIPS - j) % CHIPS
            block = 2 * source + self.core
            remote(
                self.source.at[field, block], self.steps.at[field, source],
                self.send.at[field, source], self.recv.at[field, source], (block, self.slab),
            ).wait_recv()

        loop(1, CHIPS, step)

    def finish(self, grads):
        self.arrivals(1)
        self.to_after.start()
        self.to_before.start()
        self.arrivals(0)

        def grad(step, low, high):
            grads[step] = self.steps[0, step] + (0.5 * NT) * (low - high)

        for step in range(1, STEPS - 1):
            grad(step, self.steps[1, step - 1], self.steps[1, step + 1])
        self.to_after.wait_recv()
        grad(0, self.halo[0], self.steps[1, 1])
        self.to_before.wait_recv()
        grad(STEPS - 1, self.steps[1, STEPS - 2], self.halo[1])

    def wait_sends(self):
        self.to_after.wait_send()
        self.to_before.wait_send()
        for field in range(2):
            loop(1, CHIPS, lambda j: self.copy(field, j).wait_send())


def whole_kernel(
    act_hbm, w_hbm, matrix_ref, readout_ref, forcing_ref, forward_ref, back_ref, phase_ref,
    sum_hbm, back_hbm, *rest,
):
    table_hbm, rest = rest[:PHYSICS], rest[PHYSICS:]
    act, mode_ref, lines, block, wide, fields, grads, coef, grad_mixed = rest[:9]
    act_load, table_load = rest[9:11]
    rest = rest[11:]
    tables, rest = rest[:PHYSICS], rest[PHYSICS:]
    modes = Modes(w_hbm, sum_hbm, back_hbm, rest[:MODE_SCRATCH])
    planes = Planes(forcing_ref, rest[MODE_SCRATCH : MODE_SCRATCH + PLANE_SCRATCH])
    returns = Returns(rest[MODE_SCRATCH + PLANE_SCRATCH :])

    def load(t):
        return pltpu.make_async_copy(act_hbm.at[t], act.at[t], act_load.at[t])

    table_loads = [
        pltpu.make_async_copy(src, dst, table_load.at[i])
        for i, (src, dst) in enumerate(zip(table_hbm, tables))
    ]
    greet()
    for t in range(STEPS):
        load(t).start()
    modes.start_loads()
    for copy in table_loads:
        copy.start()
    same = lax.broadcasted_iota(jnp.int32, (C, C), 0) == lax.broadcasted_iota(
        jnp.int32, (C, C), 1
    )
    unit = jnp.where(same, 1.0, 0.0).astype(BF16)
    fill_block(
        block,
        lax.dot_general(
            matrix_ref[...], unit, (((0,), (0,)), ((), ())), preferred_element_type=F32
        ).astype(BF16),
    )
    wide[...] = 0.5 * jnp.broadcast_to(
        jnp.sum(jnp.where(same, readout_ref[...], 0.0), axis=1, keepdims=True), (C, LANES)
    )

    def make_lines(group, prepare):
        def part(chunk):
            rows = pl.ds(GROUP * chunk, GROUP)
            total = None
            for inner in range(GROUP):
                t = GROUP * group + inner
                prepare(t, chunk, rows)
                term = jnp.dot(
                    act[t, rows].reshape(GROUP * C, NY), forward_ref[inner],
                    preferred_element_type=F32,
                )
                total = term if total is None else total + term
            lines[rows] = total.reshape(GROUP, C, LANES)

        loop(0, GROUP, part)

    def analyze(prepare, before, ready):
        before(0)
        make_lines(0, prepare)
        project_rows(lines, phase_ref, modes.store(0))
        ready()
        modes.start_core(0)
        before(1)
        make_lines(1, prepare)
        modes.forward(0)
        project_rows(lines, phase_ref, modes.store(1))
        modes.start_core(1)
        modes.forward(1)

    def local(quarter):
        def part(i):
            t, rows = 2 * quarter + i % 2, pl.ds(GROUP * (i // 2), GROUP)
            fields[t, rows] = jnp.dot(
                block[...], act[t, rows].reshape(GROUP * C, NY), preferred_element_type=F32
            ).reshape(GROUP, C, NY)

        loop(0, 2 * GROUP, part, unroll=UNROLL)

    def wait_load(group):
        for t in range(GROUP):
            load(GROUP * group + t).wait()

    analyze(lambda t, chunk, rows: None, wait_load, all_here)
    local(0)
    modes.exchange_slabs(False, coef, lambda: local(1), lambda: local(2))
    local(3)
    modes.wait_sums()

    c0 = math.sqrt(2.0 / math.pi)
    c1 = c0 * 0.044715

    def hide(group):
        def part(inner, chunk):
            t = GROUP * group + inner
            found = spread_part(lines[pl.ds(GROUP * chunk, GROUP)], back_ref[inner], inner)
            for x in range(GROUP):
                total = None
                for part_of in range(C // 16):
                    own = slice(16 * part_of, 16 * part_of + 16)
                    readout = jnp.concatenate([wide[own]] * (NY // LANES), axis=1)
                    place_of = C * x + 16 * part_of
                    value = found[place_of : place_of + 16] + fields[t, GROUP * chunk + x, own, :]
                    square = value * value
                    bend = jnp.tanh(value * (c0 + c1 * square))
                    scaled = readout * (1.0 + bend)
                    steep = (1.0 - bend) * (value * (c0 + 3.0 * c1 * square))
                    fields[t, GROUP * chunk + x, own, :] = scaled + scaled * steep
                    term = scaled * value
                    term = term[:8] + term[8:]
                    total = term if total is None else total + term
                planes.vort[t, pl.ds(GROUP * chunk + x, 1), :] = jnp.sum(
                    total, axis=0, keepdims=True
                )

        def step(inner):
            loop(0, GROUP, lambda chunk: part(inner, chunk), unroll=UNROLL)
            planes.send_step(0, GROUP * group + inner)

        loop(0, GROUP, step)

    def spread(group):
        spread_rows(lambda b, rows: modes.gathered[group, b, rows, :], phase_ref, lines)

    modes.pass_on(0)
    modes.gather_done(0)
    spread(0)
    modes.pass_on(1)
    hide(0)
    planes.to_before.start()
    planes.inner_rates(1, GROUP - 1)
    modes.gather_done(1)
    spread(1)
    hide(1)
    planes.to_after.start()
    planes.inner_rates(GROUP - 1, STEPS - 1)
    modes.wait_gathers()
    planes.to_after.wait_recv()
    planes.rate(0, planes.halo[0], planes.vort[1])
    planes.send_step(1, 0)
    planes.to_before.wait_recv()
    planes.rate(STEPS - 1, planes.vort[STEPS - 2], planes.halo[1])
    planes.send_step(1, STEPS - 1)
    planes.arrivals(0)
    fill_block(block, matrix_ref[...])
    for copy in table_loads:
        copy.wait()
    planes.pass_arrivals(0)

    physics(
        planes.planes, modes.slab * STEPS + modes.chip, tables,
        lambda: planes.arrivals(1), lambda: planes.pass_arrivals(1),
        lambda value: returns.start(1, value), lambda value: returns.start(0, value),
    )
    returns.finish(grads)

    def prepare(t, chunk, rows):
        for x in range(GROUP):
            weight = grads[t, pl.ds(GROUP * chunk + x, 1), :]
            act[t, GROUP * chunk + x] = (fields[t, GROUP * chunk + x] * weight).astype(BF16)

    analyze(prepare, lambda group: None, lambda: None)

    def mode_grads():
        lane = lax.broadcasted_iota(jnp.int32, (C, 2 * C), 1)
        first = lax.broadcasted_iota(jnp.int32, (C, 2 * C), 0)
        for j in range(2 * K):
            own, grad = coef[j : j + 1, :], grad_mixed[j : j + 1, :]
            real = jnp.sum(jnp.where(lane == first, own, 0.0), axis=1, keepdims=True)
            imag = jnp.sum(jnp.where(lane == first + C, own, 0.0), axis=1, keepdims=True)
            mode_ref[j // K, j % K] = real * grad + imag * turned_halves(grad)

    def second():
        local(2)
        mode_grads()
        planes.wait_sends()
        returns.wait_sends()

    local(0)
    modes.exchange_slabs(True, grad_mixed, lambda: local(1), second)
    local(3)
    modes.wait_sums()

    def put_out(group):
        def part(i):
            inner, chunk = i % GROUP, i // GROUP
            t, rows = GROUP * group + inner, pl.ds(GROUP * chunk, GROUP)
            found = spread_part(lines[rows], back_ref[inner], inner).reshape(GROUP, C, NY)
            act[t, rows] = (found + fields[t, rows]).astype(BF16)

        loop(0, GROUP * GROUP, part, unroll=UNROLL)

    modes.pass_on(0)
    modes.gather_done(0)
    spread(0)
    modes.pass_on(1)
    put_out(0)
    modes.gather_done(1)
    spread(1)
    put_out(1)
    modes.wait_gathers()


VMEM = pl.BlockSpec(memory_space=pltpu.VMEM)
SMEM = pl.BlockSpec(memory_space=pltpu.SMEM)
ANY = pl.BlockSpec(memory_space=pl.ANY)
DMA = pltpu.SemaphoreType.DMA
LIMIT = 46 * 1024 * 1024
UNROLL = 4

FIELD = (CELLS, C, NY)
PLANE = (CELLS, NY)
PART = (C, LANES)
PAIR = (2 * K, 2 * C)


def vmem(*shape, dtype=F32):
    return pltpu.VMEM(shape, dtype)


MODE_SCRATCH, PLANE_SCRATCH, PHYSICS = 24, 10, 15


def mode_scratch():
    return [
        vmem(2, K, C, 2 * C),
        vmem(K * K, 2 * LANES),
        vmem(2 * K * K, 2 * LANES),
        vmem(2, CHIPS, 2, *PART),
        vmem(CHIPS, 2, *PART),
        vmem(CHIPS, 2, *PART),
        vmem(TM, *PAIR),
        vmem(TM, *PAIR),
        vmem(*PAIR),
        vmem(TM, *PAIR),
        vmem(2, K, *PART),
        DMA((3,)),
        *[DMA((CHIPS, 2))] * 4,
        *[DMA((TM,))] * 4,
        *[DMA((CHIPS, 2))] * 4,
    ]


def shards(activations, spectral_weight, pointwise, readout, forcing):
    line_forward, line_back = (jnp.asarray(t) for t in line_tables())
    phases = jnp.asarray(row_phases())
    sum_table, back_table = (jnp.asarray(t) for t in time_tables())
    physics_parts = [jnp.asarray(t) for t in physics_tables()]
    return pl.pallas_call(
        whole_kernel,
        out_shape=(
            pltpu.VMEM((STEPS,) + FIELD, BF16),
            pltpu.VMEM((2, K, C, 2 * C), F32),
        ),
        in_specs=[ANY, ANY, VMEM, VMEM, VMEM, VMEM, VMEM, SMEM, ANY, ANY] + [ANY] * PHYSICS,
        out_specs=(VMEM, VMEM),
        scratch_shapes=[
            vmem(CELLS, *PART),
            vmem(GROUP * C, GROUP * C, dtype=BF16),
            vmem(C, LANES),
            vmem(STEPS, *FIELD),
            vmem(STEPS, *PLANE),
            vmem(*PAIR),
            vmem(*PAIR),
            DMA((STEPS,)),
            DMA((PHYSICS,)),
            *[vmem(*t.shape, dtype=t.dtype) for t in physics_parts],
            *mode_scratch(),
            vmem(STEPS, *PLANE),
            vmem(STEPS, *PLANE),
            vmem(2, *PLANE),
            vmem(2, ROWS, *PLANE),
            DMA((2,)),
            DMA((2,)),
            *[DMA((2, CHIPS))] * 4,
            vmem(2, ROWS, *PLANE),
            vmem(2, CHIPS, *PLANE),
            vmem(2, *PLANE),
            *[DMA((2, CHIPS))] * 2,
            DMA((2,)),
            DMA((2,)),
        ],
        compiler_params=pltpu.CompilerParams(
            collective_id=0, has_side_effects=True, vmem_limit_bytes=LIMIT
        ),
        name="whole",
    )(
        activations, spectral_weight, pointwise, readout.reshape(1, C), forcing, line_forward,
        line_back, phases, sum_table, back_table, *physics_parts,
    )


def solution(mesh):
    return jax.shard_map(
        shards,
        mesh=mesh,
        in_specs=(
            P("tm", "rows", None, None),
            P(("rows", "tm"), None, None, None),
            P(),
            P(),
            P("rows", None),
        ),
        out_specs=(P("tm", "rows", None, None), P(("rows", "tm"), None, None, None)),
        check_vma=False,
    )
```

```python
import math

import jax
import jax.numpy as jnp
import ml_dtypes
import numpy as np
from jax import lax
from jax.experimental import pallas as pl
from jax.experimental.pallas import tpu as pltpu
from jax.sharding import PartitionSpec as P

MESH = pl.DeviceIdType.MESH
VISCOSITY = 0.002
LOSS_WEIGHT = 0.005
C, K, NY, NX, NT = 64, 16, 512, 256, 64
ROWS, TM = 16, 8
CHIPS = ROWS // 2
STEPS, CELLS = NT // TM, NX // ROWS
HALF = NY // 2
GROUP, LANES = 4, 128
MIDDLE = (CELLS - 1) / 2
S_GRID = 1.0 / math.sqrt(NT * NX * NY)
S_MODE = 1.0 / math.sqrt(K * K * K)
TWO_PI = 2.0 * math.pi
BF16 = jnp.bfloat16
F32 = jnp.float32


def halves(table):
    table = table.astype(np.float32)
    high = table.astype(ml_dtypes.bfloat16)
    low = (table - high.astype(np.float32)).astype(ml_dtypes.bfloat16)
    return high, low


def line_tables():
    numbers = np.arange(K) - K // 2
    angles = (TWO_PI / NY) * (np.outer(numbers, np.arange(NY)) % NY)
    table = np.concatenate([np.cos(angles), -np.sin(angles)], axis=0).astype(np.float32)
    forward = np.zeros((GROUP, NY, LANES), ml_dtypes.bfloat16)
    back = np.zeros((GROUP, LANES, NY), ml_dtypes.bfloat16)
    high, low = halves(table)
    for t in range(GROUP):
        forward[t, :, 2 * K * t : 2 * K * (t + 1)] = table.astype(ml_dtypes.bfloat16).T
        for place, part in enumerate((high, high, low)):
            first = 2 * K * ((t + place) % GROUP)
            back[t, first : first + 2 * K] = part
    return forward, back


def time_tables():
    numbers = np.arange(K) - K // 2
    steps = np.arange(NT).reshape(TM, STEPS)
    angles = (TWO_PI / NT) * ((numbers[None, :, None] * steps[:, None, :]) % NT)
    unit = np.eye(K)

    def spread(real, imag):
        both = np.stack([real, imag], axis=3)
        return np.einsum("matr,ef->maetrf", both, unit).reshape(TM, K * K, STEPS * 2 * K)

    cos_part, sin_part = np.cos(angles), np.sin(angles)
    forward = spread(cos_part, sin_part)
    back = np.concatenate([spread(cos_part, sin_part), spread(-sin_part, cos_part)], axis=1)
    return forward.astype(np.float32), back.astype(np.float32)


def row_phases():
    numbers = np.arange(K) - K // 2
    angles = (TWO_PI / NX) * np.outer(CELLS * np.arange(ROWS) + MIDDLE, numbers)
    return np.stack([np.cos(angles), np.sin(angles)]).astype(np.float32)


def physics_tables():
    y = np.arange(NY)
    ky = np.arange(HALF)
    angles = (TWO_PI / NY) * (np.outer(y, ky) % NY)
    row_forward = np.concatenate([np.cos(angles), -np.sin(angles)], axis=1)
    scaling = np.where(ky == 0, 1.0, 2.0)[:, None] / NY
    row_back = np.concatenate([scaling * np.cos(angles).T, -scaling * np.sin(angles).T], axis=0)
    gap = np.arange(NY)
    gap_angles = (TWO_PI / NY) * (np.outer(gap, ky) % NY)
    slope = -(2.0 / NY) * (np.sin(gap_angles) * ky).sum(1)
    bend = -(2.0 / NY) * (np.cos(gap_angles) * ky * ky).sum(1)
    turn = (y[None, :] - y[:, None]) % NY
    row_slope, row_bend = slope[turn], bend[turn]
    x = np.arange(NX)
    kx = np.where(x < NX // 2, x, x - NX)
    dx = np.where(x == NX // 2, 0, kx)
    col_angles = (TWO_PI / NX) * (np.outer(x, x) % NX)
    col_slope = -(np.sin(col_angles) * dx).sum(1) / NX
    col_bend = -(np.cos(col_angles) * kx * kx).sum(1) / NX
    col_turn = (x[:, None] - x[None, :]) % NX
    col_slope, col_bend = col_slope[col_turn], col_bend[col_turn]
    col_wave = np.concatenate([np.cos(col_angles), np.sin(col_angles)], axis=0)
    squared = (kx[:, None] ** 2 + ky[None, :] ** 2).astype(np.float64)
    inverse = np.where(squared > 0, 1.0 / np.where(squared > 0, squared, 1.0), 0.0) / NX
    inverse = np.concatenate([inverse, inverse], axis=1).astype(np.float32)
    pairs = [
        halves(t)
        for t in (
            row_forward,
            row_back,
            row_slope,
            VISCOSITY * row_bend,
            col_wave,
            col_slope,
            VISCOSITY * col_bend,
        )
    ]
    return [t for pair in pairs for t in pair] + [inverse]


def turned_halves(z):
    moved = pltpu.roll(z, C, 1)
    low = lax.broadcasted_iota(jnp.int32, z.shape, 1) < C
    return jnp.where(low, moved, -moved)


def turned(z):
    real = lax.broadcasted_iota(jnp.int32, z.shape, 1) % (2 * K) < K
    return jnp.where(real, pltpu.roll(z, LANES - K, 1), -pltpu.roll(z, K, 1))


def loop(first, last, body, unroll=1):
    def step(j, carry):
        body(j)
        return carry

    lax.fori_loop(first, last, step, 0, unroll=unroll)


def project_rows(lines, phase_ref, store):
    row = lax.axis_index("rows")

    def part(chunk):
        rows = pl.ds(pl.multiple_of(8 * chunk, 8), 8)
        far = range(CELLS // 2, CELLS)
        pairs = [(lines[x, rows, :], lines[CELLS - 1 - x, rows, :]) for x in far]
        added = [right + left for right, left in pairs]
        taken = [turned(right - left) for right, left in pairs]
        for k in range(K // 2 + 1):
            even, odd = None, None
            for x, both, gap in zip(far, added, taken):
                angle = TWO_PI * k * (x - MIDDLE) / NX
                cos_term = both if k == 0 else math.cos(angle) * both
                even = cos_term if even is None else even + cos_term
                if k:
                    sin_term = math.sin(angle) * gap
                    odd = sin_term if odd is None else odd + sin_term
            found = []
            if k < K // 2:
                found.append((K // 2 + k, even if odd is None else even + odd))
            if k > 0:
                found.append((K // 2 - k, even - odd))
            for b, value in found:
                cos_b, sin_b = phase_ref[0, row, b], phase_ref[1, row, b]
                store(b, rows, cos_b * value + sin_b * turned(value))

    loop(0, C // 8, part)


def spread_rows(modes, phase_ref, spread):
    row = lax.axis_index("rows")

    def part(chunk):
        rows = pl.ds(pl.multiple_of(8 * chunk, 8), 8)
        z = []
        for b in range(K):
            cos_b, sin_b = phase_ref[0, row, b], phase_ref[1, row, b]
            value = modes(b, rows)
            z.append(cos_b * value - sin_b * turned(value))
        even, odd = [z[K // 2]], [None]
        for k in range(1, K // 2):
            even.append(z[K // 2 + k] + z[K // 2 - k])
            odd.append(turned(z[K // 2 - k] - z[K // 2 + k]))
        even.append(z[0])
        odd.append(turned(z[0]))
        for x in range(CELLS // 2, CELLS):
            same, changed = even[0], None
            for k in range(1, K // 2 + 1):
                angle = TWO_PI * k * (x - MIDDLE) / NX
                same = same + math.cos(angle) * even[k]
                term = math.sin(angle) * odd[k]
                changed = term if changed is None else changed + term
            spread[x, rows, :] = same + changed
            spread[CELLS - 1 - x, rows, :] = same - changed

    loop(0, C // 8, part)


def fill_block(block, matrix):
    block[...] = jnp.zeros_like(block)
    for x in range(GROUP):
        block[C * x : C * (x + 1), C * x : C * (x + 1)] = matrix


def spread_part(spread, back, t):
    total = spread.reshape(GROUP * C, LANES)
    high = total.astype(BF16).astype(F32)
    lane = lax.broadcasted_iota(jnp.int32, total.shape, 1) // (2 * K)
    left = jnp.where(
        lane == t,
        high,
        jnp.where(
            lane == (t + 1) % GROUP,
            pltpu.roll(total - high, 2 * K, 1),
            pltpu.roll(high, 4 * K, 1),
        ),
    ).astype(BF16)
    return jnp.dot(left, back, preferred_element_type=F32)


def physics(planes, step, tables, between, wait_rate, send_weighted, send_grad):
    (rf, rf_low, rb, rb_low, rs, rs_low, rc, rc_low, cw, cw_low, cs, cs_low, cc, cc_low, inverse) = (
        tables
    )

    def parts(value):
        high = value.astype(BF16)
        return high, (value - high.astype(F32)).astype(BF16)

    def dot(a, b):
        return jnp.dot(a, b, preferred_element_type=F32)

    def along(value, high, low):
        v_high, v_low = parts(value)
        return dot(v_high, high[...]) + (dot(v_low, high[...]) + dot(v_high, low[...]))

    def across(high, low, value):
        v_high, v_low = parts(value)
        return dot(high[...], v_high) + (dot(high[...], v_low) + dot(low[...], v_high))

    def minus_i(z):
        return jnp.concatenate([z[:, HALF:], -z[:, :HALF]], axis=1)

    def solve(value):
        spectrum = along(value, rf, rf_low)
        both = across(cw, cw_low, spectrum)
        spectrum = (both[:NX] + minus_i(both[NX:])) * inverse[...]
        both = across(cw, cw_low, spectrum)
        return along(both[:NX] - minus_i(both[NX:]), rb, rb_low)

    sign = jnp.where(lax.broadcasted_iota(jnp.int32, (NX, NY), 1) % 2 == 0, 1.0, -1.0).astype(F32)

    def smooth(value):
        return value - sign * (jnp.sum(value * sign, axis=1, keepdims=True) * (1.0 / NY))

    inside = (step > 0) & (step < NT - 1)
    vort = planes[0].reshape(NX, NY)
    stream = solve(vort)
    between()
    slopes = along(jnp.concatenate([vort, stream], axis=0), rs, rs_low)
    slope_right, flow_down = slopes[:NX], slopes[NX:]
    smoothed = smooth(vort)
    slopes = across(cs, cs_low, jnp.concatenate([smoothed, stream], axis=1))
    slope_down, flow_right = slopes[:, :NY], -slopes[:, NY:]
    bend = along(vort, rc, rc_low) + across(cc, cc_low, smoothed)
    wait_rate()
    rate = planes[1].reshape(NX, NY)
    residual = (
        rate
        + flow_down * slope_down
        + flow_right * slope_right
        - bend
    )
    weighted = jnp.where(inside, LOSS_WEIGHT * residual, 0.0)
    send_weighted(weighted)
    first = weighted * slope_down
    second = weighted * slope_right
    slopes = along(jnp.concatenate([first, flow_right * weighted], axis=0), rs, rs_low)
    first_along, flow_along = slopes[:NX], slopes[NX:]
    slopes = across(
        cs, cs_low, jnp.concatenate([second, smooth(flow_down * weighted)], axis=1)
    )
    second_across, flow_across = slopes[:, :NY], slopes[:, NY:]
    solved = solve(second_across - first_along)
    bend = along(weighted, rc, rc_low) + across(cc, cc_low, smooth(weighted))
    grad = solved - bend - flow_across - flow_along
    send_grad(grad)


def remote(src, dst, send, recv, device):
    return pltpu.make_async_remote_copy(
        src_ref=src, dst_ref=dst, send_sem=send, recv_sem=recv, device_id=device,
        device_id_type=MESH,
    )


def place():
    row, slab = lax.axis_index("rows"), lax.axis_index("tm")
    return row, slab, row // 2, row % 2


def greet():
    row, slab, chip, core = place()
    barrier = pltpu.get_barrier_semaphore()
    pl.semaphore_signal(
        barrier, inc=1, device_id=(row + 1 - 2 * core, slab), device_id_type=MESH
    )

    def tell(j):
        peer = 2 * ((chip + j) % CHIPS) + core
        pl.semaphore_signal(barrier, inc=1, device_id=(peer, slab), device_id_type=MESH)
        pl.semaphore_signal(
            barrier, inc=1, device_id=(row, (slab + j) % TM), device_id_type=MESH
        )

    loop(1, CHIPS, tell)


def all_here():
    pl.semaphore_wait(pltpu.get_barrier_semaphore(), 1 + (CHIPS - 1) + (TM - 1))


class Modes:
    def __init__(self, w_hbm, sum_hbm, back_hbm, scratch):
        (
            self.weight, self.sum_table, self.back_table, self.terms, self.from_core,
            self.from_rows, self.parts, self.from_slabs, self.mixed, self.slabs, self.gathered,
            self.load, self.core_send, self.core_recv, self.row_send, self.row_recv,
            self.slab_send, self.slab_recv, self.mix_send, self.mix_recv, self.out_send,
            self.out_recv, self.pass_send, self.pass_recv,
        ) = scratch
        self.row, self.slab, self.chip, self.core = place()
        self.other = (self.row + 1 - 2 * self.core, self.slab)
        self.loads = [
            pltpu.make_async_copy(src, dst, self.load.at[i])
            for i, (src, dst) in enumerate(
                (
                    (sum_hbm.at[self.slab], self.sum_table),
                    (w_hbm, self.weight),
                    (back_hbm.at[self.slab], self.back_table),
                )
            )
        ]

    def start_loads(self):
        for load in self.loads:
            load.start()

    def store(self, group):
        def put(b, rows, value):
            self.terms[b % 2, b // 2, group, rows, :] = value

        return put

    def core_copy(self, group, j):
        to = (self.chip + j) % CHIPS
        return remote(
            self.terms.at[1 - self.core, to, group], self.from_core.at[to, group],
            self.core_send.at[to, group], self.core_recv.at[to, group], self.other,
        )

    def row_copy(self, group, j):
        to = (self.chip + j) % CHIPS
        return remote(
            self.from_core.at[to, group], self.from_rows.at[self.chip, group],
            self.row_send.at[to, group], self.row_recv.at[self.chip, group],
            (2 * to + self.core, self.slab),
        )

    def start_core(self, group):
        loop(1, CHIPS + 1, lambda j: self.core_copy(group, j).start())

    def forward(self, group):
        def step(j):
            to = (self.chip + j) % CHIPS
            self.core_copy(group, j).wait_recv()
            self.from_core[to, group] = (
                self.from_core[to, group] + self.terms[self.core, to, group]
            )
            self.row_copy(group, j).start()

        loop(1, CHIPS, step)
        self.core_copy(group, CHIPS).wait_recv()
        self.from_rows[self.chip, group] = (
            self.from_core[self.chip, group] + self.terms[self.core, self.chip, group]
        )

    def arrivals(self, group):
        def step(j):
            source = (self.chip + CHIPS - j) % CHIPS
            remote(
                self.from_core.at[source, group], self.from_rows.at[source, group],
                self.row_send.at[source, group], self.row_recv.at[source, group],
                (2 * source + self.core, self.slab),
            ).wait_recv()

        loop(1, CHIPS, step)
        total = self.from_rows[0, group]
        for source in range(1, CHIPS):
            total = total + self.from_rows[source, group]
        return total

    def slab_copy(self, j):
        to = (self.slab + j) % TM
        return remote(
            self.parts.at[to], self.from_slabs.at[self.slab], self.slab_send.at[to],
            self.slab_recv.at[self.slab], (self.row, to),
        )

    def mix_copy(self, j):
        to = (self.slab + j) % TM
        return remote(
            self.mixed, self.slabs.at[self.slab], self.mix_send.at[to],
            self.mix_recv.at[self.slab], (self.row, to),
        )

    def exchange_slabs(self, gradient, coef_ref, first, second):
        totals = [self.arrivals(group) for group in range(2)]
        both = jnp.concatenate(
            [
                jnp.concatenate(totals, axis=1),
                jnp.concatenate([turned(total) for total in totals], axis=1),
            ],
            axis=0,
        )
        if not gradient:
            self.loads[0].wait()
        found = lax.dot_general(
            self.sum_table[...], both, (((1,), (1,)), ((), ())),
            precision=lax.Precision.HIGHEST, preferred_element_type=F32,
        )
        self.parts[...] = (found * (S_MODE if gradient else S_GRID)).reshape(
            TM, 2 * K, 2 * C
        )
        loop(1, TM, lambda j: self.slab_copy(j).start())
        self.from_slabs[self.slab] = self.parts[self.slab]
        first()
        if not gradient:
            self.loads[1].wait()

        def slab_arrival(j):
            source = (self.slab + TM - j) % TM
            remote(
                self.parts.at[source], self.from_slabs.at[source], self.slab_send.at[source],
                self.slab_recv.at[source], (self.row, source),
            ).wait_recv()

        loop(1, TM, slab_arrival)
        coef = self.from_slabs[0]
        for source in range(1, TM):
            coef = coef + self.from_slabs[source]
        coef_ref[...] = coef
        if gradient:
            self.mix_back(coef)
        else:
            self.mix(coef)
        loop(1, TM, lambda j: self.mix_copy(j).start())
        self.slabs[self.slab] = self.mixed[...]
        second()

        def mix_arrival(j):
            source = (self.slab + TM - j) % TM
            remote(
                self.mixed, self.slabs.at[source], self.mix_send.at[source],
                self.mix_recv.at[source], (self.row, source),
            ).wait_recv()

        loop(1, TM, mix_arrival)
        if not gradient:
            self.loads[2].wait()
        whole = jnp.transpose(self.slabs[...].reshape(K * K, 2 * C))
        spread = (S_GRID if gradient else S_MODE) * jnp.dot(
            jnp.concatenate([whole[:C], whole[C:]], axis=1), self.back_table[...],
            precision=lax.Precision.HIGHEST, preferred_element_type=F32,
        )
        self.gathered[0, self.row] = spread[:, :LANES]
        self.gathered[1, self.row] = spread[:, LANES:]
        for group in range(2):
            loop(1, CHIPS, lambda j: self.out_copy(group, j).start())
            self.pass_copy(group, self.chip).start()

    def mix(self, coef):
        columns = jnp.transpose(
            jnp.concatenate([coef, jnp.zeros((2 * C - 2 * K, 2 * C), F32)], axis=0)
        )
        for j in range(2 * K):
            weight = self.weight[j // K, j % K]
            re = jnp.sum(weight * columns[:C, j : j + 1], axis=0, keepdims=True)
            im = jnp.sum(weight * columns[C:, j : j + 1], axis=0, keepdims=True)
            self.mixed[j : j + 1, :] = re - turned_halves(im)

    def mix_back(self, coef):
        turned_coef = turned_halves(coef)
        lane = lax.broadcasted_iota(jnp.int32, (C, 2 * C), 1)
        real = jnp.zeros((C, 2 * C), F32)
        imag = jnp.zeros((C, 2 * C), F32)
        for j in range(2 * K):
            weight = self.weight[j // K, j % K]
            re = jnp.sum(weight * coef[j : j + 1, :], axis=1, keepdims=True)
            im = jnp.sum(weight * turned_coef[j : j + 1, :], axis=1, keepdims=True)
            real = jnp.where(lane == j, re, real)
            imag = jnp.where(lane == j, im, imag)
        self.mixed[...] = jnp.transpose(jnp.concatenate([real, imag], axis=0))[: 2 * K]

    def out_copy(self, group, j):
        to = (self.chip + j) % CHIPS
        block = self.gathered.at[group, self.row]
        return remote(
            block, block, self.out_send.at[to, group], self.out_recv.at[self.chip, group],
            (2 * to + self.core, self.slab),
        )

    def pass_copy(self, group, source):
        block = self.gathered.at[group, 2 * source + self.core]
        return remote(
            block, block, self.pass_send.at[source, group], self.pass_recv.at[source, group],
            self.other,
        )

    def pass_on(self, group):
        def step(j):
            source = (self.chip + CHIPS - j) % CHIPS
            block = self.gathered.at[group, 2 * source + self.core]
            remote(
                block, block, self.out_send.at[source, group], self.out_recv.at[source, group],
                (2 * source + self.core, self.slab),
            ).wait_recv()
            self.pass_copy(group, source).start()

        loop(1, CHIPS, step)

    def gather_done(self, group):
        def step(source):
            block = self.gathered.at[group, 2 * source + 1 - self.core]
            remote(
                block, block, self.pass_send.at[source, group], self.pass_recv.at[source, group],
                self.other,
            ).wait_recv()

        loop(0, CHIPS, step)

    def wait_sums(self):
        loop(1, TM, lambda j: self.slab_copy(j).wait_send())
        loop(1, TM, lambda j: self.mix_copy(j).wait_send())
        for group in range(2):
            loop(1, CHIPS + 1, lambda j: self.core_copy(group, j).wait_send())
            loop(1, CHIPS, lambda j: self.row_copy(group, j).wait_send())

    def wait_gathers(self):
        for group in range(2):
            loop(1, CHIPS, lambda j: self.out_copy(group, j).wait_send())
            loop(0, CHIPS, lambda j: self.pass_copy(group, j).wait_send())


class Planes:
    def __init__(self, forcing_ref, scratch):
        (
            self.vort, self.rates, self.halo, self.planes, self.halo_send, self.halo_recv,
            self.send, self.recv, self.pass_send, self.pass_recv,
        ) = scratch
        self.forcing = forcing_ref
        self.row, self.slab, self.chip, self.core = place()
        self.other = (self.row + 1 - 2 * self.core, self.slab)
        after, before = (self.slab + 1) % TM, (self.slab + TM - 1) % TM
        self.to_after = remote(
            self.vort.at[STEPS - 1], self.halo.at[0], self.halo_send.at[0], self.halo_recv.at[0],
            (self.row, after),
        )
        self.to_before = remote(
            self.vort.at[0], self.halo.at[1], self.halo_send.at[1], self.halo_recv.at[1],
            (self.row, before),
        )

    def copy(self, field, to):
        source = (self.vort, self.rates)[field].at[to]
        return remote(
            source, self.planes.at[field, self.row], self.send.at[field, to],
            self.recv.at[field, self.chip], (2 * to + self.core, self.slab),
        )

    def pass_copy(self, field, source):
        block = self.planes.at[field, 2 * source + self.core]
        return remote(
            block, block, self.pass_send.at[field, source], self.pass_recv.at[field, source],
            self.other,
        )

    def send_step(self, field, to):
        @pl.when(to != self.chip)
        def _():
            self.copy(field, to).start()

        @pl.when(to == self.chip)
        def _():
            self.planes[field, self.row] = (self.vort, self.rates)[field][to]
            self.pass_copy(field, self.chip).start()

    def rate(self, step, low, high):
        self.rates[step] = (0.5 * NT) * (high - low) - self.forcing[...]

    def inner_rates(self, first, last):
        for step in range(first, last):
            self.rate(step, self.vort[step - 1], self.vort[step + 1])
            self.send_step(1, step)

    def arrivals(self, field):
        def step(j):
            source = (self.chip + CHIPS - j) % CHIPS
            block = 2 * source + self.core
            remote(
                self.vort.at[source], self.planes.at[field, block], self.send.at[field, source],
                self.recv.at[field, source], (block, self.slab),
            ).wait_recv()
            self.pass_copy(field, source).start()

        loop(1, CHIPS, step)

    def pass_arrivals(self, field):
        def step(source):
            block = self.planes.at[field, 2 * source + 1 - self.core]
            remote(
                block, block, self.pass_send.at[field, source], self.pass_recv.at[field, source],
                self.other,
            ).wait_recv()

        loop(0, CHIPS, step)

    def wait_sends(self):
        self.to_after.wait_send()
        self.to_before.wait_send()
        for field in range(2):
            loop(1, CHIPS, lambda j: self.copy(field, (self.chip + j) % CHIPS).wait_send())
            loop(0, CHIPS, lambda j: self.pass_copy(field, j).wait_send())


class Returns:
    def __init__(self, scratch):
        (
            self.source, self.steps, self.halo, self.send, self.recv, self.halo_send,
            self.halo_recv,
        ) = scratch
        self.row, self.slab, self.chip, self.core = place()
        after, before = (self.slab + 1) % TM, (self.slab + TM - 1) % TM
        self.to_after = remote(
            self.steps.at[1, STEPS - 1], self.halo.at[0], self.halo_send.at[0],
            self.halo_recv.at[0], (self.row, after),
        )
        self.to_before = remote(
            self.steps.at[1, 0], self.halo.at[1], self.halo_send.at[1], self.halo_recv.at[1],
            (self.row, before),
        )

    def copy(self, field, j):
        to = (self.chip + j) % CHIPS
        block = 2 * to + self.core
        return remote(
            self.source.at[field, block], self.steps.at[field, self.chip],
            self.send.at[field, to], self.recv.at[field, self.chip], (block, self.slab),
        )

    def start(self, field, value):
        self.source[field] = value.reshape(ROWS, CELLS, NY)
        loop(1, CHIPS, lambda j: self.copy(field, j).start())
        self.steps[field, self.chip] = self.source[field, self.row]

    def arrivals(self, field):
        def step(j):
            source = (self.chip + CHIPS - j) % CHIPS
            block = 2 * source + self.core
            remote(
                self.source.at[field, block], self.steps.at[field, source],
                self.send.at[field, source], self.recv.at[field, source], (block, self.slab),
            ).wait_recv()

        loop(1, CHIPS, step)

    def finish(self, grads):
        self.arrivals(1)
        self.to_after.start()
        self.to_before.start()
        self.arrivals(0)

        def grad(step, low, high):
            grads[step] = self.steps[0, step] + (0.5 * NT) * (low - high)

        for step in range(1, STEPS - 1):
            grad(step, self.steps[1, step - 1], self.steps[1, step + 1])
        self.to_after.wait_recv()
        grad(0, self.halo[0], self.steps[1, 1])
        self.to_before.wait_recv()
        grad(STEPS - 1, self.steps[1, STEPS - 2], self.halo[1])

    def wait_sends(self):
        self.to_after.wait_send()
        self.to_before.wait_send()
        for field in range(2):
            loop(1, CHIPS, lambda j: self.copy(field, j).wait_send())


def whole_kernel(
    act_hbm, w_hbm, matrix_ref, readout_ref, forcing_ref, forward_ref, back_ref, phase_ref,
    sum_hbm, back_hbm, *rest,
):
    table_hbm, rest = rest[:PHYSICS], rest[PHYSICS:]
    act, mode_ref, lines, block, wide, fields, grads, coef, grad_mixed = rest[:9]
    act_load, table_load = rest[9:11]
    rest = rest[11:]
    tables, rest = rest[:PHYSICS], rest[PHYSICS:]
    modes = Modes(w_hbm, sum_hbm, back_hbm, rest[:MODE_SCRATCH])
    planes = Planes(forcing_ref, rest[MODE_SCRATCH : MODE_SCRATCH + PLANE_SCRATCH])
    returns = Returns(rest[MODE_SCRATCH + PLANE_SCRATCH :])

    def load(t):
        return pltpu.make_async_copy(act_hbm.at[t], act.at[t], act_load.at[t])

    table_loads = [
        pltpu.make_async_copy(src, dst, table_load.at[i])
        for i, (src, dst) in enumerate(zip(table_hbm, tables))
    ]
    greet()
    for t in range(STEPS):
        load(t).start()
    modes.start_loads()
    for copy in table_loads:
        copy.start()
    same = lax.broadcasted_iota(jnp.int32, (C, C), 0) == lax.broadcasted_iota(
        jnp.int32, (C, C), 1
    )
    unit = jnp.where(same, 1.0, 0.0).astype(BF16)
    fill_block(
        block,
        lax.dot_general(
            matrix_ref[...], unit, (((0,), (0,)), ((), ())), preferred_element_type=F32
        ).astype(BF16),
    )
    wide[...] = 0.5 * jnp.broadcast_to(
        jnp.sum(jnp.where(same, readout_ref[...], 0.0), axis=1, keepdims=True), (C, LANES)
    )

    def make_lines(group, prepare):
        def part(chunk):
            rows = pl.ds(GROUP * chunk, GROUP)
            total = None
            for inner in range(GROUP):
                t = GROUP * group + inner
                prepare(t, chunk, rows)
                term = jnp.dot(
                    act[t, rows].reshape(GROUP * C, NY), forward_ref[inner],
                    preferred_element_type=F32,
                )
                total = term if total is None else total + term
            lines[rows] = total.reshape(GROUP, C, LANES)

        loop(0, GROUP, part, unroll=2)

    def analyze(prepare, before, ready):
        before(0)
        make_lines(0, prepare)
        project_rows(lines, phase_ref, modes.store(0))
        ready()
        modes.start_core(0)
        before(1)
        make_lines(1, prepare)
        modes.forward(0)
        project_rows(lines, phase_ref, modes.store(1))
        modes.start_core(1)
        modes.forward(1)

    def local(quarter):
        def part(i):
            t, rows = 2 * quarter + i % 2, pl.ds(GROUP * (i // 2), GROUP)
            fields[t, rows] = jnp.dot(
                block[...], act[t, rows].reshape(GROUP * C, NY), preferred_element_type=F32
            ).reshape(GROUP, C, NY)

        loop(0, 2 * GROUP, part, unroll=UNROLL)

    def wait_load(group):
        for t in range(GROUP):
            load(GROUP * group + t).wait()

    analyze(lambda t, chunk, rows: None, wait_load, all_here)
    local(0)
    modes.exchange_slabs(False, coef, lambda: local(1), lambda: local(2))
    local(3)
    modes.wait_sums()

    c0 = math.sqrt(2.0 / math.pi)
    c1 = c0 * 0.044715

    def hide(group):
        def part(inner, chunk):
            t = GROUP * group + inner
            found = spread_part(lines[pl.ds(GROUP * chunk, GROUP)], back_ref[inner], inner)
            for x in range(GROUP):
                total = None
                for part_of in range(C // 16):
                    own = slice(16 * part_of, 16 * part_of + 16)
                    readout = jnp.concatenate([wide[own]] * (NY // LANES), axis=1)
                    place_of = C * x + 16 * part_of
                    value = found[place_of : place_of + 16] + fields[t, GROUP * chunk + x, own, :]
                    square = value * value
                    bend = jnp.tanh(value * (c0 + c1 * square))
                    scaled = readout * (1.0 + bend)
                    steep = (1.0 - bend) * (value * (c0 + 3.0 * c1 * square))
                    fields[t, GROUP * chunk + x, own, :] = scaled + scaled * steep
                    term = scaled * value
                    term = term[:8] + term[8:]
                    total = term if total is None else total + term
                planes.vort[t, pl.ds(GROUP * chunk + x, 1), :] = jnp.sum(
                    total, axis=0, keepdims=True
                )

        def step(inner):
            loop(0, GROUP, lambda chunk: part(inner, chunk), unroll=UNROLL)
            planes.send_step(0, GROUP * group + inner)

        loop(0, GROUP, step)

    def spread(group):
        spread_rows(lambda b, rows: modes.gathered[group, b, rows, :], phase_ref, lines)

    modes.pass_on(0)
    modes.gather_done(0)
    spread(0)
    modes.pass_on(1)
    hide(0)
    planes.to_before.start()
    planes.inner_rates(1, GROUP - 1)
    modes.gather_done(1)
    spread(1)
    hide(1)
    planes.to_after.start()
    planes.inner_rates(GROUP - 1, STEPS - 1)
    modes.wait_gathers()
    planes.to_after.wait_recv()
    planes.rate(0, planes.halo[0], planes.vort[1])
    planes.send_step(1, 0)
    planes.to_before.wait_recv()
    planes.rate(STEPS - 1, planes.vort[STEPS - 2], planes.halo[1])
    planes.send_step(1, STEPS - 1)
    planes.arrivals(0)
    fill_block(block, matrix_ref[...])
    for copy in table_loads:
        copy.wait()
    planes.pass_arrivals(0)

    physics(
        planes.planes, modes.slab * STEPS + modes.chip, tables,
        lambda: planes.arrivals(1), lambda: planes.pass_arrivals(1),
        lambda value: returns.start(1, value), lambda value: returns.start(0, value),
    )
    returns.finish(grads)

    def prepare(t, chunk, rows):
        for x in range(GROUP):
            weight = grads[t, pl.ds(GROUP * chunk + x, 1), :]
            act[t, GROUP * chunk + x] = (fields[t, GROUP * chunk + x] * weight).astype(BF16)

    analyze(prepare, lambda group: None, lambda: None)

    def mode_grads():
        lane = lax.broadcasted_iota(jnp.int32, (C, 2 * C), 1)
        first = lax.broadcasted_iota(jnp.int32, (C, 2 * C), 0)
        for j in range(2 * K):
            own, grad = coef[j : j + 1, :], grad_mixed[j : j + 1, :]
            real = jnp.sum(jnp.where(lane == first, own, 0.0), axis=1, keepdims=True)
            imag = jnp.sum(jnp.where(lane == first + C, own, 0.0), axis=1, keepdims=True)
            mode_ref[j // K, j % K] = real * grad + imag * turned_halves(grad)

    def second():
        local(2)
        mode_grads()
        planes.wait_sends()
        returns.wait_sends()

    local(0)
    modes.exchange_slabs(True, grad_mixed, lambda: local(1), second)
    local(3)
    modes.wait_sums()

    def put_out(group):
        def part(i):
            inner, chunk = i % GROUP, i // GROUP
            t, rows = GROUP * group + inner, pl.ds(GROUP * chunk, GROUP)
            found = spread_part(lines[rows], back_ref[inner], inner).reshape(GROUP, C, NY)
            act[t, rows] = (found + fields[t, rows]).astype(BF16)

        loop(0, GROUP * GROUP, part, unroll=UNROLL)

    modes.pass_on(0)
    modes.gather_done(0)
    spread(0)
    modes.pass_on(1)
    put_out(0)
    modes.gather_done(1)
    spread(1)
    put_out(1)
    modes.wait_gathers()


VMEM = pl.BlockSpec(memory_space=pltpu.VMEM)
SMEM = pl.BlockSpec(memory_space=pltpu.SMEM)
ANY = pl.BlockSpec(memory_space=pl.ANY)
DMA = pltpu.SemaphoreType.DMA
LIMIT = 46 * 1024 * 1024
UNROLL = 4

FIELD = (CELLS, C, NY)
PLANE = (CELLS, NY)
PART = (C, LANES)
PAIR = (2 * K, 2 * C)


def vmem(*shape, dtype=F32):
    return pltpu.VMEM(shape, dtype)


MODE_SCRATCH, PLANE_SCRATCH, PHYSICS = 24, 10, 15


def mode_scratch():
    return [
        vmem(2, K, C, 2 * C),
        vmem(K * K, 2 * LANES),
        vmem(2 * K * K, 2 * LANES),
        vmem(2, CHIPS, 2, *PART),
        vmem(CHIPS, 2, *PART),
        vmem(CHIPS, 2, *PART),
        vmem(TM, *PAIR),
        vmem(TM, *PAIR),
        vmem(*PAIR),
        vmem(TM, *PAIR),
        vmem(2, K, *PART),
        DMA((3,)),
        *[DMA((CHIPS, 2))] * 4,
        *[DMA((TM,))] * 4,
        *[DMA((CHIPS, 2))] * 4,
    ]


def shards(activations, spectral_weight, pointwise, readout, forcing):
    line_forward, line_back = (jnp.asarray(t) for t in line_tables())
    phases = jnp.asarray(row_phases())
    sum_table, back_table = (jnp.asarray(t) for t in time_tables())
    physics_parts = [jnp.asarray(t) for t in physics_tables()]
    return pl.pallas_call(
        whole_kernel,
        out_shape=(
            pltpu.VMEM((STEPS,) + FIELD, BF16),
            pltpu.VMEM((2, K, C, 2 * C), F32),
        ),
        in_specs=[ANY, ANY, VMEM, VMEM, VMEM, VMEM, VMEM, SMEM, ANY, ANY] + [ANY] * PHYSICS,
        out_specs=(VMEM, VMEM),
        scratch_shapes=[
            vmem(CELLS, *PART),
            vmem(GROUP * C, GROUP * C, dtype=BF16),
            vmem(C, LANES),
            vmem(STEPS, *FIELD),
            vmem(STEPS, *PLANE),
            vmem(*PAIR),
            vmem(*PAIR),
            DMA((STEPS,)),
            DMA((PHYSICS,)),
            *[vmem(*t.shape, dtype=t.dtype) for t in physics_parts],
            *mode_scratch(),
            vmem(STEPS, *PLANE),
            vmem(STEPS, *PLANE),
            vmem(2, *PLANE),
            vmem(2, ROWS, *PLANE),
            DMA((2,)),
            DMA((2,)),
            *[DMA((2, CHIPS))] * 4,
            vmem(2, ROWS, *PLANE),
            vmem(2, CHIPS, *PLANE),
            vmem(2, *PLANE),
            *[DMA((2, CHIPS))] * 2,
            DMA((2,)),
            DMA((2,)),
        ],
        compiler_params=pltpu.CompilerParams(
            collective_id=0, has_side_effects=True, vmem_limit_bytes=LIMIT
        ),
        name="whole",
    )(
        activations, spectral_weight, pointwise, readout.reshape(1, C), forcing, line_forward,
        line_back, phases, sum_table, back_table, *physics_parts,
    )


def solution(mesh):
    return jax.shard_map(
        shards,
        mesh=mesh,
        in_specs=(
            P("tm", "rows", None, None),
            P(("rows", "tm"), None, None, None),
            P(),
            P(),
            P("rows", None),
        ),
        out_specs=(P("tm", "rows", None, None), P(("rows", "tm"), None, None, None)),
        check_vma=False,
    )
```
